128 devices in a mesh: group: 8 (over x, z_hi), fsdp: 16 (over z_lo, y, core).
Axes of the slice: x: 4, y: 4, z: 4 (z_hi: 2, z_lo: 2; z = z_hi * 2 + z_lo), core: 2. Of those that a mesh axis runs over, the one named last changes fastest.
Arguments:
- tokens: bfloat16 [1024, 4608], P('fsdp'), may hold values from -6 to 6
- pre_gain: float32 [4608], replicated, may hold values from 0.1 to 1.9
- post_gain: float32 [4608], replicated, may hold values from 0.1 to 1.9
- qkv_weight: bfloat16 [4608, 16, 4, 128], P(None, 'fsdp')
- out_weight: bfloat16 [16, 2, 128, 4608], P('fsdp'), may hold values from -0.09375 to 0.09375
- doc_ids: int32 [1024], replicated, may hold values from 0 to 3, never falling along the last dimension, each value on 1 to 512 neighbouring positions
- cotangent: bfloat16 [1024, 4608], P('fsdp'), may hold values from -6 to 6
- outer_delta: bfloat16 [8, 2048, 4608], P('group', 'fsdp'), may hold values from -6 to 6
- momentum: float32 [2048, 4608], P('fsdp'), may hold values from -6 to 6
- fragment: float32 [2048, 4608], P('fsdp'), may hold values from -6 to 6
Outputs:
- output: bfloat16 [1024, 4608], P('fsdp')
- grad_qkv: bfloat16 [4608, 16, 4, 128], P(None, 'fsdp')
- grad_out: bfloat16 [16, 2, 128, 4608], P('fsdp')
- new_momentum: float32 [2048, 4608], P('fsdp')
- new_fragment: float32 [2048, 4608], P('fsdp')
The draws below stay inside these ranges and needn't reach their ends.
Inputs may be any that keep to these rules, and one draw needn't show every extreme that they name: doc_ids never falls along the sequence; each document holds 1 to 512 tokens and one holds exactly 512.
All inputs are finite; a program needn't handle non-finite values.
Results may differ from the reference program's by a relative error of at most 0.015.
The reference program's roundings to bfloat16 on the way count: a program that leaves them out, or rounds other values in their place, can miss the bound.
Values may be sent and summed in bfloat16 or wider, within the bound.
A program may use at most 192 MiB of HBM per device.

```python
import math
import jax
import jax.numpy as jnp
import numpy as np
from jax import lax

D = 4608
KVH = 16
QPER = 2
HEADS = 32
HDIM = 128
DOCS = 4
TOK_DEV = 64
SEQ = 1024
FRAG = 2048
GROUPS = 8
N_FSDP = 16


def draw_qkv_weight(key, part):
    key = jax.random.fold_in(key, 11)
    entry_key, raised_key = jax.random.split(key)
    extent = (D, KVH, QPER + 2, HDIM)
    entries = jnp.clip(jax.random.normal(entry_key, extent, jnp.float32), -4.0, 4.0)
    raised = jax.random.uniform(raised_key, (KVH, QPER + 1), jnp.float32, 0.0, 1.0)
    factor = jnp.concatenate([jnp.exp(raised * math.log(4.5)), jnp.ones((KVH, 1), jnp.float32)], axis=1)
    return (entries * factor[None, :, :, None] / math.sqrt(D)).astype(jnp.bfloat16)


def block_scale(stream_key, shape, cuts, smallest, high):
    def one(position, blocks):
        heights = jax.random.uniform(jax.random.fold_in(jax.random.fold_in(stream_key, 6), position), (blocks,), jnp.float32, smallest / len(cuts), high / len(cuts))
        return jnp.repeat(jnp.exp(heights), shape[position] // blocks).reshape((-1,) + (1,) * (len(shape) - position - 1))

    level = one(*cuts[0])
    for cut in cuts[1:]:
        level = level * one(*cut)
    return level


def split_up(amount, total, limit, skew):
    loads = [(1 << 20) // math.isqrt(standing ** skew) + 1 for standing in range(2, amount + 1)]
    rest, counts = total - limit - (amount - 1), [1] * (amount - 1)
    while rest > 0:
        movable = [i for i in range(amount - 1) if counts[i] < limit]
        whole, budget = sum([loads[i] for i in movable]), rest
        for i in movable:
            addition = min(limit - counts[i], max(1, budget * loads[i] // whole), rest)
            counts[i] = counts[i] + addition
            rest = rest - addition
    return np.array([limit] + counts)


def ragged_sizes(stream_key, amount, total, reach, skew):
    if amount == 2:
        one = jax.random.randint(stream_key, (), max(1, total - reach), min(reach, total - 1) + 1)
        return jnp.stack([one, total - one])
    tallies = jnp.asarray(split_up(amount, total, reach, skew), jnp.int32)
    twos = (amount - 1) // 2
    source_of, sink = tallies[1:1 + 2 * twos:2], tallies[2:2 + 2 * twos:2]
    slack = jnp.minimum(source_of - 1, reach - sink)
    shifted = jax.random.randint(jax.random.fold_in(stream_key, 1), (twos,), 0, 1 << 20) % (slack + 1)
    tallies = tallies.at[1:1 + 2 * twos:2].set(source_of - shifted).at[2:2 + 2 * twos:2].set(sink + shifted)
    return tallies[jax.random.permutation(jax.random.fold_in(stream_key, 2), amount)]


def centred(own_key, dims, spread, limit, cuts=(), kind=jnp.bfloat16):
    factor_of = block_scale(own_key, dims, cuts, -0.22, 0.18) if cuts else 1.0
    drawn = jax.random.normal(own_key, dims, jnp.float32) * spread * factor_of
    return jnp.minimum(jnp.maximum(drawn, -limit), limit).astype(kind)


def setup_inputs(seed: int = 0) -> dict:
    key_list = jax.random.split(jax.random.key(seed), 11)
    tokens = centred(key_list[0], (SEQ, D), 1.0, 6.0, ((0, 16),))
    pre_gain = jnp.clip(1.0 + 0.18 * jax.random.normal(key_list[1], (D,), jnp.float32), 0.1, 1.9)
    post_gain = jnp.clip(1.0 + 0.18 * jax.random.normal(key_list[2], (D,), jnp.float32), 0.1, 1.9)
    qkv_weight = draw_qkv_weight(jax.random.fold_in(key_list[10], 71), 0)
    out_weight = centred(key_list[4], (KVH, QPER, HDIM, D), (HEADS * HDIM) ** -0.5, 0.09375, ((0, 16),))
    doc_ids = jnp.searchsorted(jnp.cumsum(ragged_sizes(key_list[5], DOCS, SEQ, TOK_DEV * N_FSDP // 2, 0)), jnp.arange(SEQ), side="right").astype(jnp.int32)
    cotangent = centred(key_list[6], (SEQ, D), 1.0, 6.0, ((0, 16),))
    outer_delta = centred(key_list[7], (GROUPS, FRAG, D), 1.0, 6.0, ((0, 8), (1, 16)))
    momentum = centred(key_list[8], (FRAG, D), 1.0, 6.0, ((0, 16),), jnp.float32)
    fragment = centred(key_list[9], (FRAG, D), 1.0, 6.0, ((0, 16),), jnp.float32)
    return dict(tokens=tokens, pre_gain=pre_gain, post_gain=post_gain, qkv_weight=qkv_weight, out_weight=out_weight, doc_ids=doc_ids, cotangent=cotangent, outer_delta=outer_delta, momentum=momentum, fragment=fragment)


softcap = 50.0
query_scale = 1.0 / 12.0

def rms_norm(values, gain):
    scale = lax.rsqrt(lax.optimization_barrier(jnp.mean(values * values, axis=-1, keepdims=True)) + 1e-06)
    return values * scale * gain

def rms_backward(values, gain, grads):
    scale = lax.rsqrt(lax.optimization_barrier(jnp.mean(values * values, axis=-1, keepdims=True)) + 1e-06)
    normal = values * scale
    dnorm = grads * gain
    return scale * (dnorm - normal * lax.optimization_barrier(jnp.mean(dnorm * normal, axis=-1, keepdims=True)))

def tables(length, width):
    half = width // 2
    positions = jnp.arange(length, dtype=jnp.float32)[:, None]
    freqs = jnp.power(jnp.float32(10000.0), -(2.0 * jnp.arange(half, dtype=jnp.float32) / width))
    angle = positions * freqs[None, :]
    return (jnp.cos(angle), jnp.sin(angle))

def rotate(values, cosine, sine):
    half = values.shape[-1] // 2
    first, second = (values[..., :half], values[..., half:])
    return jnp.concatenate([first * cosine - second * sine, second * cosine + first * sine], axis=-1)

def unrotate(grads, cosine, sine):
    half = grads.shape[-1] // 2
    first, second = (grads[..., :half], grads[..., half:])
    return jnp.concatenate([first * cosine + second * sine, second * cosine - first * sine], axis=-1)

def attend(query, keyed, valued, allowed):
    scores = jnp.dot(query, keyed.T, preferred_element_type=jnp.float32) * query_scale
    capped = softcap * jnp.tanh(scores / softcap)
    weights = jnp.where(allowed, jnp.exp(capped), jnp.float32(0.0))
    probs = weights / lax.optimization_barrier(jnp.sum(weights, axis=-1, keepdims=True))
    rounded = probs.astype(jnp.bfloat16)
    result = jnp.dot(rounded, valued, preferred_element_type=jnp.float32)
    return (result, probs, rounded, capped)

def attend_back(query, keyed, valued, probs, rounded, capped, grad_head):
    dprob = jnp.dot(grad_head, valued.T, preferred_element_type=jnp.float32)
    dvalue = jnp.dot(rounded.T, grad_head, preferred_element_type=jnp.float32)
    dcap = probs * (dprob - lax.optimization_barrier(jnp.sum(dprob * probs, axis=-1, keepdims=True)))
    dscore = (dcap * (1.0 - (capped / softcap) ** 2) * query_scale).astype(jnp.bfloat16)
    dquery = jnp.dot(dscore, keyed, preferred_element_type=jnp.float32)
    dkey = jnp.dot(dscore.T, query, preferred_element_type=jnp.float32)
    return (dquery, dkey, dvalue)

def reference(tokens, pre_gain, post_gain, qkv_weight, out_weight, doc_ids, cotangent, outer_delta, momentum, fragment):
    inputs = tokens.astype(jnp.float32)
    normed = rms_norm(inputs, pre_gain).astype(jnp.bfloat16)
    parts = QPER + 2
    proj = jnp.dot(normed, qkv_weight.reshape(D, KVH * parts * HDIM), preferred_element_type=jnp.float32)
    proj = proj.reshape(SEQ, KVH, parts, HDIM)
    cosine, sine = tables(SEQ, HDIM)
    queries = rotate(proj[:, :, :QPER], cosine[:, None, None, :], sine[:, None, None, :]).astype(jnp.bfloat16)
    keys = rotate(proj[:, :, QPER], cosine[:, None, :], sine[:, None, :]).astype(jnp.bfloat16)
    values = proj[:, :, QPER + 1].astype(jnp.bfloat16)
    index = jnp.arange(SEQ, dtype=jnp.int32)
    allowed = (index[None, :] <= index[:, None]) & (doc_ids[None, :] == doc_ids[:, None])
    qhead = jnp.transpose(queries, (1, 2, 0, 3))
    khead = jnp.transpose(keys, (1, 0, 2))
    vhead = jnp.transpose(values, (1, 0, 2))

    def forward_group(items):
        query_set, keyed, valued = items
        return jax.vmap(attend, in_axes=(0, None, None, None))(query_set, keyed, valued, allowed)
    result, probs, rounded, capped = lax.map(forward_group, (qhead, khead, vhead))
    heads = jnp.transpose(result.astype(jnp.bfloat16), (2, 0, 1, 3))
    head_flat = heads.reshape(SEQ, HEADS * HDIM)
    out_flat = out_weight.reshape(HEADS * HDIM, D)
    attn = jnp.dot(head_flat, out_flat, preferred_element_type=jnp.float32)
    output = (inputs + rms_norm(attn, post_gain)).astype(jnp.bfloat16)
    grad_attn = rms_backward(attn, post_gain, cotangent.astype(jnp.float32)).astype(jnp.bfloat16)
    grad_out = jnp.dot(head_flat.T, grad_attn, preferred_element_type=jnp.float32).astype(jnp.bfloat16)
    grad_out = grad_out.reshape(KVH, QPER, HDIM, D)
    grad_heads = jnp.dot(grad_attn, out_flat.T, preferred_element_type=jnp.float32).astype(jnp.bfloat16)
    grad_heads = jnp.transpose(grad_heads.reshape(SEQ, KVH, QPER, HDIM), (1, 2, 0, 3))

    def backward_group(items):
        query_set, keyed, valued, prob_set, round_set, cap_set, grad_set = items
        dquery, dkey, dvalue = jax.vmap(attend_back, in_axes=(0, None, None, 0, 0, 0, 0))(query_set, keyed, valued, prob_set, round_set, cap_set, grad_set)
        return (dquery, lax.optimization_barrier(jnp.sum(dkey, axis=0)), lax.optimization_barrier(jnp.sum(dvalue, axis=0)))
    dquery, dkey, dvalue = lax.map(backward_group, (qhead, khead, vhead, probs, rounded, capped, grad_heads))
    dquery = unrotate(jnp.transpose(dquery, (2, 0, 1, 3)), cosine[:, None, None, :], sine[:, None, None, :])
    dkey = unrotate(jnp.transpose(dkey, (1, 0, 2)), cosine[:, None, :], sine[:, None, :])
    dvalue = jnp.transpose(dvalue, (1, 0, 2))
    grad_proj = jnp.concatenate([dquery, dkey[:, :, None], dvalue[:, :, None]], axis=2).astype(jnp.bfloat16)
    grad_qkv = jnp.dot(normed.T, grad_proj.reshape(SEQ, KVH * parts * HDIM), preferred_element_type=jnp.float32)
    grad_qkv = grad_qkv.astype(jnp.bfloat16).reshape(D, KVH, parts, HDIM)
    mean_delta = lax.optimization_barrier(jnp.sum(outer_delta.astype(jnp.float32), axis=0)) / GROUPS
    new_momentum = 0.9 * momentum + mean_delta
    new_fragment = fragment - 0.7 * (mean_delta + 0.9 * new_momentum)
    return (output, grad_qkv, grad_out, new_momentum, new_fragment)
```

```python
import functools

import jax
import jax.numpy as jnp
from jax import lax
from jax.experimental import pallas as pl
from jax.experimental.pallas import tpu as pltpu
from jax.sharding import PartitionSpec as P

softcap = 50.0
query_scale = 1.0 / 12.0
MESH = pl.DeviceIdType.MESH
WIDTH = 4608
HALF = WIDTH // 2
ROWS = 64
N1, N2, NQ = 4 * 128, 12 * 128, 5 * 128
NP = N1 + N2


def place():
    group, fsdp = lax.axis_index("group"), lax.axis_index("fsdp")
    return group // 2, group % 2, fsdp // 8, (fsdp // 2) % 4, fsdp % 2


def device(x, zh, zl, y, c):
    return (x * 2 + zh, (zl * 4 + y) * 2 + c)


class Sender:
    def __init__(self, sems):
        self.sems, self.copies = sems, []

    def __call__(self, src, dst, recv, to):
        copy = pltpu.make_async_remote_copy(
            src_ref=src,
            dst_ref=dst,
            send_sem=self.sems.at[len(self.copies)],
            recv_sem=recv,
            device_id=to,
            device_id_type=MESH,
        )
        copy.start()
        self.copies.append(copy)

    def arrived(self, ref, recv, to):
        pltpu.make_async_remote_copy(
            src_ref=ref,
            dst_ref=ref,
            send_sem=self.sems.at[0],
            recv_sem=recv,
            device_id=to,
            device_id_type=MESH,
        ).wait_recv()

    def finish(self):
        for copy in self.copies:
            copy.wait_send()


SPREAD_SENDS = 57


def spread(own, full, send, piece_sems, pair_sems, local_sem):
    x, zh, zl, y, c = place()
    k, kz = zl * 4 + y, (1 - zl) * 4 + y
    ys = [(y + 1) % 4, (y + 3) % 4, (y + 2) % 4]
    to_sib = device(x, zh, zl, y, 1 - c)
    to_z = device(x, zh, 1 - zl, y, c)
    to_y = [device(x, zh, zl, yy, c) for yy in ys]
    to_x = [device(xx, zh, zl, y, c) for xx in [(x + 1) % 4, (x + 3) % 4, (x + 2) % 4]]
    quarter = lambda w: pl.ds(pl.multiple_of(NP + w * NQ, 128), NQ)
    cols = {"a": pl.ds(0, N1), "b": pl.ds(N1, N2), "q": quarter(x)}
    index = {"a": 0, "b": 1, "q": 2 + x}

    def block(kk, t):
        return full.at[2 * kk + c, :, cols[t]]

    def push(kk, t, to):
        src = own.at[:, cols[t]] if kk is k else block(kk, t)
        send(src, block(kk, t), piece_sems.at[index[t], kk], to)

    def await_piece(kk, t):
        send.arrived(block(kk, t), piece_sems.at[index[t], kk], to_sib)

    def pair(kk, lo, size, slot):
        ref = full.at[2 * kk + c, :, pl.ds(lo, size)]
        send(ref, ref, pair_sems.at[kk, slot], to_sib)

    keep = pltpu.make_async_copy(own, full.at[2 * k + c], local_sem)
    keep.start()
    for t in ("q", "a"):
        push(k, t, to_z)
    for t in ("b", "q", "a"):
        for to in to_y:
            push(k, t, to)
    push(k, "b", to_z)
    send(own, full.at[2 * k + c], pair_sems.at[k, 0], to_sib)

    for t in ("q", "a"):
        await_piece(kz, t)
        for to in to_y:
            push(kz, t, to)
    for to in to_x:
        push(kz, "q", to)
    for yy in ys:
        kk = zl * 4 + yy
        await_piece(kk, "b")
        push(kk, "b", to_z)
        await_piece(kk, "q")
        for to in to_x:
            push(kk, "q", to)
        await_piece(kk, "a")
        pair(kk, 0, NP, 0)
    await_piece(kz, "b")
    pair(kz, 0, NP, 0)
    for yy in ys:
        kk = (1 - zl) * 4 + yy
        await_piece(kk, "q")
        for to in to_x:
            push(kk, "q", to)
        await_piece(kk, "a")
        await_piece(kk, "b")
        pair(kk, 0, NP, 0)
    others = [kz] + [zl * 4 + yy for yy in ys] + [(1 - zl) * 4 + yy for yy in ys]
    for kk in others:
        for step in (1, 3, 2):
            w = (x + step) % 4
            send.arrived(full.at[2 * kk + c, :, quarter(w)], piece_sems.at[2 + w, kk], to_sib)
        pair(kk, NP, 4 * NQ, 1)
    send.arrived(full.at[2 * k + 1 - c], pair_sems.at[k, 0], to_sib)
    for kk in others:
        send.arrived(full.at[2 * kk + 1 - c, :, pl.ds(0, NP)], pair_sems.at[kk, 0], to_sib)
        send.arrived(full.at[2 * kk + 1 - c, :, pl.ds(NP, 4 * NQ)], pair_sems.at[kk, 1], to_sib)
    keep.wait()


def near():
    x, zh, zl, y, c = place()
    out = [device(x, zh, zl, y, 1 - c), device(x, zh, 1 - zl, y, c)]
    out += [device(x, zh, zl, (y + s) % 4, c) for s in (1, 2, 3)]
    return out + [device((x + s) % 4, zh, zl, y, c) for s in (1, 2, 3)]


def greet(devices):
    barrier = pltpu.get_barrier_semaphore()
    for to in devices:
        pl.semaphore_signal(barrier, inc=1, device_id=to, device_id_type=MESH)


def met(devices):
    pl.semaphore_wait(pltpu.get_barrier_semaphore(), len(devices))


def normed_kernel(tokens, gain, full, own, send_sems, piece_sems, pair_sems, local_sem):
    greet(near())
    values = tokens[...].astype(jnp.float32)
    scale = lax.rsqrt(jnp.mean(values * values, axis=-1, keepdims=True) + 1e-06)
    own[...] = (values * scale * gain[...]).astype(jnp.bfloat16)
    met(near())
    send = Sender(send_sems)
    spread(own, full, send, piece_sems, pair_sems, local_sem)
    send.finish()


def gather_normed(tokens, gain):
    vmem = pl.BlockSpec(memory_space=pltpu.VMEM)
    return pl.pallas_call(
        normed_kernel,
        out_shape=jax.ShapeDtypeStruct((16, ROWS, WIDTH), jnp.bfloat16),
        in_specs=[vmem, vmem],
        out_specs=pl.BlockSpec(memory_space=pl.ANY),
        scratch_shapes=[
            pltpu.VMEM((ROWS, WIDTH), jnp.bfloat16),
            pltpu.SemaphoreType.DMA((SPREAD_SENDS,)),
            pltpu.SemaphoreType.DMA((6, 8)),
            pltpu.SemaphoreType.DMA((8, 2)),
            pltpu.SemaphoreType.DMA,
        ],
        compiler_params=pltpu.CompilerParams(
            collective_id=0, has_side_effects=True, vmem_limit_bytes=24 * 2**20
        ),
        name="gather_normed",
    )(tokens, gain)


def stacked(rows):
    return jnp.concatenate([rows[:, :HALF], rows[:, HALF:]], axis=0)


def unstacked(rows):
    return jnp.concatenate([rows[:8], rows[8:]], axis=1)


def middle_kernel(
    heads, weight, tokens, cotangent, gain, output, full,
    partial, received, mate, total, mine, group_in, own,
    send_sems, mate_sem, part_sems, group_sems, piece_sems, pair_sems, local_sem,
):
    x, zh, zl, y, c = place()
    k, g = zl * 4 + y, x * 2 + zh
    sib = device(x, zh, zl, y, 1 - c)
    chips = [(a, b) for a in range(2) for b in range(4)][1:]
    fellows = [((zl + a) % 2, (y + b) % 4) for a, b in chips]
    to_fellows = [device(x, zh, a, b, c) for a, b in fellows]
    kin = [((x + b) % 4, (zh + a) % 2) for a, b in chips]
    to_kin = [device(a, b, zl, y, c) for a, b in kin]
    greet([sib] + to_fellows + to_kin)
    for core in range(2):
        left = jnp.dot(heads[pl.ds(core * 64, 64)], weight[:, pl.ds(0, HALF)], preferred_element_type=jnp.float32)
        right = jnp.dot(heads[pl.ds(core * 64, 64)], weight[:, pl.ds(HALF, HALF)], preferred_element_type=jnp.float32)
        for kk in range(8):
            both = jnp.concatenate([left[kk * 8 : kk * 8 + 8], right[kk * 8 : kk * 8 + 8]], axis=0)
            partial[core, kk] = both.astype(jnp.bfloat16)
    met([sib] + to_fellows + to_kin)
    send = Sender(send_sems)
    send(partial.at[1 - c], mate, mate_sem, sib)
    send.arrived(mate, mate_sem, sib)
    for kk in range(8):
        total[kk] = (partial[c, kk].astype(jnp.float32) + mate[kk].astype(jnp.float32)).astype(jnp.bfloat16)
    for (a, b), to in zip(fellows, to_fellows):
        send(total.at[a * 4 + b], received.at[k], part_sems.at[k], to)
    both = partial[c, k].astype(jnp.float32) + mate[k].astype(jnp.float32)
    for a, b in fellows:
        kk = a * 4 + b
        send.arrived(received.at[kk], part_sems.at[kk], sib)
        both = both + received[kk].astype(jnp.float32)
    attn = unstacked(both)
    scale = lax.rsqrt(jnp.mean(attn * attn, axis=-1, keepdims=True) + 1e-06)
    normal = attn * scale
    out = tokens[...] + normal * gain[...]
    dnorm = cotangent[...] * gain[...]
    grad = scale * (dnorm - normal * jnp.mean(dnorm * normal, axis=-1, keepdims=True))
    mine[0] = stacked(grad).astype(jnp.bfloat16)
    mine[1] = stacked(out).astype(jnp.bfloat16)
    for i in range(2):
        for to in to_kin:
            send(mine.at[i], group_in.at[i, g], group_sems.at[i, g], to)
    group_in[0, g] = mine[0]
    group_in[1, g] = mine[1]
    for a, b in kin:
        gg = a * 2 + b
        send.arrived(group_in.at[0, gg], group_sems.at[0, gg], sib)
    for gg in range(0, 8, 2):
        first = unstacked(group_in[0, gg].astype(jnp.float32))
        second = unstacked(group_in[0, gg + 1].astype(jnp.float32))
        own[pl.ds(gg * 8, 16), :] = jnp.concatenate([first, second], axis=0).astype(jnp.bfloat16)
    spread(own, full, send, piece_sems, pair_sems, local_sem)
    for a, b in kin:
        gg = a * 2 + b
        send.arrived(group_in.at[1, gg], group_sems.at[1, gg], sib)
    for gg in range(0, 8, 2):
        first = unstacked(group_in[1, gg].astype(jnp.float32))
        second = unstacked(group_in[1, gg + 1].astype(jnp.float32))
        output[pl.ds(gg * 8, 16), :] = jnp.concatenate([first, second], axis=0).astype(jnp.bfloat16)
    send.finish()


def middle(heads, weight, tokens, cotangent, gain):
    vmem = pl.BlockSpec(memory_space=pltpu.VMEM)
    return pl.pallas_call(
        middle_kernel,
        out_shape=(
            jax.ShapeDtypeStruct((ROWS, WIDTH), jnp.bfloat16),
            jax.ShapeDtypeStruct((16, ROWS, WIDTH), jnp.bfloat16),
        ),
        in_specs=[vmem] * 5,
        out_specs=(vmem, pl.BlockSpec(memory_space=pl.ANY)),
        scratch_shapes=[
            pltpu.VMEM((2, 8, 16, HALF), jnp.bfloat16),
            pltpu.VMEM((8, 16, HALF), jnp.bfloat16),
            pltpu.VMEM((8, 16, HALF), jnp.bfloat16),
            pltpu.VMEM((8, 16, HALF), jnp.bfloat16),
            pltpu.VMEM((2, 16, HALF), jnp.bfloat16),
            pltpu.VMEM((2, 8, 16, HALF), jnp.bfloat16),
            pltpu.VMEM((ROWS, WIDTH), jnp.bfloat16),
            pltpu.SemaphoreType.DMA((1 + 7 + 14 + SPREAD_SENDS,)),
            pltpu.SemaphoreType.DMA,
            pltpu.SemaphoreType.DMA((8,)),
            pltpu.SemaphoreType.DMA((2, 8)),
            pltpu.SemaphoreType.DMA((6, 8)),
            pltpu.SemaphoreType.DMA((8, 2)),
            pltpu.SemaphoreType.DMA,
        ],
        compiler_params=pltpu.CompilerParams(
            collective_id=1, has_side_effects=True, vmem_limit_bytes=32 * 2**20
        ),
        name="middle",
    )(heads, weight, tokens, cotangent, gain)


def tables(length, width):
    half = width // 2
    positions = jnp.arange(length, dtype=jnp.float32)[:, None]
    freqs = jnp.power(jnp.float32(10000.0), -(2.0 * jnp.arange(half, dtype=jnp.float32) / width))
    angle = positions * freqs[None, :]
    return (jnp.cos(angle), jnp.sin(angle))


def rotate(values, cosine, sine):
    half = values.shape[-1] // 2
    first, second = (values[..., :half], values[..., half:])
    return jnp.concatenate(
        [first * cosine - second * sine, second * cosine + first * sine], axis=-1
    )


def unrotate(grads, cosine, sine):
    half = grads.shape[-1] // 2
    first, second = (grads[..., :half], grads[..., half:])
    return jnp.concatenate(
        [first * cosine + second * sine, second * cosine - first * sine], axis=-1
    )


def attend(query, keyed, valued, allowed):
    scores = jnp.dot(query, keyed.T, preferred_element_type=jnp.float32) * query_scale
    capped = softcap * jnp.tanh(scores / softcap)
    weights = jnp.where(allowed, jnp.exp(capped), jnp.float32(0.0))
    probs = weights / jnp.sum(weights, axis=-1, keepdims=True)
    rounded = probs.astype(jnp.bfloat16)
    result = jnp.dot(rounded, valued, preferred_element_type=jnp.float32)
    return (result, probs, rounded, capped)


def attend_back(query, keyed, valued, probs, rounded, capped, grad_head):
    dprob = jnp.dot(grad_head, valued.T, preferred_element_type=jnp.float32)
    dvalue = jnp.dot(rounded.T, grad_head, preferred_element_type=jnp.float32)
    dcap = probs * (dprob - jnp.sum(dprob * probs, axis=-1, keepdims=True))
    dscore = (dcap * (1.0 - (capped / softcap) ** 2) * query_scale).astype(jnp.bfloat16)
    dquery = jnp.dot(dscore, keyed, preferred_element_type=jnp.float32)
    dkey = jnp.dot(dscore.T, query, preferred_element_type=jnp.float32)
    return (dquery, dkey, dvalue)


def nesterov(mean_delta, moment_part, params_part):
    moment_next = 0.9 * moment_part + mean_delta
    return (moment_next, params_part - 0.7 * (mean_delta + 0.9 * moment_next))


def local(
    tokens,
    pre_gain,
    post_gain,
    qkv_weight,
    out_weight,
    doc_ids,
    cotangent,
    outer_delta,
    momentum,
    fragment,
):
    group = lax.axis_index("group")
    gathered = gather_normed(tokens, pre_gain[None, :]).reshape(16 * ROWS, WIDTH)
    length, width = gathered.shape
    key_heads, parts, head_dim = (qkv_weight.shape[1], qkv_weight.shape[2], qkv_weight.shape[3])
    query_count = parts - 2
    proj = jnp.dot(
        gathered,
        qkv_weight.reshape(width, key_heads * parts * head_dim),
        preferred_element_type=jnp.float32,
    )
    proj = proj.reshape(length, key_heads, parts, head_dim)
    cosine, sine = tables(length, head_dim)
    cosine_four, sine_four = (cosine[:, None, None, :], sine[:, None, None, :])
    cosine_three, sine_three = (cosine[:, None, :], sine[:, None, :])
    queries = rotate(proj[:, :, :query_count], cosine_four, sine_four).astype(jnp.bfloat16)
    keys = rotate(proj[:, :, query_count], cosine_three, sine_three).astype(jnp.bfloat16)
    values = proj[:, :, query_count + 1].astype(jnp.bfloat16)
    position = jnp.arange(length, dtype=jnp.int32)
    allowed = (position[None, :] <= position[:, None]) & (doc_ids[None, :] == doc_ids[:, None])
    qhead = jnp.transpose(queries, (1, 2, 0, 3))
    khead = jnp.transpose(keys, (1, 0, 2))
    vhead = jnp.transpose(values, (1, 0, 2))

    def forward_group(query_set, keyed, valued):
        return jax.vmap(attend, in_axes=(0, None, None, None))(query_set, keyed, valued, allowed)

    result, probs, rounded, capped = jax.vmap(forward_group)(qhead, khead, vhead)
    heads = jnp.transpose(result.astype(jnp.bfloat16), (2, 0, 1, 3))
    head_flat = heads.reshape(length, key_heads * query_count * head_dim)
    out_flat = out_weight.reshape(key_heads * query_count * head_dim, width)
    share = lax.dynamic_slice_in_dim(head_flat.reshape(8, 2, 8, 8, 256), group, 1, axis=2)
    share = jnp.transpose(share[:, :, 0], (1, 0, 2, 3)).reshape(128, 256)
    own_tokens = lax.dynamic_slice_in_dim(tokens, group * 8, 8, axis=0).astype(jnp.float32)
    own_cotangent = lax.dynamic_slice_in_dim(cotangent, group * 8, 8, axis=0).astype(jnp.float32)
    output, grad_rows = middle(share, out_flat, own_tokens, own_cotangent, post_gain[None, :])
    grad_rows = grad_rows.reshape(length, width)
    grad_out = lax.dot_general(
        head_flat, grad_rows, (((0,), (0,)), ((), ())), preferred_element_type=jnp.float32
    )
    grad_out = grad_out.astype(jnp.bfloat16).reshape(out_weight.shape)
    grad_heads = lax.dot_general(
        grad_rows, out_flat, (((1,), (1,)), ((), ())), preferred_element_type=jnp.float32
    )
    grad_heads = grad_heads.astype(jnp.bfloat16).reshape(length, key_heads, query_count, head_dim)
    grad_heads = jnp.transpose(grad_heads, (1, 2, 0, 3))

    def backward_group(query_set, keyed, valued, prob_set, round_set, cap_set, grad_set):
        dquery, dkey, dvalue = jax.vmap(attend_back, in_axes=(0, None, None, 0, 0, 0, 0))(
            query_set, keyed, valued, prob_set, round_set, cap_set, grad_set
        )
        return (dquery, jnp.sum(dkey, axis=0), jnp.sum(dvalue, axis=0))

    dquery, dkey, dvalue = jax.vmap(backward_group)(
        qhead, khead, vhead, probs, rounded, capped, grad_heads
    )
    dquery = unrotate(jnp.transpose(dquery, (2, 0, 1, 3)), cosine_four, sine_four)
    dkey = unrotate(jnp.transpose(dkey, (1, 0, 2)), cosine_three, sine_three)
    dvalue = jnp.transpose(dvalue, (1, 0, 2))
    grad_proj = jnp.concatenate([dquery, dkey[:, :, None], dvalue[:, :, None]], axis=2).astype(
        jnp.bfloat16
    )
    grad_qkv = lax.dot_general(
        gathered,
        grad_proj.reshape(length, key_heads * parts * head_dim),
        (((0,), (0,)), ((), ())),
        preferred_element_type=jnp.float32,
    )
    grad_qkv = grad_qkv.astype(jnp.bfloat16).reshape(qkv_weight.shape)
    total = lax.psum(outer_delta[0], "group").astype(jnp.float32)
    new_momentum, new_fragment = nesterov(total / lax.axis_size("group"), momentum, fragment)
    return (output, grad_qkv, grad_out, new_momentum, new_fragment)


def solution(mesh):
    placed = (
        P("fsdp", None),
        P(),
        P(),
        P(None, "fsdp", None, None),
        P("fsdp", None, None, None),
        P(),
        P("fsdp", None),
        P("group", "fsdp", None),
        P("fsdp", None),
        P("fsdp", None),
    )
    return jax.shard_map(
        local,
        mesh=mesh,
        in_specs=placed,
        out_specs=(
            P("fsdp", None),
            P(None, "fsdp", None, None),
            P("fsdp", None, None, None),
            P("fsdp", None),
            P("fsdp", None),
        ),
        check_vma=False,
    )
```

```python
import functools

import jax
import jax.numpy as jnp
from jax import lax
from jax.experimental import pallas as pl
from jax.experimental.pallas import tpu as pltpu
from jax.sharding import PartitionSpec as P

softcap = 50.0
query_scale = 1.0 / 12.0
MESH = pl.DeviceIdType.MESH
WIDTH = 4608
HALF = WIDTH // 2
ROWS = 64
N1, N2, NQ = 4 * 128, 12 * 128, 5 * 128
NP = N1 + N2


def place():
    group, fsdp = lax.axis_index("group"), lax.axis_index("fsdp")
    return group // 2, group % 2, fsdp // 8, (fsdp // 2) % 4, fsdp % 2


def device(x, zh, zl, y, c):
    return (x * 2 + zh, (zl * 4 + y) * 2 + c)


class Sender:
    def __init__(self, sems):
        self.sems, self.copies = sems, []

    def __call__(self, src, dst, recv, to):
        copy = pltpu.make_async_remote_copy(
            src_ref=src,
            dst_ref=dst,
            send_sem=self.sems.at[len(self.copies)],
            recv_sem=recv,
            device_id=to,
            device_id_type=MESH,
        )
        copy.start()
        self.copies.append(copy)

    def arrived(self, ref, recv, to):
        pltpu.make_async_remote_copy(
            src_ref=ref,
            dst_ref=ref,
            send_sem=self.sems.at[0],
            recv_sem=recv,
            device_id=to,
            device_id_type=MESH,
        ).wait_recv()

    def finish(self):
        for copy in self.copies:
            copy.wait_send()


SPREAD_SENDS = 57


def spread(own, full, send, piece_sems, pair_sems, local_sem):
    x, zh, zl, y, c = place()
    k, kz = zl * 4 + y, (1 - zl) * 4 + y
    ys = [(y + 1) % 4, (y + 3) % 4, (y + 2) % 4]
    to_sib = device(x, zh, zl, y, 1 - c)
    to_z = device(x, zh, 1 - zl, y, c)
    to_y = [device(x, zh, zl, yy, c) for yy in ys]
    to_x = [device(xx, zh, zl, y, c) for xx in [(x + 1) % 4, (x + 3) % 4, (x + 2) % 4]]
    quarter = lambda w: pl.ds(pl.multiple_of(NP + w * NQ, 128), NQ)
    cols = {"a": pl.ds(0, N1), "b": pl.ds(N1, N2), "q": quarter(x)}
    index = {"a": 0, "b": 1, "q": 2 + x}

    def block(kk, t):
        return full.at[2 * kk + c, :, cols[t]]

    def push(kk, t, to):
        src = own.at[:, cols[t]] if kk is k else block(kk, t)
        send(src, block(kk, t), piece_sems.at[index[t], kk], to)

    def await_piece(kk, t):
        send.arrived(block(kk, t), piece_sems.at[index[t], kk], to_sib)

    def pair(kk, lo, size, slot):
        ref = full.at[2 * kk + c, :, pl.ds(lo, size)]
        send(ref, ref, pair_sems.at[kk, slot], to_sib)

    keep = pltpu.make_async_copy(own, full.at[2 * k + c], local_sem)
    keep.start()
    for t in ("q", "a"):
        push(k, t, to_z)
    for t in ("b", "q", "a"):
        for to in to_y:
            push(k, t, to)
    push(k, "b", to_z)
    send(own, full.at[2 * k + c], pair_sems.at[k, 0], to_sib)

    for t in ("q", "a"):
        await_piece(kz, t)
        for to in to_y:
            push(kz, t, to)
    for to in to_x:
        push(kz, "q", to)
    for yy in ys:
        kk = zl * 4 + yy
        await_piece(kk, "b")
        push(kk, "b", to_z)
        await_piece(kk, "q")
        for to in to_x:
            push(kk, "q", to)
        await_piece(kk, "a")
        pair(kk, 0, NP, 0)
    await_piece(kz, "b")
    pair(kz, 0, NP, 0)
    for yy in ys:
        kk = (1 - zl) * 4 + yy
        await_piece(kk, "q")
        for to in to_x:
            push(kk, "q", to)
        await_piece(kk, "a")
        await_piece(kk, "b")
        pair(kk, 0, NP, 0)
    others = [kz] + [zl * 4 + yy for yy in ys] + [(1 - zl) * 4 + yy for yy in ys]
    for kk in others:
        for step in (1, 3, 2):
            w = (x + step) % 4
            send.arrived(full.at[2 * kk + c, :, quarter(w)], piece_sems.at[2 + w, kk], to_sib)
        pair(kk, NP, 4 * NQ, 1)
    send.arrived(full.at[2 * k + 1 - c], pair_sems.at[k, 0], to_sib)
    for kk in others:
        send.arrived(full.at[2 * kk + 1 - c, :, pl.ds(0, NP)], pair_sems.at[kk, 0], to_sib)
        send.arrived(full.at[2 * kk + 1 - c, :, pl.ds(NP, 4 * NQ)], pair_sems.at[kk, 1], to_sib)
    keep.wait()


def near():
    x, zh, zl, y, c = place()
    out = [device(x, zh, zl, y, 1 - c), device(x, zh, 1 - zl, y, c)]
    out += [device(x, zh, zl, (y + s) % 4, c) for s in (1, 2, 3)]
    return out + [device((x + s) % 4, zh, zl, y, c) for s in (1, 2, 3)]


def greet(devices):
    barrier = pltpu.get_barrier_semaphore()
    for to in devices:
        pl.semaphore_signal(barrier, inc=1, device_id=to, device_id_type=MESH)


def met(devices):
    pl.semaphore_wait(pltpu.get_barrier_semaphore(), len(devices))


def normed_kernel(tokens, gain, full, own, send_sems, piece_sems, pair_sems, local_sem):
    greet(near())
    values = tokens[...].astype(jnp.float32)
    scale = lax.rsqrt(jnp.mean(values * values, axis=-1, keepdims=True) + 1e-06)
    own[...] = (values * scale * gain[...]).astype(jnp.bfloat16)
    met(near())
    send = Sender(send_sems)
    spread(own, full, send, piece_sems, pair_sems, local_sem)
    send.finish()


def gather_normed(tokens, gain):
    vmem = pl.BlockSpec(memory_space=pltpu.VMEM)
    return pl.pallas_call(
        normed_kernel,
        out_shape=jax.ShapeDtypeStruct((16, ROWS, WIDTH), jnp.bfloat16),
        in_specs=[vmem, vmem],
        out_specs=pl.BlockSpec(memory_space=pl.ANY),
        scratch_shapes=[
            pltpu.VMEM((ROWS, WIDTH), jnp.bfloat16),
            pltpu.SemaphoreType.DMA((SPREAD_SENDS,)),
            pltpu.SemaphoreType.DMA((6, 8)),
            pltpu.SemaphoreType.DMA((8, 2)),
            pltpu.SemaphoreType.DMA,
        ],
        compiler_params=pltpu.CompilerParams(
            collective_id=0, has_side_effects=True, vmem_limit_bytes=24 * 2**20
        ),
        name="gather_normed",
    )(tokens, gain)


def stacked(rows):
    return jnp.concatenate([rows[:, :HALF], rows[:, HALF:]], axis=0)


def unstacked(rows):
    return jnp.concatenate([rows[:8], rows[8:]], axis=1)


def middle_kernel(
    heads, weight, tokens, cotangent, gain, output, full,
    partial, received, mate, total, mine, group_in, own,
    send_sems, mate_sem, part_sems, group_sems, piece_sems, pair_sems, local_sem,
):
    x, zh, zl, y, c = place()
    k, g = zl * 4 + y, x * 2 + zh
    sib = device(x, zh, zl, y, 1 - c)
    chips = [(a, b) for a in range(2) for b in range(4)][1:]
    fellows = [((zl + a) % 2, (y + b) % 4) for a, b in chips]
    to_fellows = [device(x, zh, a, b, c) for a, b in fellows]
    kin = [((x + b) % 4, (zh + a) % 2) for a, b in chips]
    to_kin = [device(a, b, zl, y, c) for a, b in kin]
    greet([sib] + to_fellows + to_kin)
    for core in range(2):
        left = jnp.dot(heads[pl.ds(core * 64, 64)], weight[:, pl.ds(0, HALF)], preferred_element_type=jnp.float32)
        right = jnp.dot(heads[pl.ds(core * 64, 64)], weight[:, pl.ds(HALF, HALF)], preferred_element_type=jnp.float32)
        for kk in range(8):
            both = jnp.concatenate([left[kk * 8 : kk * 8 + 8], right[kk * 8 : kk * 8 + 8]], axis=0)
            partial[core, kk] = both.astype(jnp.bfloat16)
    met([sib] + to_fellows + to_kin)
    send = Sender(send_sems)
    send(partial.at[1 - c], mate, mate_sem, sib)
    send.arrived(mate, mate_sem, sib)
    for kk in range(8):
        total[kk] = (partial[c, kk].astype(jnp.float32) + mate[kk].astype(jnp.float32)).astype(jnp.bfloat16)
    for (a, b), to in zip(fellows, to_fellows):
        send(total.at[a * 4 + b], received.at[k], part_sems.at[k], to)
    both = partial[c, k].astype(jnp.float32) + mate[k].astype(jnp.float32)
    for a, b in fellows:
        kk = a * 4 + b
        send.arrived(received.at[kk], part_sems.at[kk], sib)
        both = both + received[kk].astype(jnp.float32)
    attn = unstacked(both)
    scale = lax.rsqrt(jnp.mean(attn * attn, axis=-1, keepdims=True) + 1e-06)
    normal = attn * scale
    out = tokens[...] + normal * gain[...]
    dnorm = cotangent[...] * gain[...]
    grad = scale * (dnorm - normal * jnp.mean(dnorm * normal, axis=-1, keepdims=True))
    mine[0] = stacked(grad).astype(jnp.bfloat16)
    mine[1] = stacked(out).astype(jnp.bfloat16)
    for i in range(2):
        for to in to_kin:
            send(mine.at[i], group_in.at[i, g], group_sems.at[i, g], to)
    group_in[0, g] = mine[0]
    group_in[1, g] = mine[1]
    for a, b in kin:
        gg = a * 2 + b
        send.arrived(group_in.at[0, gg], group_sems.at[0, gg], sib)
    for gg in range(0, 8, 2):
        first = unstacked(group_in[0, gg].astype(jnp.float32))
        second = unstacked(group_in[0, gg + 1].astype(jnp.float32))
        own[pl.ds(gg * 8, 16), :] = jnp.concatenate([first, second], axis=0).astype(jnp.bfloat16)
    spread(own, full, send, piece_sems, pair_sems, local_sem)
    for a, b in kin:
        gg = a * 2 + b
        send.arrived(group_in.at[1, gg], group_sems.at[1, gg], sib)
    for gg in range(0, 8, 2):
        first = unstacked(group_in[1, gg].astype(jnp.float32))
        second = unstacked(group_in[1, gg + 1].astype(jnp.float32))
        output[pl.ds(gg * 8, 16), :] = jnp.concatenate([first, second], axis=0).astype(jnp.bfloat16)
    send.finish()


def middle(heads, weight, tokens, cotangent, gain):
    vmem = pl.BlockSpec(memory_space=pltpu.VMEM)
    return pl.pallas_call(
        middle_kernel,
        out_shape=(
            jax.ShapeDtypeStruct((ROWS, WIDTH), jnp.bfloat16),
            jax.ShapeDtypeStruct((16, ROWS, WIDTH), jnp.bfloat16),
        ),
        in_specs=[vmem] * 5,
        out_specs=(vmem, pl.BlockSpec(memory_space=pl.ANY)),
        scratch_shapes=[
            pltpu.VMEM((2, 8, 16, HALF), jnp.bfloat16),
            pltpu.VMEM((8, 16, HALF), jnp.bfloat16),
            pltpu.VMEM((8, 16, HALF), jnp.bfloat16),
            pltpu.VMEM((8, 16, HALF), jnp.bfloat16),
            pltpu.VMEM((2, 16, HALF), jnp.bfloat16),
            pltpu.VMEM((2, 8, 16, HALF), jnp.bfloat16),
            pltpu.VMEM((ROWS, WIDTH), jnp.bfloat16),
            pltpu.SemaphoreType.DMA((1 + 7 + 14 + SPREAD_SENDS,)),
            pltpu.SemaphoreType.DMA,
            pltpu.SemaphoreType.DMA((8,)),
            pltpu.SemaphoreType.DMA((2, 8)),
            pltpu.SemaphoreType.DMA((6, 8)),
            pltpu.SemaphoreType.DMA((8, 2)),
            pltpu.SemaphoreType.DMA,
        ],
        compiler_params=pltpu.CompilerParams(
            collective_id=1, has_side_effects=True, vmem_limit_bytes=32 * 2**20
        ),
        name="middle",
    )(heads, weight, tokens, cotangent, gain)


def tables(length, width):
    half = width // 2
    positions = jnp.arange(length, dtype=jnp.float32)[:, None]
    freqs = jnp.power(jnp.float32(10000.0), -(2.0 * jnp.arange(half, dtype=jnp.float32) / width))
    angle = positions * freqs[None, :]
    return (jnp.cos(angle), jnp.sin(angle))


BLOCK = 256
STEPS = 4


def turn(values, cosine, sine):
    return values * cosine + pltpu.roll(values, 64, 1) * sine


def scored(keys, queries, first_key, start_row, query_row):
    raw = lax.dot_general(keys, queries, (((1,), (1,)), ((), ())), preferred_element_type=jnp.float32)
    soft = jnp.tanh(raw * (query_scale / softcap))
    row = lax.broadcasted_iota(jnp.int32, raw.shape, 0) + first_key
    allowed = (row >= start_row) & (row <= query_row)
    return soft, jnp.where(allowed, jnp.exp(softcap * soft), 0.0)


def forward_kernel(
    starts, x, weight, cosine, sine, start_ref, query_ref, key_ref, value_ref, heads_ref, sums_ref, keep, keys, values_t
):
    i = pl.program_id(0)
    proj = jnp.dot(x[...], weight[...], preferred_element_type=jnp.float32)
    queries = [turn(proj[:, h * 128 : h * 128 + 128], cosine[...], sine[...]).astype(jnp.bfloat16) for h in range(2)]
    key = turn(proj[:, 256:384], cosine[...], sine[...]).astype(jnp.bfloat16)
    value = proj[:, 384:512]
    query_ref[:, :128] = queries[0]
    query_ref[:, 128:] = queries[1]
    key_ref[...] = key
    value_ref[...] = value.astype(jnp.bfloat16)
    keys[i] = key
    values_t[i] = value.T.astype(jnp.bfloat16)
    start_row = start_ref[...]
    query_row = lax.broadcasted_iota(jnp.int32, (1, BLOCK), 1) + i * BLOCK
    first = starts[i * BLOCK] // BLOCK

    def score(j, sums):
        out = []
        for h in range(2):
            _, e = scored(keys[j], queries[h], j * BLOCK, start_row, query_row)
            keep[h, j] = e
            out.append(sums[h] + jnp.sum(e, axis=0, keepdims=True))
        return tuple(out)

    zero = jnp.zeros((1, BLOCK), jnp.float32)
    sums = lax.fori_loop(first, i + 1, score, (zero, zero))
    inverse = [1.0 / s for s in sums]
    sums_ref[0:1, :] = inverse[0]
    sums_ref[1:2, :] = inverse[1]

    def mix(j, accs):
        out = []
        for h in range(2):
            p = (keep[h, j] * inverse[h]).astype(jnp.bfloat16)
            out.append(accs[h] + jnp.dot(values_t[j], p, preferred_element_type=jnp.float32))
        return tuple(out)

    zero = jnp.zeros((128, BLOCK), jnp.float32)
    accs = lax.fori_loop(first, i + 1, mix, (zero, zero))
    for h in range(2):
        heads_ref[:, h * 128 : h * 128 + 128] = accs[h].T.astype(jnp.bfloat16)


def forward(gathered, weight, cosine, sine, start):
    rows = lambda n: pl.BlockSpec((BLOCK, n), lambda i, s: (i, 0))
    return pl.pallas_call(
        forward_kernel,
        grid_spec=pltpu.PrefetchScalarGridSpec(
            num_scalar_prefetch=1,
            grid=(STEPS,),
            in_specs=[
                rows(WIDTH),
                pl.BlockSpec((WIDTH, 512), lambda i, s: (0, 0)),
                rows(128),
                rows(128),
                pl.BlockSpec((1, BLOCK), lambda i, s: (0, i)),
            ],
            out_specs=[rows(256), rows(128), rows(128), rows(256), pl.BlockSpec((8, BLOCK), lambda i, s: (0, i))],
            scratch_shapes=[
                pltpu.VMEM((2, STEPS, BLOCK, BLOCK), jnp.float32),
                pltpu.VMEM((STEPS, BLOCK, 128), jnp.bfloat16),
                pltpu.VMEM((STEPS, 128, BLOCK), jnp.bfloat16),
            ],
        ),
        out_shape=[
            jax.ShapeDtypeStruct((1024, 256), jnp.bfloat16),
            jax.ShapeDtypeStruct((1024, 128), jnp.bfloat16),
            jax.ShapeDtypeStruct((1024, 128), jnp.bfloat16),
            jax.ShapeDtypeStruct((1024, 256), jnp.bfloat16),
            jax.ShapeDtypeStruct((8, 1024), jnp.float32),
        ],
        compiler_params=pltpu.CompilerParams(vmem_limit_bytes=40 * 2**20),
        name="forward",
    )(start, gathered, weight, cosine, sine, start[None, :])


def backward_kernel(
    starts, grads, weight, heads, query_ref, key_ref, value_ref, inverse_ref, cosine, sine, start_ref,
    grad_proj, grad_out, total, slope, dprob, dkey, dvalue, keys_t,
):
    i = pl.program_id(0)

    @pl.when(i == 0)
    def _():
        dkey[...] = jnp.zeros_like(dkey)
        dvalue[...] = jnp.zeros_like(dvalue)

    heads_t = heads[...].astype(jnp.float32).T.astype(jnp.bfloat16)
    for n in range(0, WIDTH, 512):
        part = jnp.dot(heads_t, grads[:, n : n + 512], preferred_element_type=jnp.float32)

        @pl.when(i == 0)
        def _():
            total[:, n : n + 512] = part

        @pl.when((i > 0) & (i < STEPS - 1))
        def _():
            total[:, n : n + 512] += part

        @pl.when(i == STEPS - 1)
        def _():
            grad_out[:, n : n + 512] = (total[:, n : n + 512] + part).astype(jnp.bfloat16)

    grad_heads = lax.dot_general(
        grads[...], weight[...], (((1,), (1,)), ((), ())), preferred_element_type=jnp.float32
    ).astype(jnp.bfloat16)
    own = pl.ds(i * BLOCK, BLOCK)
    keys_t[i] = key_ref[own, :].astype(jnp.float32).T.astype(jnp.bfloat16)
    start_row = start_ref[...]
    query_row = lax.broadcasted_iota(jnp.int32, (1, BLOCK), 1) + i * BLOCK
    first = starts[i * BLOCK] // BLOCK
    head = [slice(h * 128, h * 128 + 128) for h in range(2)]
    queries = [query_ref[own, head[h]] for h in range(2)]
    grad = [grad_heads[:, head[h]] for h in range(2)]

    def score(j, sums):
        out = []
        at = pl.ds(j * BLOCK, BLOCK)
        for h in range(2):
            soft, e = scored(key_ref[at, :], queries[h], j * BLOCK, start_row, query_row)
            p = e * inverse_ref[h : h + 1, :]
            dp = lax.dot_general(
                value_ref[at, :], grad[h], (((1,), (1,)), ((), ())), preferred_element_type=jnp.float32
            )
            dvalue[at, :] += jnp.dot(p.astype(jnp.bfloat16), grad[h], preferred_element_type=jnp.float32)
            out.append(sums[h] + jnp.sum(p * dp, axis=0, keepdims=True))
            slope[h, j] = p * ((1.0 - soft * soft) * query_scale)
            dprob[h, j] = dp
        return tuple(out)

    zero = jnp.zeros((1, BLOCK), jnp.float32)
    sums = lax.fori_loop(first, i + 1, score, (zero, zero))

    def mix(j, accs):
        out = []
        at = pl.ds(j * BLOCK, BLOCK)
        for h in range(2):
            ds = (slope[h, j] * (dprob[h, j] - sums[h])).astype(jnp.bfloat16)
            dkey[at, :] += jnp.dot(ds, queries[h], preferred_element_type=jnp.float32)
            out.append(accs[h] + jnp.dot(keys_t[j], ds, preferred_element_type=jnp.float32))
        return tuple(out)

    zero = jnp.zeros((128, BLOCK), jnp.float32)
    accs = lax.fori_loop(first, i + 1, mix, (zero, zero))
    for h in range(2):
        grad_proj[own, head[h]] = turn(accs[h].T, cosine[own, :], -sine[own, :]).astype(jnp.bfloat16)

    @pl.when(i == STEPS - 1)
    def _():
        grad_proj[:, 256:384] = turn(dkey[...], cosine[...], -sine[...]).astype(jnp.bfloat16)
        grad_proj[:, 384:512] = dvalue[...].astype(jnp.bfloat16)


def backward(grads, weight, heads, query, key, value, inverse, cosine, sine, start):
    rows = lambda n: pl.BlockSpec((BLOCK, n), lambda i, s: (i, 0))
    whole = lambda *shape: pl.BlockSpec(shape, lambda i, s: (0, 0))
    return pl.pallas_call(
        backward_kernel,
        grid_spec=pltpu.PrefetchScalarGridSpec(
            num_scalar_prefetch=1,
            grid=(STEPS,),
            in_specs=[
                rows(WIDTH),
                whole(256, WIDTH),
                rows(256),
                whole(1024, 256),
                whole(1024, 128),
                whole(1024, 128),
                pl.BlockSpec((8, BLOCK), lambda i, s: (0, i)),
                whole(1024, 128),
                whole(1024, 128),
                pl.BlockSpec((1, BLOCK), lambda i, s: (0, i)),
            ],
            out_specs=[whole(1024, 512), whole(256, WIDTH)],
            scratch_shapes=[
                pltpu.VMEM((256, WIDTH), jnp.float32),
                pltpu.VMEM((2, STEPS, BLOCK, BLOCK), jnp.float32),
                pltpu.VMEM((2, STEPS, BLOCK, BLOCK), jnp.float32),
                pltpu.VMEM((1024, 128), jnp.float32),
                pltpu.VMEM((1024, 128), jnp.float32),
                pltpu.VMEM((STEPS, 128, BLOCK), jnp.bfloat16),
            ],
        ),
        out_shape=[
            jax.ShapeDtypeStruct((1024, 512), jnp.bfloat16),
            jax.ShapeDtypeStruct((256, WIDTH), jnp.bfloat16),
        ],
        compiler_params=pltpu.CompilerParams(vmem_limit_bytes=50 * 2**20),
        name="backward",
    )(start, grads, weight, heads, query, key, value, inverse, cosine, sine, start[None, :])


CHUNK = 512


def weight_grad_kernel(grad_proj, x, out, turned, mixed):
    @pl.when(pl.program_id(0) == 0)
    def _():
        turned[...] = grad_proj[...].astype(jnp.float32).T.astype(jnp.bfloat16)

    for j in range(4):
        part = jnp.dot(turned[j * 128 : j * 128 + 128, :], x[...], preferred_element_type=jnp.float32)
        mixed[pl.ds(j, CHUNK, stride=4), :] = part.T
    out[...] = mixed[...].astype(jnp.bfloat16)


def weight_grad(grad_proj, gathered):
    return pl.pallas_call(
        weight_grad_kernel,
        grid=(WIDTH // CHUNK,),
        in_specs=[
            pl.BlockSpec((1024, 512), lambda n: (0, 0)),
            pl.BlockSpec((1024, CHUNK), lambda n: (0, n)),
        ],
        out_specs=pl.BlockSpec((4 * CHUNK, 128), lambda n: (n, 0)),
        out_shape=jax.ShapeDtypeStruct((4 * WIDTH, 128), jnp.bfloat16),
        scratch_shapes=[pltpu.VMEM((512, 1024), jnp.bfloat16), pltpu.VMEM((4 * CHUNK, 128), jnp.float32)],
        compiler_params=pltpu.CompilerParams(vmem_limit_bytes=40 * 2**20),
        name="weight_grad",
    )(grad_proj, gathered)


def nesterov(mean_delta, moment_part, params_part):
    moment_next = 0.9 * moment_part + mean_delta
    return (moment_next, params_part - 0.7 * (mean_delta + 0.9 * moment_next))


def local(
    tokens,
    pre_gain,
    post_gain,
    qkv_weight,
    out_weight,
    doc_ids,
    cotangent,
    outer_delta,
    momentum,
    fragment,
):
    group = lax.axis_index("group")
    gathered = gather_normed(tokens, pre_gain[None, :]).reshape(16 * ROWS, WIDTH)
    length, width = gathered.shape
    cosine, sine = tables(length, 128)
    cosine = jnp.concatenate([cosine, cosine], axis=1)
    sine = jnp.concatenate([-sine, sine], axis=1)
    start = jnp.sum((doc_ids[None, :] < doc_ids[:, None]).astype(jnp.int32), axis=1)
    query, key, value, head_flat, inverse = forward(
        gathered, qkv_weight.reshape(width, 512), cosine, sine, start
    )
    out_flat = out_weight.reshape(256, width)
    share = lax.dynamic_slice_in_dim(head_flat.reshape(8, 2, 8, 8, 256), group, 1, axis=2)
    share = jnp.transpose(share[:, :, 0], (1, 0, 2, 3)).reshape(128, 256)
    own_tokens = lax.dynamic_slice_in_dim(tokens, group * 8, 8, axis=0).astype(jnp.float32)
    own_cotangent = lax.dynamic_slice_in_dim(cotangent, group * 8, 8, axis=0).astype(jnp.float32)
    output, grad_rows = middle(share, out_flat, own_tokens, own_cotangent, post_gain[None, :])
    grad_rows = grad_rows.reshape(length, width)
    grad_proj, grad_out = backward(
        grad_rows, out_flat, head_flat, query, key, value, inverse, cosine, sine, start
    )
    grad_out = grad_out.reshape(out_weight.shape)
    grad_qkv = weight_grad(grad_proj, gathered).reshape(qkv_weight.shape)
    total = lax.psum(outer_delta[0], "group").astype(jnp.float32)
    new_momentum, new_fragment = nesterov(total / lax.axis_size("group"), momentum, fragment)
    return (output, grad_qkv, grad_out, new_momentum, new_fragment)


def solution(mesh):
    placed = (
        P("fsdp", None),
        P(),
        P(),
        P(None, "fsdp", None, None),
        P("fsdp", None, None, None),
        P(),
        P("fsdp", None),
        P("group", "fsdp", None),
        P("fsdp", None),
        P("fsdp", None),
    )
    return jax.shard_map(
        local,
        mesh=mesh,
        in_specs=placed,
        out_specs=(
            P("fsdp", None),
            P(None, "fsdp", None, None),
            P("fsdp", None, None, None),
            P("fsdp", None),
            P("fsdp", None),
        ),
        check_vma=False,
    )
```

```python
import functools

import jax
import jax.numpy as jnp
import numpy as np
from jax import lax
from jax.experimental import pallas as pl
from jax.experimental.pallas import tpu as pltpu
from jax.sharding import PartitionSpec as P

softcap = 50.0
query_scale = 1.0 / 12.0
MESH = pl.DeviceIdType.MESH
WIDTH = 4608
HALF = WIDTH // 2
ROWS = 64
N1, N2, NQ = 10 * 128, 10 * 128, 4 * 128
NP = N1 + N2


def place():
    group, fsdp = lax.axis_index("group"), lax.axis_index("fsdp")
    return group // 2, group % 2, fsdp // 8, (fsdp // 2) % 4, fsdp % 2


def device(x, zh, zl, y, c):
    return (x * 2 + zh, (zl * 4 + y) * 2 + c)


class Sender:
    def __init__(self, sems):
        self.sems, self.copies = sems, []

    def __call__(self, src, dst, recv, to):
        copy = pltpu.make_async_remote_copy(
            src_ref=src,
            dst_ref=dst,
            send_sem=self.sems.at[len(self.copies)],
            recv_sem=recv,
            device_id=to,
            device_id_type=MESH,
        )
        copy.start()
        self.copies.append(copy)

    def arrived(self, ref, recv, to):
        pltpu.make_async_remote_copy(
            src_ref=ref,
            dst_ref=ref,
            send_sem=self.sems.at[0],
            recv_sem=recv,
            device_id=to,
            device_id_type=MESH,
        ).wait_recv()

    def finish(self):
        for copy in self.copies:
            copy.wait_send()


SPREAD_SENDS = 69


def spread(own, full, send, piece_sems, pair_sems, local_sem, work=iter(()), later=None):
    x, zh, zl, y, c = place()
    k, kz = zl * 4 + y, (1 - zl) * 4 + y
    near_k, near_kz = ([b * 4 + (y + s) % 4 for s in (1, 3, 2)] for b in (zl, 1 - zl))
    to_sib = device(x, zh, zl, y, 1 - c)
    to_z = device(x, zh, 1 - zl, y, c)
    to_y = [device(x, zh, zl, (y + s) % 4, c) for s in (1, 3)]
    to_x = [device((x + s) % 4, zh, zl, y, c) for s in (1, 3)]
    quarters = [x, (x + 1) % 4, (x + 3) % 4, (x + 2) % 4]
    starts = {"a": 0, "b": N1} | {w: NP + quarters[w] * NQ for w in range(4)}
    sizes = {"a": N1, "b": N2} | {w: NQ for w in range(4)}
    index = {"a": 0, "b": 1} | {w: 2 + quarters[w] for w in range(4)}

    def cols(t, half):
        lo, size = starts[t], sizes[t]
        if half is not None:
            size = size // 2
            lo = lo + half * size
        if not isinstance(lo, int):
            lo = pl.multiple_of(lo, 128)
        return pl.ds(lo, size)

    def push(kk, t, to, half=None):
        at = cols(t, half)
        src = own.at[:, at] if kk is k else full.at[2 * kk + c, :, at]
        send(src, full.at[2 * kk + c, :, at], piece_sems.at[half or 0, index[t], kk], to)

    def here(kk, t, half=None):
        next(work, None)
        send.arrived(full.at[2 * kk + c, :, cols(t, half)], piece_sems.at[half or 0, index[t], kk], to_sib)

    def pair(kk, lo, size, slot):
        ref = full.at[2 * kk + c, :, pl.ds(lo, size)]
        send(ref, ref, pair_sems.at[kk, slot], to_sib)

    def ring(kk, t, links, side):
        push(kk, t, links[1 - side], side)

    def both(kk, t, links):
        for to in links:
            push(kk, t, to)

    keep = pltpu.make_async_copy(own, full.at[2 * k + c], local_sem)
    keep.start()
    push(k, 0, to_z)
    both(k, 0, to_y)
    push(k, "a", to_z)
    both(k, "b", to_y)
    push(k, "b", to_z)
    both(k, "a", to_y)
    send(own, full.at[2 * k + c], pair_sems.at[k, 0], to_sib)

    here(kz, 0)
    both(kz, 0, to_y)
    both(kz, 0, to_x)
    for side in range(2):
        kk = near_k[side]
        here(kk, 0)
        ring(kk, 0, to_y, side)
        both(kk, 0, to_x)
    here(kz, "a")
    both(kz, "a", to_y)
    for side in range(2):
        kk = near_k[side]
        here(kk, "b")
        push(kk, "b", to_z)
        ring(kk, "b", to_y, side)
    for side in range(2):
        kk = near_kz[side]
        here(kk, 0)
        ring(kk, 0, to_y, side)
        both(kk, 0, to_x)
    here(near_k[2], 0, 0)
    here(near_k[2], 0, 1)
    both(near_k[2], 0, to_x)
    for side in range(2):
        kk = near_k[side]
        here(kk, "a")
        ring(kk, "a", to_y, side)
        pair(kk, 0, NP, 0)
    here(near_k[2], "b", 0)
    here(near_k[2], "b", 1)
    push(near_k[2], "b", to_z)
    here(near_kz[2], 0, 0)
    here(near_kz[2], 0, 1)
    both(near_kz[2], 0, to_x)
    for side in range(2):
        here(near_kz[side], "a")
        ring(near_kz[side], "a", to_y, side)
    others = [kz, near_k[0], near_k[1], near_kz[0], near_kz[1], near_k[2], near_kz[2]]
    for kk in others[:5]:
        for side in range(2):
            here(kk, 1 + side)
            ring(kk, 1 + side, to_x, side)
    here(kz, "b")
    pair(kz, 0, NP, 0)
    for kk in others[5:]:
        for side in range(2):
            here(kk, 1 + side)
            ring(kk, 1 + side, to_x, side)
    if later is not None:
        later()
    here(near_k[2], "a", 0)
    here(near_k[2], "a", 1)
    pair(near_k[2], 0, NP, 0)
    for side in range(2):
        here(near_kz[side], "b")
        pair(near_kz[side], 0, NP, 0)
    for kk in others[:5]:
        here(kk, 3, 0)
        here(kk, 3, 1)
        pair(kk, NP, 4 * NQ, 1)
    here(near_kz[2], "a", 0)
    here(near_kz[2], "a", 1)
    here(near_kz[2], "b")
    pair(near_kz[2], 0, NP, 0)
    for kk in others[5:]:
        here(kk, 3, 0)
        here(kk, 3, 1)
        pair(kk, NP, 4 * NQ, 1)
    for _ in work:
        pass
    send.arrived(full.at[2 * k + 1 - c], pair_sems.at[k, 0], to_sib)
    for kk in others:
        send.arrived(full.at[2 * kk + 1 - c, :, pl.ds(0, NP)], pair_sems.at[kk, 0], to_sib)
        send.arrived(full.at[2 * kk + 1 - c, :, pl.ds(NP, 4 * NQ)], pair_sems.at[kk, 1], to_sib)
    keep.wait()


def near():
    x, zh, zl, y, c = place()
    out = [device(x, zh, zl, y, 1 - c), device(x, zh, 1 - zl, y, c)]
    out += [device(x, zh, zl, (y + s) % 4, c) for s in (1, 3)]
    return out + [device((x + s) % 4, zh, zl, y, c) for s in (1, 3)]


def greet(devices):
    barrier = pltpu.get_barrier_semaphore()
    for to in devices:
        pl.semaphore_signal(barrier, inc=1, device_id=to, device_id_type=MESH)


def met(devices):
    pl.semaphore_wait(pltpu.get_barrier_semaphore(), len(devices))


PARTS = 8
PART = WIDTH // PARTS


def weight_parts(weight, wide, rough, mixed, flat, in_sems, out_sems):
    def load(n):
        return pltpu.make_async_copy(weight.at[pl.ds(4 * PART * n, 4 * PART), :], rough.at[n % 2], in_sems.at[n])

    def store(n):
        return pltpu.make_async_copy(flat.at[n % 2], wide.at[pl.ds(PART * n, PART), :], out_sems.at[n])

    load(0).start()
    for n in range(PARTS):
        if n + 1 < PARTS:
            load(n + 1).start()
        yield
        load(n).wait()
        mixed[...] = rough[n % 2].astype(jnp.float32)
        if n >= 2:
            store(n - 2).wait()
        for j in range(4):
            flat[n % 2, :, j * 128 : j * 128 + 128] = mixed[pl.ds(j, PART, stride=4), :].astype(jnp.bfloat16)
        store(n).start()
    store(PARTS - 2).wait()
    store(PARTS - 1).wait()


def normed_kernel(
    tokens, gain, weight, full, wide, own, rough, mixed, flat,
    send_sems, piece_sems, pair_sems, local_sem, in_sems, out_sems,
):
    work = weight_parts(weight, wide, rough, mixed, flat, in_sems, out_sems)
    next(work)
    greet(near())
    values = tokens[...].astype(jnp.float32)
    scale = lax.rsqrt(jnp.mean(values * values, axis=-1, keepdims=True) + 1e-06)
    own[...] = (values * scale * gain[...]).astype(jnp.bfloat16)
    met(near())
    send = Sender(send_sems)
    spread(own, full, send, piece_sems, pair_sems, local_sem, work)
    send.finish()


def gather_normed(tokens, gain, weight):
    vmem = pl.BlockSpec(memory_space=pltpu.VMEM)
    return pl.pallas_call(
        normed_kernel,
        out_shape=(
            jax.ShapeDtypeStruct((16, ROWS, WIDTH), jnp.bfloat16),
            jax.ShapeDtypeStruct((WIDTH, 512), jnp.bfloat16),
        ),
        in_specs=[vmem, vmem, pl.BlockSpec(memory_space=pl.ANY)],
        out_specs=(pl.BlockSpec(memory_space=pl.ANY), pl.BlockSpec(memory_space=pl.ANY)),
        scratch_shapes=[
            pltpu.VMEM((ROWS, WIDTH), jnp.bfloat16),
            pltpu.VMEM((2, 4 * PART, 128), jnp.bfloat16),
            pltpu.VMEM((4 * PART, 128), jnp.float32),
            pltpu.VMEM((2, PART, 512), jnp.bfloat16),
            pltpu.SemaphoreType.DMA((SPREAD_SENDS,)),
            pltpu.SemaphoreType.DMA((2, 6, 8)),
            pltpu.SemaphoreType.DMA((8, 2)),
            pltpu.SemaphoreType.DMA,
            pltpu.SemaphoreType.DMA((PARTS,)),
            pltpu.SemaphoreType.DMA((PARTS,)),
        ],
        compiler_params=pltpu.CompilerParams(
            collective_id=0, has_side_effects=True, vmem_limit_bytes=60 * 2**20
        ),
        name="gather_normed",
    )(tokens, gain, weight)


def stacked(rows):
    return jnp.concatenate([rows[:, :HALF], rows[:, HALF:]], axis=0)


def unstacked(rows):
    return jnp.concatenate([rows[:8], rows[8:]], axis=1)


def middle_kernel(
    heads, weight, tokens, cotangent, gain, output, full,
    partial, received, mate, total, mine, group_in, own,
    send_sems, mate_sem, part_sems, group_sems, piece_sems, pair_sems, local_sem,
):
    x, zh, zl, y, c = place()
    k, g = zl * 4 + y, x * 2 + zh
    sib = device(x, zh, zl, y, 1 - c)
    chips = [(a, b) for a in range(2) for b in range(4)][1:]
    fellows = [((zl + a) % 2, (y + b) % 4) for a, b in chips]
    to_fellows = [device(x, zh, a, b, c) for a, b in fellows]
    kin = [((x + b) % 4, (zh + a) % 2) for a, b in chips]
    to_kin = [device(a, b, zl, y, c) for a, b in kin]
    greet([sib] + to_fellows + to_kin)
    for core in range(2):
        left = jnp.dot(heads[pl.ds(core * 64, 64)], weight[:, pl.ds(0, HALF)], preferred_element_type=jnp.float32)
        right = jnp.dot(heads[pl.ds(core * 64, 64)], weight[:, pl.ds(HALF, HALF)], preferred_element_type=jnp.float32)
        for kk in range(8):
            both = jnp.concatenate([left[kk * 8 : kk * 8 + 8], right[kk * 8 : kk * 8 + 8]], axis=0)
            partial[core, kk] = both.astype(jnp.bfloat16)
    met([sib] + to_fellows + to_kin)
    send = Sender(send_sems)
    send(partial.at[1 - c], mate, mate_sem, sib)
    send.arrived(mate, mate_sem, sib)
    for kk in range(8):
        total[kk] = (partial[c, kk].astype(jnp.float32) + mate[kk].astype(jnp.float32)).astype(jnp.bfloat16)
    for (a, b), to in zip(fellows, to_fellows):
        send(total.at[a * 4 + b], received.at[k], part_sems.at[k], to)
    both = partial[c, k].astype(jnp.float32) + mate[k].astype(jnp.float32)
    for a, b in fellows:
        kk = a * 4 + b
        send.arrived(received.at[kk], part_sems.at[kk], sib)
        both = both + received[kk].astype(jnp.float32)
    attn = unstacked(both)
    scale = lax.rsqrt(jnp.mean(attn * attn, axis=-1, keepdims=True) + 1e-06)
    normal = attn * scale
    out = tokens[...] + normal * gain[...]
    dnorm = cotangent[...] * gain[...]
    grad = scale * (dnorm - normal * jnp.mean(dnorm * normal, axis=-1, keepdims=True))
    mine[0] = stacked(grad).astype(jnp.bfloat16)
    mine[1] = stacked(out).astype(jnp.bfloat16)
    for to in to_kin:
        send(mine.at[0], group_in.at[0, g], group_sems.at[0, g], to)

    def later():
        for to in to_kin:
            send(mine.at[1], group_in.at[1, g], group_sems.at[1, g], to)

    group_in[0, g] = mine[0]
    group_in[1, g] = mine[1]
    for a, b in kin:
        gg = a * 2 + b
        send.arrived(group_in.at[0, gg], group_sems.at[0, gg], sib)
    for gg in range(0, 8, 2):
        first = unstacked(group_in[0, gg].astype(jnp.float32))
        second = unstacked(group_in[0, gg + 1].astype(jnp.float32))
        own[pl.ds(gg * 8, 16), :] = jnp.concatenate([first, second], axis=0).astype(jnp.bfloat16)
    spread(own, full, send, piece_sems, pair_sems, local_sem, later=later)
    for a, b in kin:
        gg = a * 2 + b
        send.arrived(group_in.at[1, gg], group_sems.at[1, gg], sib)
    for gg in range(0, 8, 2):
        first = unstacked(group_in[1, gg].astype(jnp.float32))
        second = unstacked(group_in[1, gg + 1].astype(jnp.float32))
        output[pl.ds(gg * 8, 16), :] = jnp.concatenate([first, second], axis=0).astype(jnp.bfloat16)
    send.finish()


def middle(heads, weight, tokens, cotangent, gain):
    vmem = pl.BlockSpec(memory_space=pltpu.VMEM)
    return pl.pallas_call(
        middle_kernel,
        out_shape=(
            jax.ShapeDtypeStruct((ROWS, WIDTH), jnp.bfloat16),
            jax.ShapeDtypeStruct((16, ROWS, WIDTH), jnp.bfloat16),
        ),
        in_specs=[vmem] * 5,
        out_specs=(vmem, pl.BlockSpec(memory_space=pl.ANY)),
        scratch_shapes=[
            pltpu.VMEM((2, 8, 16, HALF), jnp.bfloat16),
            pltpu.VMEM((8, 16, HALF), jnp.bfloat16),
            pltpu.VMEM((8, 16, HALF), jnp.bfloat16),
            pltpu.VMEM((8, 16, HALF), jnp.bfloat16),
            pltpu.VMEM((2, 16, HALF), jnp.bfloat16),
            pltpu.VMEM((2, 8, 16, HALF), jnp.bfloat16),
            pltpu.VMEM((ROWS, WIDTH), jnp.bfloat16),
            pltpu.SemaphoreType.DMA((1 + 7 + 14 + SPREAD_SENDS,)),
            pltpu.SemaphoreType.DMA,
            pltpu.SemaphoreType.DMA((8,)),
            pltpu.SemaphoreType.DMA((2, 8)),
            pltpu.SemaphoreType.DMA((2, 6, 8)),
            pltpu.SemaphoreType.DMA((8, 2)),
            pltpu.SemaphoreType.DMA,
        ],
        compiler_params=pltpu.CompilerParams(
            collective_id=1, has_side_effects=True, vmem_limit_bytes=60 * 2**20
        ),
        name="middle",
    )(heads, weight, tokens, cotangent, gain)


def tables(length, width):
    half = width // 2
    positions = np.arange(length, dtype=np.float32)[:, None]
    freqs = np.power(np.float32(10000.0), -(np.float32(2.0) * np.arange(half, dtype=np.float32) / np.float32(width)))
    angle = positions * freqs[None, :].astype(np.float32)
    cosine, sine = np.cos(angle), np.sin(angle)
    return (
        jnp.asarray(np.concatenate([cosine, cosine], axis=1)),
        jnp.asarray(np.concatenate([-sine, sine], axis=1)),
    )


BLOCK = 256
STEPS = 4


def turn(values, cosine, sine):
    return values * cosine + pltpu.roll(values, 64, 1) * sine


def scored(keys, queries, first_key, start_row, query_row):
    raw = lax.dot_general(keys, queries, (((1,), (1,)), ((), ())), preferred_element_type=jnp.float32)
    soft = jnp.tanh(raw * (query_scale / softcap))
    row = lax.broadcasted_iota(jnp.int32, raw.shape, 0) + first_key
    allowed = (row >= start_row) & (row <= query_row)
    return soft, jnp.where(allowed, jnp.exp(softcap * soft), 0.0)


def forward_kernel(
    starts, x, weight, cosine, sine, start_ref, query_ref, key_ref, value_ref, heads_ref, sums_ref, keep, keys, values_t
):
    i = pl.program_id(0)
    proj = jnp.dot(x[...], weight[...], preferred_element_type=jnp.float32)
    queries = [turn(proj[:, h * 128 : h * 128 + 128], cosine[...], sine[...]).astype(jnp.bfloat16) for h in range(2)]
    key = turn(proj[:, 256:384], cosine[...], sine[...]).astype(jnp.bfloat16)
    value = proj[:, 384:512]
    query_ref[:, :128] = queries[0]
    query_ref[:, 128:] = queries[1]
    key_ref[...] = key
    value_ref[...] = value.astype(jnp.bfloat16)
    keys[i] = key
    values_t[i] = value.T.astype(jnp.bfloat16)
    start_row = start_ref[...]
    query_row = lax.broadcasted_iota(jnp.int32, (1, BLOCK), 1) + i * BLOCK
    first = starts[i * BLOCK] // BLOCK

    def score(j, sums):
        out = []
        for h in range(2):
            _, e = scored(keys[j], queries[h], j * BLOCK, start_row, query_row)
            keep[h, j] = e
            out.append(sums[h] + jnp.sum(e, axis=0, keepdims=True))
        return tuple(out)

    zero = jnp.zeros((1, BLOCK), jnp.float32)
    sums = lax.fori_loop(first, i + 1, score, (zero, zero))
    inverse = [1.0 / s for s in sums]
    sums_ref[0:1, :] = inverse[0]
    sums_ref[1:2, :] = inverse[1]

    def mix(j, accs):
        out = []
        for h in range(2):
            p = (keep[h, j] * inverse[h]).astype(jnp.bfloat16)
            out.append(accs[h] + jnp.dot(values_t[j], p, preferred_element_type=jnp.float32))
        return tuple(out)

    zero = jnp.zeros((128, BLOCK), jnp.float32)
    accs = lax.fori_loop(first, i + 1, mix, (zero, zero))
    for h in range(2):
        heads_ref[:, h * 128 : h * 128 + 128] = accs[h].T.astype(jnp.bfloat16)


def forward(gathered, weight, cosine, sine, start):
    rows = lambda n: pl.BlockSpec((BLOCK, n), lambda i, s: (i, 0))
    return pl.pallas_call(
        forward_kernel,
        grid_spec=pltpu.PrefetchScalarGridSpec(
            num_scalar_prefetch=1,
            grid=(STEPS,),
            in_specs=[
                rows(WIDTH),
                pl.BlockSpec((WIDTH, 512), lambda i, s: (0, 0)),
                rows(128),
                rows(128),
                pl.BlockSpec((1, BLOCK), lambda i, s: (0, i)),
            ],
            out_specs=[rows(256), rows(128), rows(128), rows(256), pl.BlockSpec((8, BLOCK), lambda i, s: (0, i))],
            scratch_shapes=[
                pltpu.VMEM((2, STEPS, BLOCK, BLOCK), jnp.float32),
                pltpu.VMEM((STEPS, BLOCK, 128), jnp.bfloat16),
                pltpu.VMEM((STEPS, 128, BLOCK), jnp.bfloat16),
            ],
        ),
        out_shape=[
            jax.ShapeDtypeStruct((1024, 256), jnp.bfloat16),
            jax.ShapeDtypeStruct((1024, 128), jnp.bfloat16),
            jax.ShapeDtypeStruct((1024, 128), jnp.bfloat16),
            jax.ShapeDtypeStruct((1024, 256), jnp.bfloat16),
            jax.ShapeDtypeStruct((8, 1024), jnp.float32),
        ],
        compiler_params=pltpu.CompilerParams(vmem_limit_bytes=60 * 2**20),
        name="forward",
    )(start, gathered, weight, cosine, sine, start[None, :])


CHUNK = 512
CHUNKS = WIDTH // CHUNK


def backward_kernel(
    starts, grads_hbm, x_hbm, weight, heads, query_ref, key_ref, value_ref, inverse_ref, cosine, sine, start_ref,
    qkv_out, out_out, grads, x, slope, dprob, dkey, dvalue, keys_t, grad_proj, turned, heads_t, mixed, sems,
):
    i = pl.program_id(0)

    def load(n, which):
        rows = pl.ds(n * BLOCK, BLOCK)
        src, dst = ((grads_hbm, grads), (x_hbm, x))[which]
        return pltpu.make_async_copy(src.at[rows, :], dst.at[rows, :], sems.at[which, n])

    @pl.when(i == 0)
    def _():
        for which in range(2):
            for n in range(STEPS):
                load(n, which).start()
        dkey[...] = jnp.zeros_like(dkey)
        dvalue[...] = jnp.zeros_like(dvalue)

    head = [slice(h * 128, h * 128 + 128) for h in range(2)]

    @pl.when(i < STEPS)
    def _():
        load(i, 0).wait()
        own = pl.ds(pl.multiple_of(i * BLOCK, BLOCK), BLOCK)
        grad_heads = lax.dot_general(
            grads[own, :], weight[...], (((1,), (1,)), ((), ())), preferred_element_type=jnp.float32
        ).astype(jnp.bfloat16)
        keys_t[i] = key_ref[own, :].astype(jnp.float32).T.astype(jnp.bfloat16)
        start_row = start_ref[...]
        query_row = lax.broadcasted_iota(jnp.int32, (1, BLOCK), 1) + i * BLOCK
        first = starts[i * BLOCK] // BLOCK
        queries = [query_ref[own, head[h]] for h in range(2)]
        grad = [grad_heads[:, head[h]] for h in range(2)]

        def score(j, sums):
            out = []
            at = pl.ds(pl.multiple_of(j * BLOCK, BLOCK), BLOCK)
            for h in range(2):
                soft, e = scored(key_ref[at, :], queries[h], j * BLOCK, start_row, query_row)
                p = e * inverse_ref[h : h + 1, :]
                dp = lax.dot_general(
                    value_ref[at, :], grad[h], (((1,), (1,)), ((), ())), preferred_element_type=jnp.float32
                )
                dvalue[at, :] += jnp.dot(p.astype(jnp.bfloat16), grad[h], preferred_element_type=jnp.float32)
                out.append(sums[h] + jnp.sum(p * dp, axis=0, keepdims=True))
                slope[h, j] = p * ((1.0 - soft * soft) * query_scale)
                dprob[h, j] = dp
            return tuple(out)

        zero = jnp.zeros((1, BLOCK), jnp.float32)
        sums = lax.fori_loop(first, i + 1, score, (zero, zero))

        def mix(j, accs):
            out = []
            at = pl.ds(pl.multiple_of(j * BLOCK, BLOCK), BLOCK)
            for h in range(2):
                ds = (slope[h, j] * (dprob[h, j] - sums[h])).astype(jnp.bfloat16)
                dkey[at, :] += jnp.dot(ds, queries[h], preferred_element_type=jnp.float32)
                out.append(accs[h] + jnp.dot(keys_t[j], ds, preferred_element_type=jnp.float32))
            return tuple(out)

        zero = jnp.zeros((128, BLOCK), jnp.float32)
        accs = lax.fori_loop(first, i + 1, mix, (zero, zero))
        for h in range(2):
            grad_proj[own, head[h]] = turn(accs[h].T, cosine[own, :], -sine[own, :])

    @pl.when(i == STEPS)
    def _():
        grad_proj[:, 256:384] = turn(dkey[...], cosine[...], -sine[...])
        grad_proj[:, 384:512] = dvalue[...]
        turned[...] = grad_proj[...].T.astype(jnp.bfloat16)
        heads_t[...] = heads[...].astype(jnp.float32).T.astype(jnp.bfloat16)
        for n in range(STEPS):
            load(n, 1).wait()

    @pl.when(i >= STEPS)
    def _():
        at = pl.ds(pl.multiple_of((i - STEPS) * CHUNK, CHUNK), CHUNK)
        for j in range(4):
            part = jnp.dot(turned[j * 128 : j * 128 + 128, :], x[:, at], preferred_element_type=jnp.float32)
            mixed[pl.ds(j, CHUNK, stride=4), :] = part.T
        out_out[...] = jnp.dot(heads_t[...], grads[:, at], preferred_element_type=jnp.float32).astype(jnp.bfloat16)
        qkv_out[...] = mixed[...].astype(jnp.bfloat16)


def backward(grads, gathered, weight, heads, query, key, value, inverse, cosine, sine, start):
    whole = lambda *shape: pl.BlockSpec(shape, lambda i, s: (0, 0), pipeline_mode=pl.Buffered(1))
    place_of = lambda i: jnp.minimum(i, STEPS - 1)
    chunk_of = lambda i: jnp.maximum(i - STEPS, 0)
    hbm = pl.BlockSpec(memory_space=pl.ANY)
    return pl.pallas_call(
        backward_kernel,
        grid_spec=pltpu.PrefetchScalarGridSpec(
            num_scalar_prefetch=1,
            grid=(STEPS + CHUNKS,),
            in_specs=[
                hbm,
                hbm,
                whole(256, WIDTH),
                whole(1024, 256),
                whole(1024, 256),
                whole(1024, 128),
                whole(1024, 128),
                pl.BlockSpec((8, BLOCK), lambda i, s: (0, place_of(i))),
                whole(1024, 128),
                whole(1024, 128),
                pl.BlockSpec((1, BLOCK), lambda i, s: (0, place_of(i))),
            ],
            out_specs=[
                pl.BlockSpec((4 * CHUNK, 128), lambda i, s: (chunk_of(i), 0)),
                pl.BlockSpec((256, CHUNK), lambda i, s: (0, chunk_of(i))),
            ],
            scratch_shapes=[
                pltpu.VMEM((1024, WIDTH), jnp.bfloat16),
                pltpu.VMEM((1024, WIDTH), jnp.bfloat16),
                pltpu.VMEM((2, STEPS, BLOCK, BLOCK), jnp.float32),
                pltpu.VMEM((2, STEPS, BLOCK, BLOCK), jnp.float32),
                pltpu.VMEM((1024, 128), jnp.float32),
                pltpu.VMEM((1024, 128), jnp.float32),
                pltpu.VMEM((STEPS, 128, BLOCK), jnp.bfloat16),
                pltpu.VMEM((1024, 512), jnp.float32),
                pltpu.VMEM((512, 1024), jnp.bfloat16),
                pltpu.VMEM((256, 1024), jnp.bfloat16),
                pltpu.VMEM((4 * CHUNK, 128), jnp.float32),
                pltpu.SemaphoreType.DMA((2, STEPS)),
            ],
        ),
        out_shape=[
            jax.ShapeDtypeStruct((4 * WIDTH, 128), jnp.bfloat16),
            jax.ShapeDtypeStruct((256, WIDTH), jnp.bfloat16),
        ],
        compiler_params=pltpu.CompilerParams(vmem_limit_bytes=60 * 2**20),
        name="backward",
    )(start, grads, gathered, weight, heads, query, key, value, inverse, cosine, sine, start[None, :])


def nesterov(mean_delta, moment_part, params_part):
    moment_next = 0.9 * moment_part + mean_delta
    return (moment_next, params_part - 0.7 * (mean_delta + 0.9 * moment_next))


def over_x(values, step):
    pairs = [(x * 2 + zh, (x + step) % 4 * 2 + zh) for x in range(4) for zh in range(2)]
    return lax.ppermute(values, "group", pairs)


def delta_over_x(delta):
    x = lax.axis_index("group") // 2
    quarter = lambda n: lax.dynamic_slice_in_dim(delta, n % 4 * 32, 32, axis=0)
    summed = quarter(x).astype(jnp.float32)
    for step in (1, 2, 3):
        summed = summed + over_x(quarter(x + step), step).astype(jnp.float32)
    return summed.astype(jnp.bfloat16)


def delta_over_group(summed):
    x = lax.axis_index("group") // 2
    other = lax.ppermute(summed, "group", [(g, g ^ 1) for g in range(8)])
    total = (summed.astype(jnp.float32) + other.astype(jnp.float32)).astype(jnp.bfloat16)
    quarters = jnp.stack([total] + [over_x(total, step) for step in (1, 2, 3)])
    ordered = jnp.take(quarters, (x - jnp.arange(4)) % 4, axis=0)
    return ordered.reshape(128, WIDTH).astype(jnp.float32)


def local(
    tokens,
    pre_gain,
    post_gain,
    qkv_weight,
    out_weight,
    doc_ids,
    cotangent,
    outer_delta,
    momentum,
    fragment,
):
    group = lax.axis_index("group")
    gathered, wide = gather_normed(tokens, pre_gain[None, :], qkv_weight.reshape(4 * WIDTH, 128))
    gathered = gathered.reshape(16 * ROWS, WIDTH)
    delta, gathered = lax.optimization_barrier((outer_delta[0], gathered))
    summed = delta_over_x(delta)
    length, width = gathered.shape
    cosine, sine = tables(length, 128)
    start = jnp.sum((doc_ids[None, :] < doc_ids[:, None]).astype(jnp.int32), axis=1)
    query, key, value, head_flat, inverse = forward(
        gathered, wide, cosine, sine, start
    )
    out_flat = out_weight.reshape(256, width)
    share = lax.dynamic_slice_in_dim(head_flat.reshape(8, 2, 8, 8, 256), group, 1, axis=2)
    share = jnp.transpose(share[:, :, 0], (1, 0, 2, 3)).reshape(128, 256)
    own_tokens = lax.dynamic_slice_in_dim(tokens, group * 8, 8, axis=0).astype(jnp.float32)
    own_cotangent = lax.dynamic_slice_in_dim(cotangent, group * 8, 8, axis=0).astype(jnp.float32)
    output, grad_rows = middle(share, out_flat, own_tokens, own_cotangent, post_gain[None, :])
    grad_rows = grad_rows.reshape(length, width)
    summed, grad_rows = lax.optimization_barrier((summed, grad_rows))
    total_delta = delta_over_group(summed)
    grad_qkv, grad_out = backward(
        grad_rows, gathered, out_flat, head_flat, query, key, value, inverse, cosine, sine, start
    )
    grad_qkv, grad_out = grad_qkv.reshape(qkv_weight.shape), grad_out.reshape(out_weight.shape)
    new_momentum, new_fragment = nesterov(total_delta / lax.axis_size("group"), momentum, fragment)
    return (output, grad_qkv, grad_out, new_momentum, new_fragment)


def solution(mesh):
    placed = (
        P("fsdp", None),
        P(),
        P(),
        P(None, "fsdp", None, None),
        P("fsdp", None, None, None),
        P(),
        P("fsdp", None),
        P("group", "fsdp", None),
        P("fsdp", None),
        P("fsdp", None),
    )
    return jax.shard_map(
        local,
        mesh=mesh,
        in_specs=placed,
        out_specs=(
            P("fsdp", None),
            P(None, "fsdp", None, None),
            P("fsdp", None, None, None),
            P("fsdp", None),
            P("fsdp", None),
        ),
        check_vma=False,
    )
```

```python
import functools

import jax
import jax.numpy as jnp
import numpy as np
from jax import lax
from jax.experimental import pallas as pl
from jax.experimental.pallas import tpu as pltpu
from jax.sharding import PartitionSpec as P

softcap = 50.0
query_scale = 1.0 / 12.0
MESH = pl.DeviceIdType.MESH
WIDTH = 4608
HALF = WIDTH // 2
ROWS = 64
FIRST_SPLIT = (10 * 128, 10 * 128, 4 * 128)
SECOND_SPLIT = (14 * 128, 14 * 128, 2 * 128)


def place():
    group, fsdp = lax.axis_index("group"), lax.axis_index("fsdp")
    return group // 2, group % 2, fsdp // 8, (fsdp // 2) % 4, fsdp % 2


def device(x, zh, zl, y, c):
    return (x * 2 + zh, (zl * 4 + y) * 2 + c)


class Sender:
    def __init__(self, sems):
        self.sems, self.copies = sems, []

    def __call__(self, src, dst, recv, to):
        copy = pltpu.make_async_remote_copy(
            src_ref=src,
            dst_ref=dst,
            send_sem=self.sems.at[len(self.copies)],
            recv_sem=recv,
            device_id=to,
            device_id_type=MESH,
        )
        copy.start()
        self.copies.append(copy)

    def arrived(self, ref, recv, to):
        pltpu.make_async_remote_copy(
            src_ref=ref,
            dst_ref=ref,
            send_sem=self.sems.at[0],
            recv_sem=recv,
            device_id=to,
            device_id_type=MESH,
        ).wait_recv()

    def finish(self):
        for copy in self.copies:
            copy.wait_send()


SPREAD_SENDS = 69


def spread(split, own, full, send, piece_sems, pair_sems, local_sem, work=iter(()), later=None):
    N1, N2, NQ = split
    NP = N1 + N2
    x, zh, zl, y, c = place()
    k, kz = zl * 4 + y, (1 - zl) * 4 + y
    near_k, near_kz = ([b * 4 + (y + s) % 4 for s in (1, 3, 2)] for b in (zl, 1 - zl))
    to_sib = device(x, zh, zl, y, 1 - c)
    to_z = device(x, zh, 1 - zl, y, c)
    to_y = [device(x, zh, zl, (y + s) % 4, c) for s in (1, 3)]
    to_x = [device((x + s) % 4, zh, zl, y, c) for s in (1, 3)]
    quarters = [x, (x + 1) % 4, (x + 3) % 4, (x + 2) % 4]
    starts = {"a": 0, "b": N1} | {w: NP + quarters[w] * NQ for w in range(4)}
    sizes = {"a": N1, "b": N2} | {w: NQ for w in range(4)}
    index = {"a": 0, "b": 1} | {w: 2 + quarters[w] for w in range(4)}

    def cols(t, half):
        lo, size = starts[t], sizes[t]
        if half is not None:
            size = size // 2
            lo = lo + half * size
        if not isinstance(lo, int):
            lo = pl.multiple_of(lo, 128)
        return pl.ds(lo, size)

    def push(kk, t, to, half=None):
        at = cols(t, half)
        src = own.at[:, at] if kk is k else full.at[2 * kk + c, :, at]
        send(src, full.at[2 * kk + c, :, at], piece_sems.at[half or 0, index[t], kk], to)

    def here(kk, t, half=None):
        next(work, None)
        send.arrived(full.at[2 * kk + c, :, cols(t, half)], piece_sems.at[half or 0, index[t], kk], to_sib)

    def pair(kk, lo, size, slot):
        ref = full.at[2 * kk + c, :, pl.ds(lo, size)]
        send(ref, ref, pair_sems.at[kk, slot], to_sib)

    def ring(kk, t, links, side):
        push(kk, t, links[1 - side], side)

    def both(kk, t, links):
        for to in links:
            push(kk, t, to)

    keep = pltpu.make_async_copy(own, full.at[2 * k + c], local_sem)
    keep.start()
    push(k, 0, to_z)
    both(k, 0, to_y)
    push(k, "a", to_z)
    both(k, "b", to_y)
    push(k, "b", to_z)
    both(k, "a", to_y)
    send(own, full.at[2 * k + c], pair_sems.at[k, 0], to_sib)

    here(kz, 0)
    both(kz, 0, to_y)
    both(kz, 0, to_x)
    for side in range(2):
        kk = near_k[side]
        here(kk, 0)
        ring(kk, 0, to_y, side)
        both(kk, 0, to_x)
    here(kz, "a")
    both(kz, "a", to_y)
    for side in range(2):
        kk = near_k[side]
        here(kk, "b")
        push(kk, "b", to_z)
        ring(kk, "b", to_y, side)
    for side in range(2):
        kk = near_kz[side]
        here(kk, 0)
        ring(kk, 0, to_y, side)
        both(kk, 0, to_x)
    here(near_k[2], 0, 0)
    here(near_k[2], 0, 1)
    both(near_k[2], 0, to_x)
    for side in range(2):
        kk = near_k[side]
        here(kk, "a")
        ring(kk, "a", to_y, side)
        pair(kk, 0, NP, 0)
    here(near_k[2], "b", 0)
    here(near_k[2], "b", 1)
    push(near_k[2], "b", to_z)
    here(near_kz[2], 0, 0)
    here(near_kz[2], 0, 1)
    both(near_kz[2], 0, to_x)
    for side in range(2):
        here(near_kz[side], "a")
        ring(near_kz[side], "a", to_y, side)
    others = [kz, near_k[0], near_k[1], near_kz[0], near_kz[1], near_k[2], near_kz[2]]
    for kk in others[:5]:
        for side in range(2):
            here(kk, 1 + side)
            ring(kk, 1 + side, to_x, side)
    here(kz, "b")
    pair(kz, 0, NP, 0)
    for kk in others[5:]:
        for side in range(2):
            here(kk, 1 + side)
            ring(kk, 1 + side, to_x, side)
    if later is not None:
        later()
    here(near_k[2], "a", 0)
    here(near_k[2], "a", 1)
    pair(near_k[2], 0, NP, 0)
    for side in range(2):
        here(near_kz[side], "b")
        pair(near_kz[side], 0, NP, 0)
    for kk in others[:5]:
        here(kk, 3, 0)
        here(kk, 3, 1)
        pair(kk, NP, 4 * NQ, 1)
    here(near_kz[2], "a", 0)
    here(near_kz[2], "a", 1)
    here(near_kz[2], "b")
    pair(near_kz[2], 0, NP, 0)
    for kk in others[5:]:
        here(kk, 3, 0)
        here(kk, 3, 1)
        pair(kk, NP, 4 * NQ, 1)
    for _ in work:
        pass
    send.arrived(full.at[2 * k + 1 - c], pair_sems.at[k, 0], to_sib)
    for kk in others:
        send.arrived(full.at[2 * kk + 1 - c, :, pl.ds(0, NP)], pair_sems.at[kk, 0], to_sib)
        send.arrived(full.at[2 * kk + 1 - c, :, pl.ds(NP, 4 * NQ)], pair_sems.at[kk, 1], to_sib)
    keep.wait()


def near():
    x, zh, zl, y, c = place()
    out = [device(x, zh, zl, y, 1 - c), device(x, zh, 1 - zl, y, c)]
    out += [device(x, zh, zl, (y + s) % 4, c) for s in (1, 3)]
    return out + [device((x + s) % 4, zh, zl, y, c) for s in (1, 3)]


def greet(devices):
    barrier = pltpu.get_barrier_semaphore()
    for to in devices:
        pl.semaphore_signal(barrier, inc=1, device_id=to, device_id_type=MESH)


def met(devices):
    pl.semaphore_wait(pltpu.get_barrier_semaphore(), len(devices))


def as_row(gain):
    return jnp.concatenate([gain[n : n + 1, :] for n in range(WIDTH // 128)], axis=1)


PARTS = 8
PART = WIDTH // PARTS


def weight_parts(weight, wide, rough, mixed, flat, in_sems, out_sems):
    def load(n):
        return pltpu.make_async_copy(weight.at[pl.ds(4 * PART * n, 4 * PART), :], rough.at[n % 2], in_sems.at[n])

    def store(n):
        return pltpu.make_async_copy(flat.at[n % 2], wide.at[pl.ds(PART * n, PART), :], out_sems.at[n])

    load(0).start()
    for n in range(PARTS):
        if n + 1 < PARTS:
            load(n + 1).start()
        yield
        load(n).wait()
        mixed[...] = rough[n % 2].astype(jnp.float32)
        if n >= 2:
            store(n - 2).wait()
        for j in range(4):
            flat[n % 2, :, j * 128 : j * 128 + 128] = mixed[pl.ds(j, PART, stride=4), :].astype(jnp.bfloat16)
        store(n).start()
    store(PARTS - 2).wait()
    store(PARTS - 1).wait()


def normed_kernel(
    tokens, gain, weight, full, wide, own, rough, mixed, flat,
    send_sems, piece_sems, pair_sems, local_sem, in_sems, out_sems,
):
    work = weight_parts(weight, wide, rough, mixed, flat, in_sems, out_sems)
    next(work)
    greet(near())
    values = tokens[...].astype(jnp.float32)
    scale = lax.rsqrt(jnp.mean(values * values, axis=-1, keepdims=True) + 1e-06)
    own[...] = (values * scale * as_row(gain)).astype(jnp.bfloat16)
    met(near())
    send = Sender(send_sems)
    spread(FIRST_SPLIT, own, full, send, piece_sems, pair_sems, local_sem, work)
    send.finish()


def gather_normed(tokens, gain, weight):
    vmem = pl.BlockSpec(memory_space=pltpu.VMEM)
    return pl.pallas_call(
        normed_kernel,
        out_shape=(
            jax.ShapeDtypeStruct((16, ROWS, WIDTH), jnp.bfloat16),
            jax.ShapeDtypeStruct((WIDTH, 512), jnp.bfloat16),
        ),
        in_specs=[vmem, vmem, pl.BlockSpec(memory_space=pl.ANY)],
        out_specs=(pl.BlockSpec(memory_space=pl.ANY), pl.BlockSpec(memory_space=pl.ANY)),
        scratch_shapes=[
            pltpu.VMEM((ROWS, WIDTH), jnp.bfloat16),
            pltpu.VMEM((2, 4 * PART, 128), jnp.bfloat16),
            pltpu.VMEM((4 * PART, 128), jnp.float32),
            pltpu.VMEM((2, PART, 512), jnp.bfloat16),
            pltpu.SemaphoreType.DMA((SPREAD_SENDS,)),
            pltpu.SemaphoreType.DMA((2, 6, 8)),
            pltpu.SemaphoreType.DMA((8, 2)),
            pltpu.SemaphoreType.DMA,
            pltpu.SemaphoreType.DMA((PARTS,)),
            pltpu.SemaphoreType.DMA((PARTS,)),
        ],
        compiler_params=pltpu.CompilerParams(
            collective_id=0, has_side_effects=True, vmem_limit_bytes=60 * 2**20
        ),
        name="gather_normed",
    )(tokens, gain, weight)


def stacked(rows):
    return jnp.concatenate([rows[:, :HALF], rows[:, HALF:]], axis=0)


def unstacked(rows):
    return jnp.concatenate([rows[:8], rows[8:]], axis=1)


def middle_kernel(
    heads, weight_hbm, tokens, cotangent, gain, delta, output, full, delta_sum,
    weight, partial, received, mate, total, mine, group_in, out_in, own, own_part, parts_in, summed, other, delta_total,
    send_sems, mate_sems, part_sems, group_sems, out_sems, piece_sems, pair_sems, local_sems, delta_sems, sum_sems,
):
    x, zh, zl, y, c = place()
    k, g = zl * 4 + y, x * 2 + zh
    sib = device(x, zh, zl, y, 1 - c)
    chips = [(a, b) for a in range(2) for b in range(4)][1:]
    fellows = [((zl + a) % 2, (y + b) % 4) for a, b in chips]
    to_fellows = [device(x, zh, a, b, c) for a, b in fellows]
    kin = [((x + b) % 4, (zh + a) % 2) for a, b in chips]
    to_kin = [device(a, b, zl, y, c) for a, b in kin]
    to_x = [device((x + step) % 4, zh, zl, y, c) for step in (1, 2, 3)]
    to_zh = device(x, 1 - zh, zl, y, c)
    greet([sib] + to_fellows + to_kin)
    load = pltpu.make_async_copy(weight_hbm, weight, local_sems.at[1])
    load.start()
    load_part = pltpu.make_async_copy(delta.at[pl.ds(pl.multiple_of(x * 32, 32), 32), :], own_part, local_sems.at[2])
    load_part.start()
    share = heads[:, pl.ds(pl.multiple_of(g * 8, 8), 8), :]
    load.wait()
    for core in range(2):
        rows = jnp.concatenate([share[2 * kk + core] for kk in range(8)], axis=0).astype(jnp.bfloat16)
        left = jnp.dot(rows, weight[:, :HALF], preferred_element_type=jnp.float32)
        right = jnp.dot(rows, weight[:, HALF:], preferred_element_type=jnp.float32)
        for kk in range(8):
            both = jnp.concatenate([left[kk * 8 : kk * 8 + 8], right[kk * 8 : kk * 8 + 8]], axis=0)
            partial[core, kk] = both.astype(jnp.bfloat16)
    met([sib] + to_fellows + to_kin)
    send = Sender(send_sems)
    for n, (a, b) in enumerate(fellows):
        kk = a * 4 + b
        send(partial.at[1 - c, kk], mate.at[kk], mate_sems.at[kk], sib)
    send(partial.at[1 - c, k], mate.at[k], mate_sems.at[k], sib)
    for n, step in enumerate((1, 2, 3)):
        rows = pl.ds(pl.multiple_of((x + step) % 4 * 32, 32), 32)
        send(delta.at[rows, :], parts_in.at[n], delta_sems.at[n], to_x[n])
    for (a, b), to in zip(fellows, to_fellows):
        kk = a * 4 + b
        send.arrived(mate.at[kk], mate_sems.at[kk], sib)
        total[kk] = (partial[c, kk].astype(jnp.float32) + mate[kk].astype(jnp.float32)).astype(jnp.bfloat16)
        send(total.at[kk], received.at[k], part_sems.at[k], to)
    send.arrived(mate.at[k], mate_sems.at[k], sib)
    both = partial[c, k].astype(jnp.float32) + mate[k].astype(jnp.float32)
    gain_row = as_row(gain)
    pick = lambda rows: jnp.where(g % 2 == 0, rows[:8], rows[8:])
    near_rows = pl.ds(pl.multiple_of(g // 2 * 16, 16), 16)
    own_tokens = pick(tokens[near_rows, :].astype(jnp.float32))
    dnorm = pick(cotangent[near_rows, :].astype(jnp.float32)) * gain_row
    for a, b in fellows:
        kk = a * 4 + b
        send.arrived(received.at[kk], part_sems.at[kk], sib)
        both = both + received[kk].astype(jnp.float32)
    attn = unstacked(both)
    scale = lax.rsqrt(jnp.mean(attn * attn, axis=-1, keepdims=True) + 1e-06)
    normal = attn * scale
    grad = scale * (dnorm - normal * jnp.mean(dnorm * normal, axis=-1, keepdims=True))
    mine[...] = stacked(grad).astype(jnp.bfloat16)
    for to in to_kin:
        send(mine, group_in.at[g], group_sems.at[g], to)
    group_in[g] = mine[...]
    out_in[zh, x] = stacked(own_tokens + normal * gain_row).astype(jnp.bfloat16)
    load_part.wait()
    for n, step in enumerate((1, 2, 3)):
        send.arrived(parts_in.at[n], delta_sems.at[n], sib)
    summed[...] = (
        own_part[...].astype(jnp.float32)
        + parts_in[0].astype(jnp.float32)
        + parts_in[1].astype(jnp.float32)
        + parts_in[2].astype(jnp.float32)
    ).astype(jnp.bfloat16)
    for a, b in kin:
        gg = a * 2 + b
        send.arrived(group_in.at[gg], group_sems.at[gg], sib)
    for gg in range(0, 8, 2):
        first = unstacked(group_in[gg].astype(jnp.float32))
        second = unstacked(group_in[gg + 1].astype(jnp.float32))
        own[pl.ds(gg * 8, 16), :] = jnp.concatenate([first, second], axis=0).astype(jnp.bfloat16)

    def later():
        yield
        send(summed, other, sum_sems.at[0, 0], to_zh)
        for n, to in enumerate(to_x):
            send(out_in.at[zh, x], out_in.at[zh, x], out_sems.at[x], to)
        for _ in range(12):
            yield
        send.arrived(other, sum_sems.at[0, 0], sib)
        delta_total[...] = (summed[...].astype(jnp.float32) + other[...].astype(jnp.float32)).astype(jnp.bfloat16)
        for to in (to_x[0], to_x[2]):
            send(delta_total, delta_sum.at[x], sum_sems.at[1, x], to)
        for step in (1, 2, 3):
            there = out_in.at[zh, (x + step) % 4]
            send.arrived(there, out_sems.at[(x + step) % 4], sib)
        send(out_in.at[zh], out_in.at[zh], out_sems.at[4], to_zh)
        for _ in range(8):
            yield
        for side, step in enumerate((1, 3)):
            n = (x + step) % 4
            send.arrived(delta_sum.at[n], sum_sems.at[1, n], sib)
            half = delta_sum.at[n, pl.ds(side * 16, 16), :]
            send(half, half, sum_sems.at[2 + side, n], to_x[2 - 2 * side])

    spread(SECOND_SPLIT, own, full, send, piece_sems, pair_sems, local_sems.at[0], later())
    keep = pltpu.make_async_copy(delta_total, delta_sum.at[x], local_sems.at[1])
    keep.start()
    send.arrived(out_in.at[1 - zh], out_sems.at[4], sib)
    for gg in range(0, 8, 2):
        first = unstacked(out_in[0, gg // 2].astype(jnp.float32))
        second = unstacked(out_in[1, gg // 2].astype(jnp.float32))
        output[pl.ds(gg * 8, 16), :] = jnp.concatenate([first, second], axis=0).astype(jnp.bfloat16)
    n = (x + 2) % 4
    for side in range(2):
        send.arrived(delta_sum.at[n, pl.ds(side * 16, 16), :], sum_sems.at[2 + side, n], sib)
    keep.wait()
    send.finish()


def middle(heads, weight, tokens, cotangent, gain, delta):
    vmem = pl.BlockSpec(memory_space=pltpu.VMEM)
    hbm = pl.BlockSpec(memory_space=pl.ANY)
    return pl.pallas_call(
        middle_kernel,
        out_shape=(
            jax.ShapeDtypeStruct((ROWS, WIDTH), jnp.bfloat16),
            jax.ShapeDtypeStruct((16, ROWS, WIDTH), jnp.bfloat16),
            jax.ShapeDtypeStruct((4, 32, WIDTH), jnp.bfloat16),
        ),
        in_specs=[vmem, hbm, vmem, vmem, vmem, hbm],
        out_specs=(vmem, hbm, hbm),
        scratch_shapes=[
            pltpu.VMEM((256, WIDTH), jnp.bfloat16),
            pltpu.VMEM((2, 8, 16, HALF), jnp.bfloat16),
            pltpu.VMEM((8, 16, HALF), jnp.bfloat16),
            pltpu.VMEM((8, 16, HALF), jnp.bfloat16),
            pltpu.VMEM((8, 16, HALF), jnp.bfloat16),
            pltpu.VMEM((16, HALF), jnp.bfloat16),
            pltpu.VMEM((8, 16, HALF), jnp.bfloat16),
            pltpu.VMEM((2, 4, 16, HALF), jnp.bfloat16),
            pltpu.VMEM((ROWS, WIDTH), jnp.bfloat16),
            pltpu.VMEM((32, WIDTH), jnp.bfloat16),
            pltpu.VMEM((3, 32, WIDTH), jnp.bfloat16),
            pltpu.VMEM((32, WIDTH), jnp.bfloat16),
            pltpu.VMEM((32, WIDTH), jnp.bfloat16),
            pltpu.VMEM((32, WIDTH), jnp.bfloat16),
            pltpu.SemaphoreType.DMA((8 + 3 + 7 + 7 + 9 + SPREAD_SENDS,)),
            pltpu.SemaphoreType.DMA((8,)),
            pltpu.SemaphoreType.DMA((8,)),
            pltpu.SemaphoreType.DMA((8,)),
            pltpu.SemaphoreType.DMA((5,)),
            pltpu.SemaphoreType.DMA((2, 6, 8)),
            pltpu.SemaphoreType.DMA((8, 2)),
            pltpu.SemaphoreType.DMA((3,)),
            pltpu.SemaphoreType.DMA((3,)),
            pltpu.SemaphoreType.DMA((4, 4)),
        ],
        compiler_params=pltpu.CompilerParams(
            collective_id=1, has_side_effects=True, vmem_limit_bytes=60 * 2**20
        ),
        name="middle",
    )(heads, weight, tokens, cotangent, gain, delta)


def tables(length, width):
    half = width // 2
    positions = np.arange(length, dtype=np.float32)[:, None]
    freqs = np.power(np.float32(10000.0), -(np.float32(2.0) * np.arange(half, dtype=np.float32) / np.float32(width)))
    angle = positions * freqs[None, :].astype(np.float32)
    cosine, sine = np.cos(angle), np.sin(angle)
    return (
        jnp.asarray(np.concatenate([cosine, cosine], axis=1)),
        jnp.asarray(np.concatenate([-sine, sine], axis=1)),
    )


BLOCK = 256
STEPS = 4


def turn(values, cosine, sine):
    return values * cosine + pltpu.roll(values, 64, 1) * sine


def document_starts(doc_ids, starts):
    ids = doc_ids[...]
    first = jnp.zeros_like(ids)
    for n in range(3):
        first += jnp.where(ids > n, jnp.sum((ids == n).astype(jnp.int32)), 0)
    starts[...] = first


def start_of(starts, i):
    row = jnp.concatenate([starts[pl.ds(2 * i, 1), :], starts[pl.ds(2 * i + 1, 1), :]], axis=1)
    return row, jnp.min(row) // BLOCK


def scored(keys, queries, first_key, start_row, query_row):
    raw = lax.dot_general(keys, queries, (((1,), (1,)), ((), ())), preferred_element_type=jnp.float32)
    soft = jnp.tanh(raw * (query_scale / softcap))
    row = lax.broadcasted_iota(jnp.int32, raw.shape, 0) + first_key
    allowed = (row >= start_row) & (row <= query_row)
    return soft, jnp.where(allowed, jnp.exp(softcap * soft), 0.0)


def forward_kernel(
    x, weight, cosine, sine, doc_ids, query_ref, key_ref, value_ref, heads_ref, sums_ref, keep, keys, values_t, starts
):
    i = pl.program_id(0)

    @pl.when(i == 0)
    def _():
        document_starts(doc_ids, starts)

    proj = jnp.dot(x[...], weight[...], preferred_element_type=jnp.float32)
    queries = [turn(proj[:, h * 128 : h * 128 + 128], cosine[...], sine[...]).astype(jnp.bfloat16) for h in range(2)]
    key = turn(proj[:, 256:384], cosine[...], sine[...]).astype(jnp.bfloat16)
    value = proj[:, 384:512]
    query_ref[:, :128] = queries[0]
    query_ref[:, 128:] = queries[1]
    key_ref[...] = key
    value_ref[...] = value.astype(jnp.bfloat16)
    keys[i] = key
    values_t[i] = value.T.astype(jnp.bfloat16)
    start_row, first = start_of(starts, i)
    query_row = lax.broadcasted_iota(jnp.int32, (1, BLOCK), 1) + i * BLOCK

    def score(j, sums):
        out = []
        for h in range(2):
            _, e = scored(keys[j], queries[h], j * BLOCK, start_row, query_row)
            keep[h, j] = e
            out.append(sums[h] + jnp.sum(e, axis=0, keepdims=True))
        return tuple(out)

    zero = jnp.zeros((1, BLOCK), jnp.float32)
    sums = lax.fori_loop(first, i + 1, score, (zero, zero))
    inverse = [1.0 / s for s in sums]
    sums_ref[0:1, :] = inverse[0]
    sums_ref[1:2, :] = inverse[1]

    def mix(j, accs):
        out = []
        for h in range(2):
            p = (keep[h, j] * inverse[h]).astype(jnp.bfloat16)
            out.append(accs[h] + jnp.dot(values_t[j], p, preferred_element_type=jnp.float32))
        return tuple(out)

    zero = jnp.zeros((128, BLOCK), jnp.float32)
    accs = lax.fori_loop(first, i + 1, mix, (zero, zero))
    for h in range(2):
        heads_ref[:, h * 128 : h * 128 + 128] = accs[h].T


def forward(gathered, weight, cosine, sine, doc_ids):
    rows = lambda n: pl.BlockSpec((BLOCK, n), lambda i: (i, 0))
    return pl.pallas_call(
        forward_kernel,
        grid=(STEPS,),
        in_specs=[
            rows(WIDTH),
            pl.BlockSpec((WIDTH, 512), lambda i: (0, 0), pipeline_mode=pl.Buffered(1)),
            rows(128),
            rows(128),
            pl.BlockSpec((8, 128), lambda i: (0, 0)),
        ],
        out_specs=[rows(256), rows(128), rows(128), rows(256), pl.BlockSpec((8, BLOCK), lambda i: (0, i))],
        scratch_shapes=[
            pltpu.VMEM((2, STEPS, BLOCK, BLOCK), jnp.float32),
            pltpu.VMEM((STEPS, BLOCK, 128), jnp.bfloat16),
            pltpu.VMEM((STEPS, 128, BLOCK), jnp.bfloat16),
            pltpu.VMEM((8, 128), jnp.int32),
        ],
        out_shape=[
            jax.ShapeDtypeStruct((1024, 256), jnp.bfloat16),
            jax.ShapeDtypeStruct((1024, 128), jnp.bfloat16),
            jax.ShapeDtypeStruct((1024, 128), jnp.bfloat16),
            jax.ShapeDtypeStruct((1024, 256), jnp.float32),
            jax.ShapeDtypeStruct((8, 1024), jnp.float32),
        ],
        compiler_params=pltpu.CompilerParams(vmem_limit_bytes=60 * 2**20),
        name="forward",
    )(gathered, weight, cosine, sine, doc_ids)


CHUNK = 512
CHUNKS = WIDTH // CHUNK


def backward_kernel(
    grads_hbm, x_hbm, weight, heads, query_ref, key_ref, value_ref, inverse_ref, cosine, sine, doc_ids,
    delta, momentum, fragment, output, qkv_out, out_out, new_momentum, new_fragment, new_output, grads, x, slope, dprob, dkey, dvalue, keys_t, grad_proj, turned, heads_t, mixed, starts, sems,
):
    i = pl.program_id(0)

    def load(n, which):
        rows = pl.ds(n * BLOCK, BLOCK)
        src, dst = ((grads_hbm, grads), (x_hbm, x))[which]
        return pltpu.make_async_copy(src.at[rows, :], dst.at[rows, :], sems.at[which, n])

    @pl.when(i == 0)
    def _():
        for which in range(2):
            for n in range(STEPS):
                load(n, which).start()
        document_starts(doc_ids, starts)
        dkey[...] = jnp.zeros_like(dkey)
        dvalue[...] = jnp.zeros_like(dvalue)

    head = [slice(h * 128, h * 128 + 128) for h in range(2)]

    @pl.when(i < STEPS)
    def _():
        load(i, 0).wait()
        own = pl.ds(pl.multiple_of(i * BLOCK, BLOCK), BLOCK)
        grad_heads = lax.dot_general(
            grads[own, :], weight[...], (((1,), (1,)), ((), ())), preferred_element_type=jnp.float32
        ).astype(jnp.bfloat16)
        keys_t[i] = key_ref[own, :].astype(jnp.float32).T.astype(jnp.bfloat16)
        start_row, first = start_of(starts, i)
        query_row = lax.broadcasted_iota(jnp.int32, (1, BLOCK), 1) + i * BLOCK
        queries = [query_ref[own, head[h]] for h in range(2)]
        grad = [grad_heads[:, head[h]] for h in range(2)]

        def score(j, sums):
            out = []
            at = pl.ds(pl.multiple_of(j * BLOCK, BLOCK), BLOCK)
            for h in range(2):
                soft, e = scored(key_ref[at, :], queries[h], j * BLOCK, start_row, query_row)
                p = e * inverse_ref[h : h + 1, :]
                dp = lax.dot_general(
                    value_ref[at, :], grad[h], (((1,), (1,)), ((), ())), preferred_element_type=jnp.float32
                )
                dvalue[at, :] += jnp.dot(p.astype(jnp.bfloat16), grad[h], preferred_element_type=jnp.float32)
                out.append(sums[h] + jnp.sum(p * dp, axis=0, keepdims=True))
                slope[h, j] = p * ((1.0 - soft * soft) * query_scale)
                dprob[h, j] = dp
            return tuple(out)

        zero = jnp.zeros((1, BLOCK), jnp.float32)
        sums = lax.fori_loop(first, i + 1, score, (zero, zero))

        def mix(j, accs):
            out = []
            at = pl.ds(pl.multiple_of(j * BLOCK, BLOCK), BLOCK)
            for h in range(2):
                ds = (slope[h, j] * (dprob[h, j] - sums[h])).astype(jnp.bfloat16)
                dkey[at, :] += jnp.dot(ds, queries[h], preferred_element_type=jnp.float32)
                out.append(accs[h] + jnp.dot(keys_t[j], ds, preferred_element_type=jnp.float32))
            return tuple(out)

        zero = jnp.zeros((128, BLOCK), jnp.float32)
        accs = lax.fori_loop(first, i + 1, mix, (zero, zero))
        for h in range(2):
            grad_proj[own, head[h]] = turn(accs[h].T, cosine[own, :], -sine[own, :])

    @pl.when(i == STEPS)
    def _():
        grad_proj[:, 256:384] = turn(dkey[...], cosine[...], -sine[...])
        grad_proj[:, 384:512] = dvalue[...]
        turned[...] = grad_proj[...].T.astype(jnp.bfloat16)
        heads_t[...] = heads[...].T.astype(jnp.bfloat16)
        for n in range(STEPS):
            load(n, 1).wait()

    @pl.when(i >= STEPS)
    def _():
        at = pl.ds(pl.multiple_of((i - STEPS) * CHUNK, CHUNK), CHUNK)
        for j in range(4):
            part = jnp.dot(turned[j * 128 : j * 128 + 128, :], x[:, at], preferred_element_type=jnp.float32)
            mixed[pl.ds(j, CHUNK, stride=4), :] = part.T
        out_out[...] = jnp.dot(heads_t[...], grads[:, at], preferred_element_type=jnp.float32).astype(jnp.bfloat16)
        qkv_out[...] = mixed[...].astype(jnp.bfloat16)
        mean_delta = delta[...].astype(jnp.float32) / 8.0
        moment = 0.9 * momentum[...] + mean_delta
        new_momentum[...] = moment
        new_fragment[...] = fragment[...] - 0.7 * (mean_delta + 0.9 * moment)
        new_output[...] = output[...]


def backward(grads, gathered, weight, heads, query, key, value, inverse, cosine, sine, doc_ids, delta, momentum, fragment, output):
    whole = lambda *shape: pl.BlockSpec(shape, lambda i: (0, 0), pipeline_mode=pl.Buffered(1))
    chunk_of = lambda i: jnp.maximum(i - STEPS, 0)
    columns = lambda n: pl.BlockSpec((n, CHUNK), lambda i: (0, chunk_of(i)))
    hbm = pl.BlockSpec(memory_space=pl.ANY)
    return pl.pallas_call(
        backward_kernel,
        grid=(STEPS + CHUNKS,),
        in_specs=[
            hbm,
            hbm,
            whole(256, WIDTH),
            whole(1024, 256),
            whole(1024, 256),
            whole(1024, 128),
            whole(1024, 128),
            pl.BlockSpec((8, BLOCK), lambda i: (0, jnp.minimum(i, STEPS - 1))),
            whole(1024, 128),
            whole(1024, 128),
            whole(8, 128),
            columns(128),
            columns(128),
            columns(128),
            columns(ROWS),
        ],
        out_specs=[
            pl.BlockSpec((4 * CHUNK, 128), lambda i: (chunk_of(i), 0)),
            columns(256),
            columns(128),
            columns(128),
            columns(ROWS),
        ],
        scratch_shapes=[
            pltpu.VMEM((1024, WIDTH), jnp.bfloat16),
            pltpu.VMEM((1024, WIDTH), jnp.bfloat16),
            pltpu.VMEM((2, STEPS, BLOCK, BLOCK), jnp.float32),
            pltpu.VMEM((2, STEPS, BLOCK, BLOCK), jnp.float32),
            pltpu.VMEM((1024, 128), jnp.float32),
            pltpu.VMEM((1024, 128), jnp.float32),
            pltpu.VMEM((STEPS, 128, BLOCK), jnp.bfloat16),
            pltpu.VMEM((1024, 512), jnp.float32),
            pltpu.VMEM((512, 1024), jnp.bfloat16),
            pltpu.VMEM((256, 1024), jnp.bfloat16),
            pltpu.VMEM((4 * CHUNK, 128), jnp.float32),
            pltpu.VMEM((8, 128), jnp.int32),
            pltpu.SemaphoreType.DMA((2, STEPS)),
        ],
        out_shape=[
            jax.ShapeDtypeStruct((4 * WIDTH, 128), jnp.bfloat16),
            jax.ShapeDtypeStruct((256, WIDTH), jnp.bfloat16),
            jax.ShapeDtypeStruct((128, WIDTH), jnp.float32),
            jax.ShapeDtypeStruct((128, WIDTH), jnp.float32),
            jax.ShapeDtypeStruct((ROWS, WIDTH), jnp.bfloat16),
        ],
        compiler_params=pltpu.CompilerParams(vmem_limit_bytes=60 * 2**20),
        name="backward",
    )(
        grads, gathered, weight, heads, query, key, value, inverse, cosine, sine, doc_ids, delta, momentum, fragment, output
    )


def local(
    tokens,
    pre_gain,
    post_gain,
    qkv_weight,
    out_weight,
    doc_ids,
    cotangent,
    outer_delta,
    momentum,
    fragment,
):
    cosine, sine = tables(16 * ROWS, 128)
    doc_ids = doc_ids.reshape(8, 128)
    gathered, wide = gather_normed(tokens, pre_gain.reshape(36, 128), qkv_weight.reshape(4 * WIDTH, 128))
    gathered = gathered.reshape(16 * ROWS, WIDTH)
    query, key, value, heads, inverse = forward(gathered, wide, cosine, sine, doc_ids)
    out_flat = out_weight.reshape(256, WIDTH)
    output, grad_rows, delta = middle(
        heads.reshape(16, ROWS, 256), out_flat, tokens, cotangent, post_gain.reshape(36, 128), outer_delta[0]
    )
    grad_qkv, grad_out, new_momentum, new_fragment, output = backward(
        grad_rows.reshape(16 * ROWS, WIDTH), gathered, out_flat, heads, query, key, value, inverse, cosine, sine,
        doc_ids, delta.reshape(128, WIDTH), momentum, fragment, output,
    )
    return (output, grad_qkv.reshape(qkv_weight.shape), grad_out.reshape(out_weight.shape), new_momentum, new_fragment)


def solution(mesh):
    placed = (
        P("fsdp", None),
        P(),
        P(),
        P(None, "fsdp", None, None),
        P("fsdp", None, None, None),
        P(),
        P("fsdp", None),
        P("group", "fsdp", None),
        P("fsdp", None),
        P("fsdp", None),
    )
    return jax.shard_map(
        local,
        mesh=mesh,
        in_specs=placed,
        out_specs=(
            P("fsdp", None),
            P(None, "fsdp", None, None),
            P("fsdp", None, None, None),
            P("fsdp", None),
            P("fsdp", None),
        ),
        check_vma=False,
    )
```

```python
import functools

import jax
import jax.numpy as jnp
import numpy as np
from jax import lax
from jax.experimental import pallas as pl
from jax.experimental.pallas import tpu as pltpu
from jax.sharding import PartitionSpec as P

softcap = 50.0
query_scale = 1.0 / 12.0
MESH = pl.DeviceIdType.MESH
WIDTH = 4608
HALF = WIDTH // 2
ROWS = 64
N1, N2, NQ = 10 * 128, 10 * 128, 4 * 128
NP = N1 + N2
REGIONS = {"q": (NP, 4 * NQ), "a": (0, N1), "b": (N1, N2)}


def place():
    group, fsdp = lax.axis_index("group"), lax.axis_index("fsdp")
    return group // 2, group % 2, fsdp // 8, (fsdp // 2) % 4, fsdp % 2


def device(x, zh, zl, y, c):
    return (x * 2 + zh, (zl * 4 + y) * 2 + c)


class Sender:
    def __init__(self, sems):
        self.sems, self.copies = sems, []

    def __call__(self, src, dst, recv, to):
        copy = pltpu.make_async_remote_copy(
            src_ref=src,
            dst_ref=dst,
            send_sem=self.sems.at[len(self.copies)],
            recv_sem=recv,
            device_id=to,
            device_id_type=MESH,
        )
        copy.start()
        self.copies.append(copy)

    def arrived(self, ref, recv, to):
        pltpu.make_async_remote_copy(
            src_ref=ref,
            dst_ref=ref,
            send_sem=self.sems.at[0],
            recv_sem=recv,
            device_id=to,
            device_id_type=MESH,
        ).wait_recv()

    def finish(self):
        for copy in self.copies:
            copy.wait_send()


SPREAD_SENDS = 69


def spread(own, full, send, piece_sems, pair_sems, local_sem, work=iter(()), ready=lambda region: None):
    x, zh, zl, y, c = place()
    k, kz = zl * 4 + y, (1 - zl) * 4 + y
    near_k, near_kz = ([b * 4 + (y + s) % 4 for s in (1, 3, 2)] for b in (zl, 1 - zl))
    to_sib = device(x, zh, zl, y, 1 - c)
    to_z = device(x, zh, 1 - zl, y, c)
    to_y = [device(x, zh, zl, (y + s) % 4, c) for s in (1, 3)]
    to_x = [device((x + s) % 4, zh, zl, y, c) for s in (1, 3)]
    quarters = [x, (x + 1) % 4, (x + 3) % 4, (x + 2) % 4]
    starts = {"a": 0, "b": N1} | {w: NP + quarters[w] * NQ for w in range(4)}
    sizes = {"a": N1, "b": N2} | {w: NQ for w in range(4)}
    index = {"a": 0, "b": 1} | {w: 2 + quarters[w] for w in range(4)}

    def cols(t, half):
        lo, size = starts[t], sizes[t]
        if half is not None:
            size = size // 2
            lo = lo + half * size
        if not isinstance(lo, int):
            lo = pl.multiple_of(lo, 128)
        return pl.ds(lo, size)

    def push(kk, t, to, half=None):
        at = cols(t, half)
        src = own.at[:, at] if kk is k else full.at[2 * kk + c, :, at]
        send(src, full.at[2 * kk + c, :, at], piece_sems.at[half or 0, index[t], kk], to)

    def here(kk, t, half=None):
        next(work, None)
        send.arrived(full.at[2 * kk + c, :, cols(t, half)], piece_sems.at[half or 0, index[t], kk], to_sib)

    def pair(kk, lo, size, slot):
        ref = full.at[2 * kk + c, :, pl.ds(lo, size)]
        send(ref, ref, pair_sems.at[kk, slot], to_sib)

    def ring(kk, t, links, side):
        push(kk, t, links[1 - side], side)

    def both(kk, t, links):
        for to in links:
            push(kk, t, to)

    ready("q")
    push(k, 0, to_z)
    both(k, 0, to_y)
    ready("a")
    push(k, "a", to_z)
    ready("b")
    both(k, "b", to_y)
    push(k, "b", to_z)
    both(k, "a", to_y)
    keep = pltpu.make_async_copy(own, full.at[2 * k + c], local_sem)
    keep.start()
    send(own, full.at[2 * k + c], pair_sems.at[k, 0], to_sib)

    here(kz, 0)
    both(kz, 0, to_y)
    both(kz, 0, to_x)
    for side in range(2):
        kk = near_k[side]
        here(kk, 0)
        ring(kk, 0, to_y, side)
        both(kk, 0, to_x)
    here(kz, "a")
    both(kz, "a", to_y)
    for side in range(2):
        kk = near_k[side]
        here(kk, "b")
        push(kk, "b", to_z)
        ring(kk, "b", to_y, side)
    for side in range(2):
        kk = near_kz[side]
        here(kk, 0)
        ring(kk, 0, to_y, side)
        both(kk, 0, to_x)
    here(near_k[2], 0, 0)
    here(near_k[2], 0, 1)
    both(near_k[2], 0, to_x)
    for side in range(2):
        kk = near_k[side]
        here(kk, "a")
        ring(kk, "a", to_y, side)
        pair(kk, 0, NP, 0)
    here(near_k[2], "b", 0)
    here(near_k[2], "b", 1)
    push(near_k[2], "b", to_z)
    here(near_kz[2], 0, 0)
    here(near_kz[2], 0, 1)
    both(near_kz[2], 0, to_x)
    for side in range(2):
        here(near_kz[side], "a")
        ring(near_kz[side], "a", to_y, side)
    others = [kz, near_k[0], near_k[1], near_kz[0], near_kz[1], near_k[2], near_kz[2]]
    for kk in others[:5]:
        for side in range(2):
            here(kk, 1 + side)
            ring(kk, 1 + side, to_x, side)
    here(kz, "b")
    pair(kz, 0, NP, 0)
    for kk in others[5:]:
        for side in range(2):
            here(kk, 1 + side)
            ring(kk, 1 + side, to_x, side)
    here(near_k[2], "a", 0)
    here(near_k[2], "a", 1)
    pair(near_k[2], 0, NP, 0)
    for side in range(2):
        here(near_kz[side], "b")
        pair(near_kz[side], 0, NP, 0)
    for kk in others[:5]:
        here(kk, 3, 0)
        here(kk, 3, 1)
        pair(kk, NP, 4 * NQ, 1)
    here(near_kz[2], "a", 0)
    here(near_kz[2], "a", 1)
    here(near_kz[2], "b")
    pair(near_kz[2], 0, NP, 0)
    for kk in others[5:]:
        here(kk, 3, 0)
        here(kk, 3, 1)
        pair(kk, NP, 4 * NQ, 1)
    for _ in work:
        pass
    send.arrived(full.at[2 * k + 1 - c], pair_sems.at[k, 0], to_sib)
    for kk in others:
        send.arrived(full.at[2 * kk + 1 - c, :, pl.ds(0, NP)], pair_sems.at[kk, 0], to_sib)
        send.arrived(full.at[2 * kk + 1 - c, :, pl.ds(NP, 4 * NQ)], pair_sems.at[kk, 1], to_sib)
    keep.wait()


def near():
    x, zh, zl, y, c = place()
    out = [device(x, zh, zl, y, 1 - c), device(x, zh, 1 - zl, y, c)]
    out += [device(x, zh, zl, (y + s) % 4, c) for s in (1, 3)]
    return out + [device((x + s) % 4, zh, zl, y, c) for s in (1, 3)]


def greet(devices):
    barrier = pltpu.get_barrier_semaphore()
    for to in devices:
        pl.semaphore_signal(barrier, inc=1, device_id=to, device_id_type=MESH)


def met(devices):
    pl.semaphore_wait(pltpu.get_barrier_semaphore(), len(devices))


def as_row(gain):
    return jnp.concatenate([gain[n : n + 1, :] for n in range(WIDTH // 128)], axis=1)


PARTS = 8
PART = WIDTH // PARTS


def weight_parts(weight, wide, rough, mixed, flat, in_sems, out_sems):
    def load(n):
        return pltpu.make_async_copy(weight.at[pl.ds(4 * PART * n, 4 * PART), :], rough.at[n % 2], in_sems.at[n])

    def store(n):
        return pltpu.make_async_copy(flat.at[n % 2], wide.at[pl.ds(PART * n, PART), :], out_sems.at[n])

    load(0).start()
    for n in range(PARTS):
        if n + 1 < PARTS:
            load(n + 1).start()
        yield
        load(n).wait()
        mixed[...] = rough[n % 2].astype(jnp.float32)
        if n >= 2:
            store(n - 2).wait()
        for j in range(4):
            flat[n % 2, :, j * 128 : j * 128 + 128] = mixed[pl.ds(j, PART, stride=4), :].astype(jnp.bfloat16)
        store(n).start()
    store(PARTS - 2).wait()
    store(PARTS - 1).wait()


def normed_kernel(
    tokens, gain, weight, delta, full, wide, delta_part, own, rough, mixed, flat, own_part, parts_in, summed, other,
    send_sems, piece_sems, pair_sems, local_sem, in_sems, out_sems, delta_sems,
):
    x, zh, zl, y, c = place()
    sib = device(x, zh, zl, y, 1 - c)
    to_x = [device((x + step) % 4, zh, zl, y, c) for step in (1, 2, 3)]
    to_zh = device(x, 1 - zh, zl, y, c)
    everyone = near() + [to_x[1], to_zh]
    rows_of = lambda n: pl.ds(pl.multiple_of(n % 4 * 32, 32), 32)
    load = pltpu.make_async_copy(delta.at[rows_of(x), :], own_part, delta_sems.at[4])
    load.start()

    def background():
        for _ in weight_parts(weight, wide, rough, mixed, flat, in_sems, out_sems):
            yield
        load.wait()
        total = own_part[...].astype(jnp.float32)
        for n in range(3):
            send.arrived(parts_in.at[n], delta_sems.at[n], sib)
            total = total + parts_in[n].astype(jnp.float32)
        summed[...] = total.astype(jnp.bfloat16)
        send(summed, other, delta_sems.at[3], to_zh)
        for _ in range(12):
            yield
        send.arrived(other, delta_sems.at[3], sib)
        delta_part[...] = (summed[...].astype(jnp.float32) + other[...].astype(jnp.float32)).astype(jnp.bfloat16)

    work = background()
    next(work)
    greet(everyone)
    values = tokens[...].astype(jnp.float32)
    scale = lax.rsqrt(jnp.mean(values * values, axis=-1, keepdims=True) + 1e-06)
    own[...] = (values * scale * as_row(gain)).astype(jnp.bfloat16)
    met(everyone)
    send = Sender(send_sems)
    for n, step in enumerate((1, 2, 3)):
        send(delta.at[rows_of(x + step), :], parts_in.at[n], delta_sems.at[n], to_x[n])
    spread(own, full, send, piece_sems, pair_sems, local_sem, work)
    send.finish()


def gather_normed(tokens, gain, weight, delta):
    vmem = pl.BlockSpec(memory_space=pltpu.VMEM)
    hbm = pl.BlockSpec(memory_space=pl.ANY)
    return pl.pallas_call(
        normed_kernel,
        out_shape=(
            jax.ShapeDtypeStruct((16, ROWS, WIDTH), jnp.bfloat16),
            jax.ShapeDtypeStruct((WIDTH, 512), jnp.bfloat16),
            jax.ShapeDtypeStruct((32, WIDTH), jnp.bfloat16),
        ),
        in_specs=[vmem, vmem, hbm, hbm],
        out_specs=(hbm, hbm, vmem),
        scratch_shapes=[
            pltpu.VMEM((ROWS, WIDTH), jnp.bfloat16),
            pltpu.VMEM((2, 4 * PART, 128), jnp.bfloat16),
            pltpu.VMEM((4 * PART, 128), jnp.float32),
            pltpu.VMEM((2, PART, 512), jnp.bfloat16),
            pltpu.VMEM((32, WIDTH), jnp.bfloat16),
            pltpu.VMEM((3, 32, WIDTH), jnp.bfloat16),
            pltpu.VMEM((32, WIDTH), jnp.bfloat16),
            pltpu.VMEM((32, WIDTH), jnp.bfloat16),
            pltpu.SemaphoreType.DMA((4 + SPREAD_SENDS,)),
            pltpu.SemaphoreType.DMA((2, 6, 8)),
            pltpu.SemaphoreType.DMA((8, 2)),
            pltpu.SemaphoreType.DMA,
            pltpu.SemaphoreType.DMA((PARTS,)),
            pltpu.SemaphoreType.DMA((PARTS,)),
            pltpu.SemaphoreType.DMA((5,)),
        ],
        compiler_params=pltpu.CompilerParams(
            collective_id=0, has_side_effects=True, vmem_limit_bytes=60 * 2**20
        ),
        name="gather_normed",
    )(tokens, gain, weight, delta)


def stacked(rows):
    half = rows.shape[1] // 2
    return jnp.concatenate([rows[:, :half], rows[:, half:]], axis=0)


def unstacked(rows):
    return jnp.concatenate([rows[:8], rows[8:]], axis=1)


def middle_kernel(
    heads, weight_hbm, tokens, cotangent, gain, delta_part, output, full, delta_sum,
    weight, partial, received, mate, total, group_q, group_a, group_b, out_in, own,
    send_sems, mate_sems, part_sems, group_sems, out_sems, piece_sems, pair_sems, local_sems, sum_sems,
):
    x, zh, zl, y, c = place()
    k, g = zl * 4 + y, x * 2 + zh
    sib = device(x, zh, zl, y, 1 - c)
    chips = [(a, b) for a in range(2) for b in range(4)][1:]
    fellows = [((zl + a) % 2, (y + b) % 4) for a, b in chips]
    to_fellows = [device(x, zh, a, b, c) for a, b in fellows]
    kin = [((x + b) % 4, (zh + a) % 2) for a, b in chips]
    to_kin = [device(a, b, zl, y, c) for a, b in kin]
    to_x = [device((x + step) % 4, zh, zl, y, c) for step in (1, 2, 3)]
    to_zh = device(x, 1 - zh, zl, y, c)
    group_in = {"q": group_q, "a": group_a, "b": group_b}
    greet([sib] + to_fellows + to_kin)
    load = pltpu.make_async_copy(weight_hbm, weight, local_sems.at[1])
    load.start()
    keep = pltpu.make_async_copy(delta_part, delta_sum.at[x], local_sems.at[2])
    keep.start()
    share = heads[:, pl.ds(pl.multiple_of(g * 8, 8), 8), :]
    load.wait()
    for core in range(2):
        rows = jnp.concatenate([share[2 * kk + core] for kk in range(8)], axis=0).astype(jnp.bfloat16)
        left = jnp.dot(rows, weight[:, :HALF], preferred_element_type=jnp.float32)
        right = jnp.dot(rows, weight[:, HALF:], preferred_element_type=jnp.float32)
        for kk in range(8):
            both = jnp.concatenate([left[kk * 8 : kk * 8 + 8], right[kk * 8 : kk * 8 + 8]], axis=0)
            partial[core, kk] = both.astype(jnp.bfloat16)
    met([sib] + to_fellows + to_kin)
    send = Sender(send_sems)
    for n, (a, b) in enumerate(fellows):
        kk = a * 4 + b
        send(partial.at[1 - c, kk], mate.at[kk], mate_sems.at[kk], sib)
    send(partial.at[1 - c, k], mate.at[k], mate_sems.at[k], sib)
    for to in (to_x[0], to_x[2]):
        send(delta_part, delta_sum.at[x], sum_sems.at[0, x], to)
    for (a, b), to in zip(fellows, to_fellows):
        kk = a * 4 + b
        send.arrived(mate.at[kk], mate_sems.at[kk], sib)
        total[kk] = (partial[c, kk].astype(jnp.float32) + mate[kk].astype(jnp.float32)).astype(jnp.bfloat16)
        send(total.at[kk], received.at[k], part_sems.at[k], to)
    send.arrived(mate.at[k], mate_sems.at[k], sib)
    both = partial[c, k].astype(jnp.float32) + mate[k].astype(jnp.float32)
    gain_row = as_row(gain)
    pick = lambda rows: jnp.where(g % 2 == 0, rows[:8], rows[8:])
    near_rows = pl.ds(pl.multiple_of(g // 2 * 16, 16), 16)
    own_tokens = pick(tokens[near_rows, :].astype(jnp.float32))
    dnorm = pick(cotangent[near_rows, :].astype(jnp.float32)) * gain_row
    for a, b in fellows:
        kk = a * 4 + b
        send.arrived(received.at[kk], part_sems.at[kk], sib)
        both = both + received[kk].astype(jnp.float32)
    attn = unstacked(both)
    scale = lax.rsqrt(jnp.mean(attn * attn, axis=-1, keepdims=True) + 1e-06)
    normal = attn * scale
    grad = scale * (dnorm - normal * jnp.mean(dnorm * normal, axis=-1, keepdims=True))
    for t, (region, (lo, size)) in enumerate(REGIONS.items()):
        into = group_in[region]
        into[g] = stacked(grad[:, lo : lo + size]).astype(jnp.bfloat16)
        for to in to_kin:
            send(into.at[g], into.at[g], group_sems.at[t, g], to)
    out_in[zh, x] = stacked(own_tokens + normal * gain_row).astype(jnp.bfloat16)
    for side, step in enumerate((1, 3)):
        n = (x + step) % 4
        send.arrived(delta_sum.at[n], sum_sems.at[0, n], sib)
        half = delta_sum.at[n, pl.ds(side * 16, 16), :]
        send(half, half, sum_sems.at[1 + side, n], to_x[2 - 2 * side])

    def ready(region):
        t, (lo, size) = list(REGIONS).index(region), REGIONS[region]
        into = group_in[region]
        for a, b in kin:
            gg = a * 2 + b
            send.arrived(into.at[gg], group_sems.at[t, gg], sib)
        for gg in range(0, 8, 2):
            first = unstacked(into[gg].astype(jnp.float32))
            second = unstacked(into[gg + 1].astype(jnp.float32))
            own[pl.ds(gg * 8, 16), pl.ds(lo, size)] = jnp.concatenate([first, second], axis=0).astype(jnp.bfloat16)

    def background():
        for _ in range(9):
            yield
        for to in to_x:
            send(out_in.at[zh, x], out_in.at[zh, x], out_sems.at[x], to)
        for _ in range(12):
            yield
        for step in (1, 2, 3):
            there = out_in.at[zh, (x + step) % 4]
            send.arrived(there, out_sems.at[(x + step) % 4], sib)
        send(out_in.at[zh], out_in.at[zh], out_sems.at[4], to_zh)

    spread(own, full, send, piece_sems, pair_sems, local_sems.at[0], background(), ready)
    send.arrived(out_in.at[1 - zh], out_sems.at[4], sib)
    for gg in range(0, 8, 2):
        first = unstacked(out_in[0, gg // 2].astype(jnp.float32))
        second = unstacked(out_in[1, gg // 2].astype(jnp.float32))
        output[pl.ds(gg * 8, 16), :] = jnp.concatenate([first, second], axis=0).astype(jnp.bfloat16)
    n = (x + 2) % 4
    for side in range(2):
        send.arrived(delta_sum.at[n, pl.ds(side * 16, 16), :], sum_sems.at[1 + side, n], sib)
    keep.wait()
    send.finish()


def middle(heads, weight, tokens, cotangent, gain, delta_part):
    vmem = pl.BlockSpec(memory_space=pltpu.VMEM)
    hbm = pl.BlockSpec(memory_space=pl.ANY)
    return pl.pallas_call(
        middle_kernel,
        out_shape=(
            jax.ShapeDtypeStruct((ROWS, WIDTH), jnp.bfloat16),
            jax.ShapeDtypeStruct((16, ROWS, WIDTH), jnp.bfloat16),
            jax.ShapeDtypeStruct((4, 32, WIDTH), jnp.bfloat16),
        ),
        in_specs=[vmem, hbm, vmem, vmem, vmem, hbm],
        out_specs=(vmem, hbm, hbm),
        scratch_shapes=[
            pltpu.VMEM((256, WIDTH), jnp.bfloat16),
            pltpu.VMEM((2, 8, 16, HALF), jnp.bfloat16),
            pltpu.VMEM((8, 16, HALF), jnp.bfloat16),
            pltpu.VMEM((8, 16, HALF), jnp.bfloat16),
            pltpu.VMEM((8, 16, HALF), jnp.bfloat16),
            pltpu.VMEM((8, 16, 2 * NQ), jnp.bfloat16),
            pltpu.VMEM((8, 16, N1 // 2), jnp.bfloat16),
            pltpu.VMEM((8, 16, N2 // 2), jnp.bfloat16),
            pltpu.VMEM((2, 4, 16, HALF), jnp.bfloat16),
            pltpu.VMEM((ROWS, WIDTH), jnp.bfloat16),
            pltpu.SemaphoreType.DMA((8 + 2 + 7 + 21 + 2 + 4 + SPREAD_SENDS,)),
            pltpu.SemaphoreType.DMA((8,)),
            pltpu.SemaphoreType.DMA((8,)),
            pltpu.SemaphoreType.DMA((3, 8)),
            pltpu.SemaphoreType.DMA((5,)),
            pltpu.SemaphoreType.DMA((2, 6, 8)),
            pltpu.SemaphoreType.DMA((8, 2)),
            pltpu.SemaphoreType.DMA((3,)),
            pltpu.SemaphoreType.DMA((3, 4)),
        ],
        compiler_params=pltpu.CompilerParams(
            collective_id=1, has_side_effects=True, vmem_limit_bytes=60 * 2**20
        ),
        name="middle",
    )(heads, weight, tokens, cotangent, gain, delta_part)


def tables(length, width):
    half = width // 2
    positions = np.arange(length, dtype=np.float32)[:, None]
    freqs = np.power(np.float32(10000.0), -(np.float32(2.0) * np.arange(half, dtype=np.float32) / np.float32(width)))
    angle = positions * freqs[None, :].astype(np.float32)
    cosine, sine = np.cos(angle), np.sin(angle)
    return (
        jnp.asarray(np.concatenate([cosine, cosine], axis=1)),
        jnp.asarray(np.concatenate([-sine, sine], axis=1)),
    )


BLOCK = 256
STEPS = 4


def turn(values, cosine, sine):
    return values * cosine + pltpu.roll(values, 64, 1) * sine


def document_starts(doc_ids, starts):
    ids = doc_ids[...]
    first = jnp.zeros_like(ids)
    for n in range(3):
        first += jnp.where(ids > n, jnp.sum((ids == n).astype(jnp.int32)), 0)
    starts[...] = first


def start_of(starts, i):
    row = jnp.concatenate([starts[pl.ds(2 * i, 1), :], starts[pl.ds(2 * i + 1, 1), :]], axis=1)
    return row, jnp.min(row) // BLOCK


def scored(keys, queries, first_key, start_row, query_row):
    raw = lax.dot_general(keys, queries, (((1,), (1,)), ((), ())), preferred_element_type=jnp.float32)
    soft = jnp.tanh(raw * (query_scale / softcap))
    row = lax.broadcasted_iota(jnp.int32, raw.shape, 0) + first_key
    allowed = (row >= start_row) & (row <= query_row)
    return soft, jnp.where(allowed, jnp.exp(softcap * soft), 0.0)


def forward_kernel(
    x, weight, cosine, sine, doc_ids, query_ref, key_ref, value_ref, heads_ref, sums_ref, keep, keys, values_t, starts
):
    i = pl.program_id(0)

    @pl.when(i == 0)
    def _():
        document_starts(doc_ids, starts)

    proj = jnp.dot(x[...], weight[...], preferred_element_type=jnp.float32)
    queries = [turn(proj[:, h * 128 : h * 128 + 128], cosine[...], sine[...]).astype(jnp.bfloat16) for h in range(2)]
    key = turn(proj[:, 256:384], cosine[...], sine[...]).astype(jnp.bfloat16)
    value = proj[:, 384:512]
    query_ref[:, :128] = queries[0]
    query_ref[:, 128:] = queries[1]
    key_ref[...] = key
    value_ref[...] = value.astype(jnp.bfloat16)
    keys[i] = key
    values_t[i] = value.T.astype(jnp.bfloat16)
    start_row, first = start_of(starts, i)
    query_row = lax.broadcasted_iota(jnp.int32, (1, BLOCK), 1) + i * BLOCK

    def score(j, sums):
        out = []
        for h in range(2):
            _, e = scored(keys[j], queries[h], j * BLOCK, start_row, query_row)
            keep[h, j] = e
            out.append(sums[h] + jnp.sum(e, axis=0, keepdims=True))
        return tuple(out)

    zero = jnp.zeros((1, BLOCK), jnp.float32)
    sums = lax.fori_loop(first, i + 1, score, (zero, zero))
    inverse = [1.0 / s for s in sums]
    sums_ref[0:1, :] = inverse[0]
    sums_ref[1:2, :] = inverse[1]

    def mix(j, accs):
        out = []
        for h in range(2):
            p = (keep[h, j] * inverse[h]).astype(jnp.bfloat16)
            out.append(accs[h] + jnp.dot(values_t[j], p, preferred_element_type=jnp.float32))
        return tuple(out)

    zero = jnp.zeros((128, BLOCK), jnp.float32)
    accs = lax.fori_loop(first, i + 1, mix, (zero, zero))
    for h in range(2):
        heads_ref[:, h * 128 : h * 128 + 128] = accs[h].T


def forward(gathered, weight, cosine, sine, doc_ids):
    rows = lambda n: pl.BlockSpec((BLOCK, n), lambda i: (i, 0))
    return pl.pallas_call(
        forward_kernel,
        grid=(STEPS,),
        in_specs=[
            rows(WIDTH),
            pl.BlockSpec((WIDTH, 512), lambda i: (0, 0), pipeline_mode=pl.Buffered(1)),
            rows(128),
            rows(128),
            pl.BlockSpec((8, 128), lambda i: (0, 0)),
        ],
        out_specs=[rows(256), rows(128), rows(128), rows(256), pl.BlockSpec((8, BLOCK), lambda i: (0, i))],
        scratch_shapes=[
            pltpu.VMEM((2, STEPS, BLOCK, BLOCK), jnp.float32),
            pltpu.VMEM((STEPS, BLOCK, 128), jnp.bfloat16),
            pltpu.VMEM((STEPS, 128, BLOCK), jnp.bfloat16),
            pltpu.VMEM((8, 128), jnp.int32),
        ],
        out_shape=[
            jax.ShapeDtypeStruct((1024, 256), jnp.bfloat16),
            jax.ShapeDtypeStruct((1024, 128), jnp.bfloat16),
            jax.ShapeDtypeStruct((1024, 128), jnp.bfloat16),
            jax.ShapeDtypeStruct((1024, 256), jnp.float32),
            jax.ShapeDtypeStruct((8, 1024), jnp.float32),
        ],
        compiler_params=pltpu.CompilerParams(vmem_limit_bytes=60 * 2**20),
        name="forward",
    )(gathered, weight, cosine, sine, doc_ids)


CHUNK = 512
CHUNKS = WIDTH // CHUNK


def backward_kernel(
    grads_hbm, x_hbm, weight, heads, query_ref, key_ref, value_ref, inverse_ref, cosine, sine, doc_ids,
    delta, momentum, fragment, output, qkv_out, out_out, new_momentum, new_fragment, new_output, grads, x, slope, dprob, dkey, dvalue, keys_t, grad_proj, turned, heads_t, mixed, starts, sems,
):
    i = pl.program_id(0)

    def load(n, which):
        rows = pl.ds(n * BLOCK, BLOCK)
        src, dst = ((grads_hbm, grads), (x_hbm, x))[which]
        return pltpu.make_async_copy(src.at[rows, :], dst.at[rows, :], sems.at[which, n])

    @pl.when(i == 0)
    def _():
        for which in range(2):
            for n in range(STEPS):
                load(n, which).start()
        document_starts(doc_ids, starts)
        dkey[...] = jnp.zeros_like(dkey)
        dvalue[...] = jnp.zeros_like(dvalue)

    head = [slice(h * 128, h * 128 + 128) for h in range(2)]

    @pl.when(i < STEPS)
    def _():
        load(i, 0).wait()
        own = pl.ds(pl.multiple_of(i * BLOCK, BLOCK), BLOCK)
        grad_heads = lax.dot_general(
            grads[own, :], weight[...], (((1,), (1,)), ((), ())), preferred_element_type=jnp.float32
        ).astype(jnp.bfloat16)
        keys_t[i] = key_ref[own, :].astype(jnp.float32).T.astype(jnp.bfloat16)
        start_row, first = start_of(starts, i)
        query_row = lax.broadcasted_iota(jnp.int32, (1, BLOCK), 1) + i * BLOCK
        queries = [query_ref[own, head[h]] for h in range(2)]
        grad = [grad_heads[:, head[h]] for h in range(2)]

        def score(j, sums):
            out = []
            at = pl.ds(pl.multiple_of(j * BLOCK, BLOCK), BLOCK)
            for h in range(2):
                soft, e = scored(key_ref[at, :], queries[h], j * BLOCK, start_row, query_row)
                p = e * inverse_ref[h : h + 1, :]
                dp = lax.dot_general(
                    value_ref[at, :], grad[h], (((1,), (1,)), ((), ())), preferred_element_type=jnp.float32
                )
                dvalue[at, :] += jnp.dot(p.astype(jnp.bfloat16), grad[h], preferred_element_type=jnp.float32)
                out.append(sums[h] + jnp.sum(p * dp, axis=0, keepdims=True))
                slope[h, j] = p * ((1.0 - soft * soft) * query_scale)
                dprob[h, j] = dp
            return tuple(out)

        zero = jnp.zeros((1, BLOCK), jnp.float32)
        sums = lax.fori_loop(first, i + 1, score, (zero, zero))

        def mix(j, accs):
            out = []
            at = pl.ds(pl.multiple_of(j * BLOCK, BLOCK), BLOCK)
            for h in range(2):
                ds = (slope[h, j] * (dprob[h, j] - sums[h])).astype(jnp.bfloat16)
                dkey[at, :] += jnp.dot(ds, queries[h], preferred_element_type=jnp.float32)
                out.append(accs[h] + jnp.dot(keys_t[j], ds, preferred_element_type=jnp.float32))
            return tuple(out)

        zero = jnp.zeros((128, BLOCK), jnp.float32)
        accs = lax.fori_loop(first, i + 1, mix, (zero, zero))
        for h in range(2):
            grad_proj[own, head[h]] = turn(accs[h].T, cosine[own, :], -sine[own, :])

    @pl.when(i == STEPS)
    def _():
        grad_proj[:, 256:384] = turn(dkey[...], cosine[...], -sine[...])
        grad_proj[:, 384:512] = dvalue[...]
        turned[...] = grad_proj[...].T.astype(jnp.bfloat16)
        heads_t[...] = heads[...].T.astype(jnp.bfloat16)
        for n in range(STEPS):
            load(n, 1).wait()

    @pl.when(i >= STEPS)
    def _():
        at = pl.ds(pl.multiple_of((i - STEPS) * CHUNK, CHUNK), CHUNK)
        for j in range(4):
            part = jnp.dot(turned[j * 128 : j * 128 + 128, :], x[:, at], preferred_element_type=jnp.float32)
            mixed[pl.ds(j, CHUNK, stride=4), :] = part.T
        out_out[...] = jnp.dot(heads_t[...], grads[:, at], preferred_element_type=jnp.float32).astype(jnp.bfloat16)
        qkv_out[...] = mixed[...].astype(jnp.bfloat16)
        mean_delta = delta[...].astype(jnp.float32) / 8.0
        moment = 0.9 * momentum[...] + mean_delta
        new_momentum[...] = moment
        new_fragment[...] = fragment[...] - 0.7 * (mean_delta + 0.9 * moment)
        new_output[...] = output[...]


def backward(grads, gathered, weight, heads, query, key, value, inverse, cosine, sine, doc_ids, delta, momentum, fragment, output):
    whole = lambda *shape: pl.BlockSpec(shape, lambda i: (0, 0), pipeline_mode=pl.Buffered(1))
    chunk_of = lambda i: jnp.maximum(i - STEPS, 0)
    columns = lambda n: pl.BlockSpec((n, CHUNK), lambda i: (0, chunk_of(i)))
    hbm = pl.BlockSpec(memory_space=pl.ANY)
    return pl.pallas_call(
        backward_kernel,
        grid=(STEPS + CHUNKS,),
        in_specs=[
            hbm,
            hbm,
            whole(256, WIDTH),
            whole(1024, 256),
            whole(1024, 256),
            whole(1024, 128),
            whole(1024, 128),
            pl.BlockSpec((8, BLOCK), lambda i: (0, jnp.minimum(i, STEPS - 1))),
            whole(1024, 128),
            whole(1024, 128),
            whole(8, 128),
            columns(128),
            columns(128),
            columns(128),
            columns(ROWS),
        ],
        out_specs=[
            pl.BlockSpec((4 * CHUNK, 128), lambda i: (chunk_of(i), 0)),
            columns(256),
            columns(128),
            columns(128),
            columns(ROWS),
        ],
        scratch_shapes=[
            pltpu.VMEM((1024, WIDTH), jnp.bfloat16),
            pltpu.VMEM((1024, WIDTH), jnp.bfloat16),
            pltpu.VMEM((2, STEPS, BLOCK, BLOCK), jnp.float32),
            pltpu.VMEM((2, STEPS, BLOCK, BLOCK), jnp.float32),
            pltpu.VMEM((1024, 128), jnp.float32),
            pltpu.VMEM((1024, 128), jnp.float32),
            pltpu.VMEM((STEPS, 128, BLOCK), jnp.bfloat16),
            pltpu.VMEM((1024, 512), jnp.float32),
            pltpu.VMEM((512, 1024), jnp.bfloat16),
            pltpu.VMEM((256, 1024), jnp.bfloat16),
            pltpu.VMEM((4 * CHUNK, 128), jnp.float32),
            pltpu.VMEM((8, 128), jnp.int32),
            pltpu.SemaphoreType.DMA((2, STEPS)),
        ],
        out_shape=[
            jax.ShapeDtypeStruct((4 * WIDTH, 128), jnp.bfloat16),
            jax.ShapeDtypeStruct((256, WIDTH), jnp.bfloat16),
            jax.ShapeDtypeStruct((128, WIDTH), jnp.float32),
            jax.ShapeDtypeStruct((128, WIDTH), jnp.float32),
            jax.ShapeDtypeStruct((ROWS, WIDTH), jnp.bfloat16),
        ],
        compiler_params=pltpu.CompilerParams(vmem_limit_bytes=60 * 2**20),
        name="backward",
    )(
        grads, gathered, weight, heads, query, key, value, inverse, cosine, sine, doc_ids, delta, momentum, fragment, output
    )


def local(
    tokens,
    pre_gain,
    post_gain,
    qkv_weight,
    out_weight,
    doc_ids,
    cotangent,
    outer_delta,
    momentum,
    fragment,
):
    cosine, sine = tables(16 * ROWS, 128)
    doc_ids = doc_ids.reshape(8, 128)
    gathered, wide, delta_part = gather_normed(
        tokens, pre_gain.reshape(36, 128), qkv_weight.reshape(4 * WIDTH, 128), outer_delta[0]
    )
    gathered = gathered.reshape(16 * ROWS, WIDTH)
    query, key, value, heads, inverse = forward(gathered, wide, cosine, sine, doc_ids)
    out_flat = out_weight.reshape(256, WIDTH)
    output, grad_rows, delta = middle(
        heads.reshape(16, ROWS, 256), out_flat, tokens, cotangent, post_gain.reshape(36, 128), delta_part
    )
    grad_qkv, grad_out, new_momentum, new_fragment, output = backward(
        grad_rows.reshape(16 * ROWS, WIDTH), gathered, out_flat, heads, query, key, value, inverse, cosine, sine,
        doc_ids, delta.reshape(128, WIDTH), momentum, fragment, output,
    )
    return (output, grad_qkv.reshape(qkv_weight.shape), grad_out.reshape(out_weight.shape), new_momentum, new_fragment)


def solution(mesh):
    placed = (
        P("fsdp", None),
        P(),
        P(),
        P(None, "fsdp", None, None),
        P("fsdp", None, None, None),
        P(),
        P("fsdp", None),
        P("group", "fsdp", None),
        P("fsdp", None),
        P("fsdp", None),
    )
    return jax.shard_map(
        local,
        mesh=mesh,
        in_specs=placed,
        out_specs=(
            P("fsdp", None),
            P(None, "fsdp", None, None),
            P("fsdp", None, None, None),
            P("fsdp", None),
            P("fsdp", None),
        ),
        check_vma=False,
    )
```

```python
import functools

import jax
import jax.numpy as jnp
import numpy as np
from jax import lax
from jax.experimental import pallas as pl
from jax.experimental.pallas import tpu as pltpu
from jax.sharding import PartitionSpec as P

softcap = 50.0
query_scale = 1.0 / 12.0
MESH = pl.DeviceIdType.MESH
WIDTH = 4608
HALF = WIDTH // 2
ROWS = 64
N1, N2, NQ = 10 * 128, 10 * 128, 4 * 128
NP = N1 + N2
REGIONS = {"q": (NP, 4 * NQ), "a": (0, N1), "b": (N1, N2)}


def place():
    group, fsdp = lax.axis_index("group"), lax.axis_index("fsdp")
    return group // 2, group % 2, fsdp // 8, (fsdp // 2) % 4, fsdp % 2


def device(x, zh, zl, y, c):
    return (x * 2 + zh, (zl * 4 + y) * 2 + c)


class Sender:
    def __init__(self, sems):
        self.sems, self.copies = sems, []

    def __call__(self, src, dst, recv, to):
        copy = pltpu.make_async_remote_copy(
            src_ref=src,
            dst_ref=dst,
            send_sem=self.sems.at[len(self.copies)],
            recv_sem=recv,
            device_id=to,
            device_id_type=MESH,
        )
        copy.start()
        self.copies.append(copy)

    def arrived(self, ref, recv, to):
        pltpu.make_async_remote_copy(
            src_ref=ref,
            dst_ref=ref,
            send_sem=self.sems.at[0],
            recv_sem=recv,
            device_id=to,
            device_id_type=MESH,
        ).wait_recv()

    def finish(self):
        for copy in self.copies:
            copy.wait_send()


SPREAD_SENDS = 69


def spread(own, full, send, piece_sems, pair_sems, local_sem, work=iter(()), ready=lambda region: None):
    x, zh, zl, y, c = place()
    k, kz = zl * 4 + y, (1 - zl) * 4 + y
    near_k, near_kz = ([b * 4 + (y + s) % 4 for s in (1, 3, 2)] for b in (zl, 1 - zl))
    to_sib = device(x, zh, zl, y, 1 - c)
    to_z = device(x, zh, 1 - zl, y, c)
    to_y = [device(x, zh, zl, (y + s) % 4, c) for s in (1, 3)]
    to_x = [device((x + s) % 4, zh, zl, y, c) for s in (1, 3)]
    quarters = [x, (x + 1) % 4, (x + 3) % 4, (x + 2) % 4]
    starts = {"a": 0, "b": N1} | {w: NP + quarters[w] * NQ for w in range(4)}
    sizes = {"a": N1, "b": N2} | {w: NQ for w in range(4)}
    index = {"a": 0, "b": 1} | {w: 2 + quarters[w] for w in range(4)}

    def cols(t, half):
        lo, size = starts[t], sizes[t]
        if half is not None:
            size = size // 2
            lo = lo + half * size
        if not isinstance(lo, int):
            lo = pl.multiple_of(lo, 128)
        return pl.ds(lo, size)

    def push(kk, t, to, half=None):
        at = cols(t, half)
        src = own.at[:, at] if kk is k else full.at[2 * kk + c, :, at]
        send(src, full.at[2 * kk + c, :, at], piece_sems.at[half or 0, index[t], kk], to)

    def here(kk, t, half=None):
        next(work, None)
        send.arrived(full.at[2 * kk + c, :, cols(t, half)], piece_sems.at[half or 0, index[t], kk], to_sib)

    def pair(kk, lo, size, slot):
        ref = full.at[2 * kk + c, :, pl.ds(lo, size)]
        send(ref, ref, pair_sems.at[kk, slot], to_sib)

    def ring(kk, t, links, side):
        push(kk, t, links[1 - side], side)

    def both(kk, t, links):
        for to in links:
            push(kk, t, to)

    ready("q")
    push(k, 0, to_z)
    both(k, 0, to_y)
    ready("a")
    push(k, "a", to_z)
    ready("b")
    both(k, "b", to_y)
    push(k, "b", to_z)
    both(k, "a", to_y)
    keep = pltpu.make_async_copy(own, full.at[2 * k + c], local_sem)
    keep.start()
    send(own, full.at[2 * k + c], pair_sems.at[k, 0], to_sib)

    here(kz, 0)
    both(kz, 0, to_y)
    both(kz, 0, to_x)
    for side in range(2):
        kk = near_k[side]
        here(kk, 0)
        ring(kk, 0, to_y, side)
        both(kk, 0, to_x)
    here(kz, "a")
    both(kz, "a", to_y)
    for side in range(2):
        kk = near_k[side]
        here(kk, "b")
        push(kk, "b", to_z)
        ring(kk, "b", to_y, side)
    for side in range(2):
        kk = near_kz[side]
        here(kk, 0)
        ring(kk, 0, to_y, side)
        both(kk, 0, to_x)
    here(near_k[2], 0, 0)
    here(near_k[2], 0, 1)
    both(near_k[2], 0, to_x)
    for side in range(2):
        kk = near_k[side]
        here(kk, "a")
        ring(kk, "a", to_y, side)
        pair(kk, 0, NP, 0)
    here(near_k[2], "b", 0)
    here(near_k[2], "b", 1)
    push(near_k[2], "b", to_z)
    here(near_kz[2], 0, 0)
    here(near_kz[2], 0, 1)
    both(near_kz[2], 0, to_x)
    for side in range(2):
        here(near_kz[side], "a")
        ring(near_kz[side], "a", to_y, side)
    others = [kz, near_k[0], near_k[1], near_kz[0], near_kz[1], near_k[2], near_kz[2]]
    for kk in others[:5]:
        for side in range(2):
            here(kk, 1 + side)
            ring(kk, 1 + side, to_x, side)
    here(kz, "b")
    pair(kz, 0, NP, 0)
    for kk in others[5:]:
        for side in range(2):
            here(kk, 1 + side)
            ring(kk, 1 + side, to_x, side)
    here(near_k[2], "a", 0)
    here(near_k[2], "a", 1)
    pair(near_k[2], 0, NP, 0)
    for side in range(2):
        here(near_kz[side], "b")
        pair(near_kz[side], 0, NP, 0)
    for kk in others[:5]:
        here(kk, 3, 0)
        here(kk, 3, 1)
        pair(kk, NP, 4 * NQ, 1)
    here(near_kz[2], "a", 0)
    here(near_kz[2], "a", 1)
    here(near_kz[2], "b")
    pair(near_kz[2], 0, NP, 0)
    for kk in others[5:]:
        here(kk, 3, 0)
        here(kk, 3, 1)
        pair(kk, NP, 4 * NQ, 1)
    for _ in work:
        pass
    send.arrived(full.at[2 * k + 1 - c], pair_sems.at[k, 0], to_sib)
    for kk in others:
        send.arrived(full.at[2 * kk + 1 - c, :, pl.ds(0, NP)], pair_sems.at[kk, 0], to_sib)
        send.arrived(full.at[2 * kk + 1 - c, :, pl.ds(NP, 4 * NQ)], pair_sems.at[kk, 1], to_sib)
    keep.wait()


def greet(devices):
    barrier = pltpu.get_barrier_semaphore()
    for to in devices:
        pl.semaphore_signal(barrier, inc=1, device_id=to, device_id_type=MESH)


def met(devices):
    pl.semaphore_wait(pltpu.get_barrier_semaphore(), len(devices))


def stacked(rows):
    half = rows.shape[1] // 2
    return jnp.concatenate([rows[:, :half], rows[:, half:]], axis=0)


def unstacked(rows):
    return jnp.concatenate([rows[:8], rows[8:]], axis=1)


def tables(length, width):
    half = width // 2
    positions = np.arange(length, dtype=np.float32)[:, None]
    freqs = np.power(np.float32(10000.0), -(np.float32(2.0) * np.arange(half, dtype=np.float32) / np.float32(width)))
    angle = positions * freqs[None, :].astype(np.float32)
    cosine, sine = np.cos(angle), np.sin(angle)
    return (
        jnp.asarray(np.concatenate([cosine, cosine], axis=1)),
        jnp.asarray(np.concatenate([-sine, sine], axis=1)),
    )


BLOCK = 256
STEPS = 4


def turn(values, cosine, sine):
    return values * cosine + pltpu.roll(values, 64, 1) * sine


def document_starts(doc_ids, starts):
    ids = doc_ids[...]
    first = jnp.zeros_like(ids)
    for n in range(3):
        first += jnp.where(ids > n, jnp.sum((ids == n).astype(jnp.int32)), 0)
    starts[...] = first


def start_of(starts, i):
    row = jnp.concatenate([starts[pl.ds(2 * i, 1), :], starts[pl.ds(2 * i + 1, 1), :]], axis=1)
    return row, jnp.min(row) // BLOCK


def scored(keys, queries, first_key, start_row, query_row):
    raw = lax.dot_general(keys, queries, (((1,), (1,)), ((), ())), preferred_element_type=jnp.float32)
    soft = jnp.tanh(raw * (query_scale / softcap))
    row = lax.broadcasted_iota(jnp.int32, raw.shape, 0) + first_key
    allowed = (row >= start_row) & (row <= query_row)
    return soft, jnp.where(allowed, jnp.exp(softcap * soft), 0.0)


def as_row(gain):
    return jnp.concatenate([gain[n : n + 1, :] for n in range(WIDTH // 128)], axis=1)


PARTS = 8
PART = WIDTH // PARTS


def weight_parts(weight, wide, rough, mixed, in_sems):
    def load(n):
        return pltpu.make_async_copy(weight.at[pl.ds(4 * PART * n, 4 * PART), :], rough.at[n % 2], in_sems.at[n])

    load(0).start()
    for n in range(PARTS):
        if n + 1 < PARTS:
            load(n + 1).start()
        yield
        load(n).wait()
        mixed[...] = rough[n % 2].astype(jnp.float32)
        for j in range(4):
            wide[pl.ds(PART * n, PART), j * 128 : j * 128 + 128] = mixed[pl.ds(j, PART, stride=4), :].astype(jnp.bfloat16)


def front_kernel(
    tokens, pre_gain, post_gain, qkv_hbm, weight_hbm, doc_ids, cotangent, delta, cosine, sine,
    output, gathered, full, delta_sum, query_ref, key_ref, value_ref, sums_ref, heads_ref,
    everything, own, own_grad, wide, rough, mixed, own_part, parts_in, summed, other, delta_part, starts, scores, values_t,
    weight, partial, received, mate, total, group_q, group_a, group_b, out_in,
    send_sems, piece_sems, pair_sems, local_sems, in_sems, delta_sems,
    mate_sems, part_sems, group_sems, out_sems, sum_sems,
):
    x, zh, zl, y, c = place()
    k, g = zl * 4 + y, x * 2 + zh
    sib = device(x, zh, zl, y, 1 - c)
    chips = [(a, b) for a in range(2) for b in range(4)][1:]
    fellows = [((zl + a) % 2, (y + b) % 4) for a, b in chips]
    to_fellows = [device(x, zh, a, b, c) for a, b in fellows]
    kin = [((x + b) % 4, (zh + a) % 2) for a, b in chips]
    to_kin = [device(a, b, zl, y, c) for a, b in kin]
    to_x = [device((x + step) % 4, zh, zl, y, c) for step in (1, 2, 3)]
    to_zh = device(x, 1 - zh, zl, y, c)
    group_in = {"q": group_q, "a": group_a, "b": group_b}
    greet([sib] + to_fellows + to_kin)
    send = Sender(send_sems)
    rows_of = lambda n: pl.ds(pl.multiple_of(n % 4 * 32, 32), 32)
    load_part = pltpu.make_async_copy(delta.at[rows_of(x), :], own_part, delta_sems.at[4])
    load_part.start()

    def background():
        for _ in weight_parts(qkv_hbm, wide, rough, mixed, in_sems):
            yield
        load_weight.start()
        for _ in range(12):
            yield
        for n, step in enumerate((1, 2, 3)):
            send(delta.at[rows_of(x + step), :], parts_in.at[n], delta_sems.at[n], to_x[n])

    load_weight = pltpu.make_async_copy(weight_hbm, weight, local_sems.at[1])
    work = background()
    next(work)
    values = tokens[...].astype(jnp.float32)
    scale = lax.rsqrt(jnp.mean(values * values, axis=-1, keepdims=True) + 1e-06)
    own[...] = (values * scale * as_row(pre_gain)).astype(jnp.bfloat16)
    document_starts(doc_ids, starts)
    met([sib] + to_fellows + to_kin)
    spread(own, everything, send, piece_sems.at[0], pair_sems.at[0], local_sems.at[0], work)
    store = pltpu.make_async_copy(everything, gathered, local_sems.at[3])
    store.start()

    for i in range(STEPS):
        at = pl.ds(i * BLOCK, BLOCK)
        rows = everything[pl.ds(4 * i, 4)].reshape(BLOCK, WIDTH)
        proj = jnp.dot(rows, wide[...], preferred_element_type=jnp.float32)
        queries = [turn(proj[:, h * 128 : h * 128 + 128], cosine[at, :], sine[at, :]).astype(jnp.bfloat16) for h in range(2)]
        query_ref[at, :128] = queries[0]
        query_ref[at, 128:] = queries[1]
        key_ref[at, :] = turn(proj[:, 256:384], cosine[at, :], sine[at, :]).astype(jnp.bfloat16)
        value_ref[at, :] = proj[:, 384:].astype(jnp.bfloat16)
        values_t[i] = proj[:, 384:].T.astype(jnp.bfloat16)
        start_row, _ = start_of(starts, i)
        query_row = lax.broadcasted_iota(jnp.int32, (1, BLOCK), 1) + i * BLOCK
        blocks = range(max(0, i - 2), i + 1)
        for h in range(2):
            sums = jnp.zeros((1, BLOCK), jnp.float32)
            for n, j in enumerate(blocks):
                _, e = scored(key_ref[j * BLOCK : j * BLOCK + BLOCK, :], queries[h], j * BLOCK, start_row, query_row)
                scores[h, n] = e
                sums = sums + jnp.sum(e, axis=0, keepdims=True)
            inverse = 1.0 / sums
            sums_ref[h : h + 1, at] = inverse
            acc = jnp.zeros((128, BLOCK), jnp.float32)
            for n, j in enumerate(blocks):
                p = (scores[h, n] * inverse).astype(jnp.bfloat16)
                acc = acc + jnp.dot(values_t[j], p, preferred_element_type=jnp.float32)
            heads_ref[pl.ds(4 * i, 4), :, h * 128 : h * 128 + 128] = acc.T.reshape(4, ROWS, 128)
        if i == 2:
            load_part.wait()
            delta_total = own_part[...].astype(jnp.float32)
            for n in range(3):
                send.arrived(parts_in.at[n], delta_sems.at[n], sib)
                delta_total = delta_total + parts_in[n].astype(jnp.float32)
            summed[...] = delta_total.astype(jnp.bfloat16)
            send(summed, other, delta_sems.at[3], to_zh)

    share = heads_ref[:, pl.ds(pl.multiple_of(g * 8, 8), 8), :]
    load_weight.wait()
    for core in range(2):
        rows = jnp.concatenate([share[2 * kk + core] for kk in range(8)], axis=0).astype(jnp.bfloat16)
        left = jnp.dot(rows, weight[:, :HALF], preferred_element_type=jnp.float32)
        right = jnp.dot(rows, weight[:, HALF:], preferred_element_type=jnp.float32)
        for kk in range(8):
            both = jnp.concatenate([left[kk * 8 : kk * 8 + 8], right[kk * 8 : kk * 8 + 8]], axis=0)
            partial[core, kk] = both.astype(jnp.bfloat16)
    for n, (a, b) in enumerate(fellows):
        kk = a * 4 + b
        send(partial.at[1 - c, kk], mate.at[kk], mate_sems.at[kk], sib)
    send(partial.at[1 - c, k], mate.at[k], mate_sems.at[k], sib)
    send.arrived(other, delta_sems.at[3], sib)
    delta_part[...] = (summed[...].astype(jnp.float32) + other[...].astype(jnp.float32)).astype(jnp.bfloat16)
    keep = pltpu.make_async_copy(delta_part, delta_sum.at[x], local_sems.at[2])
    keep.start()
    for to in (to_x[0], to_x[2]):
        send(delta_part, delta_sum.at[x], sum_sems.at[0, x], to)
    for (a, b), to in zip(fellows, to_fellows):
        kk = a * 4 + b
        send.arrived(mate.at[kk], mate_sems.at[kk], sib)
        total[kk] = (partial[c, kk].astype(jnp.float32) + mate[kk].astype(jnp.float32)).astype(jnp.bfloat16)
        send(total.at[kk], received.at[k], part_sems.at[k], to)
    send.arrived(mate.at[k], mate_sems.at[k], sib)
    both = partial[c, k].astype(jnp.float32) + mate[k].astype(jnp.float32)
    gain_row = as_row(post_gain)
    pick = lambda rows: jnp.where(g % 2 == 0, rows[:8], rows[8:])
    near_rows = pl.ds(pl.multiple_of(g // 2 * 16, 16), 16)
    own_tokens = pick(tokens[near_rows, :].astype(jnp.float32))
    dnorm = pick(cotangent[near_rows, :].astype(jnp.float32)) * gain_row
    for a, b in fellows:
        kk = a * 4 + b
        send.arrived(received.at[kk], part_sems.at[kk], sib)
        both = both + received[kk].astype(jnp.float32)
    attn = unstacked(both)
    scale = lax.rsqrt(jnp.mean(attn * attn, axis=-1, keepdims=True) + 1e-06)
    normal = attn * scale
    grad = scale * (dnorm - normal * jnp.mean(dnorm * normal, axis=-1, keepdims=True))
    for t, (region, (lo, size)) in enumerate(REGIONS.items()):
        into = group_in[region]
        into[g] = stacked(grad[:, lo : lo + size]).astype(jnp.bfloat16)
        for to in to_kin:
            send(into.at[g], into.at[g], group_sems.at[t, g], to)
    out_in[zh, x] = stacked(own_tokens + normal * gain_row).astype(jnp.bfloat16)
    for side, step in enumerate((1, 3)):
        n = (x + step) % 4
        send.arrived(delta_sum.at[n], sum_sems.at[0, n], sib)
        half = delta_sum.at[n, pl.ds(side * 16, 16), :]
        send(half, half, sum_sems.at[1 + side, n], to_x[2 - 2 * side])

    def ready(region):
        t, (lo, size) = list(REGIONS).index(region), REGIONS[region]
        into = group_in[region]
        for a, b in kin:
            gg = a * 2 + b
            send.arrived(into.at[gg], group_sems.at[t, gg], sib)
        for gg in range(0, 8, 2):
            first = unstacked(into[gg].astype(jnp.float32))
            second = unstacked(into[gg + 1].astype(jnp.float32))
            own_grad[pl.ds(gg * 8, 16), pl.ds(lo, size)] = jnp.concatenate([first, second], axis=0).astype(jnp.bfloat16)

    def returning():
        for _ in range(9):
            yield
        for to in to_x:
            send(out_in.at[zh, x], out_in.at[zh, x], out_sems.at[x], to)
        for _ in range(12):
            yield
        for step in (1, 2, 3):
            there = out_in.at[zh, (x + step) % 4]
            send.arrived(there, out_sems.at[(x + step) % 4], sib)
        send(out_in.at[zh], out_in.at[zh], out_sems.at[4], to_zh)

    spread(own_grad, full, send, piece_sems.at[1], pair_sems.at[1], local_sems.at[0], returning(), ready)
    send.arrived(out_in.at[1 - zh], out_sems.at[4], sib)
    for gg in range(0, 8, 2):
        first = unstacked(out_in[0, gg // 2].astype(jnp.float32))
        second = unstacked(out_in[1, gg // 2].astype(jnp.float32))
        output[pl.ds(gg * 8, 16), :] = jnp.concatenate([first, second], axis=0).astype(jnp.bfloat16)
    n = (x + 2) % 4
    for side in range(2):
        send.arrived(delta_sum.at[n, pl.ds(side * 16, 16), :], sum_sems.at[1 + side, n], sib)
    keep.wait()
    store.wait()
    send.finish()


def front(tokens, pre_gain, post_gain, qkv_weight, weight, doc_ids, cotangent, delta, cosine, sine):
    vmem = pl.BlockSpec(memory_space=pltpu.VMEM)
    hbm = pl.BlockSpec(memory_space=pl.ANY)
    shape = jax.ShapeDtypeStruct
    bf16, f32 = jnp.bfloat16, jnp.float32
    return pl.pallas_call(
        front_kernel,
        out_shape=(
            shape((ROWS, WIDTH), bf16),
            shape((16, ROWS, WIDTH), bf16),
            shape((16, ROWS, WIDTH), bf16),
            shape((4, 32, WIDTH), bf16),
            shape((1024, 256), bf16),
            shape((1024, 128), bf16),
            shape((1024, 128), bf16),
            shape((8, 1024), f32),
            shape((16, ROWS, 256), f32),
        ),
        in_specs=[vmem, vmem, vmem, hbm, hbm, vmem, vmem, hbm, vmem, vmem],
        out_specs=(vmem, hbm, hbm, hbm, vmem, vmem, vmem, vmem, vmem),
        scratch_shapes=[
            pltpu.VMEM((16, ROWS, WIDTH), bf16),
            pltpu.VMEM((ROWS, WIDTH), bf16),
            pltpu.VMEM((ROWS, WIDTH), bf16),
            pltpu.VMEM((WIDTH, 512), bf16),
            pltpu.VMEM((2, 4 * PART, 128), bf16),
            pltpu.VMEM((4 * PART, 128), f32),
            pltpu.VMEM((32, WIDTH), bf16),
            pltpu.VMEM((3, 32, WIDTH), bf16),
            pltpu.VMEM((32, WIDTH), bf16),
            pltpu.VMEM((32, WIDTH), bf16),
            pltpu.VMEM((32, WIDTH), bf16),
            pltpu.VMEM((8, 128), jnp.int32),
            pltpu.VMEM((2, 3, BLOCK, BLOCK), f32),
            pltpu.VMEM((STEPS, 128, BLOCK), bf16),
            pltpu.VMEM((256, WIDTH), bf16),
            pltpu.VMEM((2, 8, 16, HALF), bf16),
            pltpu.VMEM((8, 16, HALF), bf16),
            pltpu.VMEM((8, 16, HALF), bf16),
            pltpu.VMEM((8, 16, HALF), bf16),
            pltpu.VMEM((8, 16, 2 * NQ), bf16),
            pltpu.VMEM((8, 16, N1 // 2), bf16),
            pltpu.VMEM((8, 16, N2 // 2), bf16),
            pltpu.VMEM((2, 4, 16, HALF), bf16),
            pltpu.SemaphoreType.DMA((4 + 8 + 2 + 7 + 21 + 2 + 4 + 2 * SPREAD_SENDS,)),
            pltpu.SemaphoreType.DMA((2, 2, 6, 8)),
            pltpu.SemaphoreType.DMA((2, 8, 2)),
            pltpu.SemaphoreType.DMA((4,)),
            pltpu.SemaphoreType.DMA((PARTS,)),
            pltpu.SemaphoreType.DMA((5,)),
            pltpu.SemaphoreType.DMA((8,)),
            pltpu.SemaphoreType.DMA((8,)),
            pltpu.SemaphoreType.DMA((3, 8)),
            pltpu.SemaphoreType.DMA((5,)),
            pltpu.SemaphoreType.DMA((3, 4)),
        ],
        compiler_params=pltpu.CompilerParams(
            collective_id=0, has_side_effects=True, vmem_limit_bytes=60 * 2**20
        ),
        name="front",
    )(tokens, pre_gain, post_gain, qkv_weight, weight, doc_ids, cotangent, delta, cosine, sine)


CHUNK = 512
CHUNKS = WIDTH // CHUNK


def backward_kernel(
    grads_hbm, x_hbm, weight, heads, query_ref, key_ref, value_ref, inverse_ref, cosine, sine, doc_ids,
    delta, momentum, fragment, output, qkv_out, out_out, new_momentum, new_fragment, new_output, grads, x, slope, dprob, dkey, dvalue, keys_t, grad_proj, turned, heads_t, mixed, starts, sems,
):
    i = pl.program_id(0)

    def load(n, which):
        rows = pl.ds(n * BLOCK, BLOCK)
        src, dst = ((grads_hbm, grads), (x_hbm, x))[which]
        return pltpu.make_async_copy(src.at[rows, :], dst.at[rows, :], sems.at[which, n])

    @pl.when(i == 0)
    def _():
        for which in range(2):
            for n in range(STEPS):
                load(n, which).start()
        document_starts(doc_ids, starts)
        dkey[...] = jnp.zeros_like(dkey)
        dvalue[...] = jnp.zeros_like(dvalue)

    head = [slice(h * 128, h * 128 + 128) for h in range(2)]

    @pl.when(i < STEPS)
    def _():
        load(i, 0).wait()
        own = pl.ds(pl.multiple_of(i * BLOCK, BLOCK), BLOCK)
        grad_heads = lax.dot_general(
            grads[own, :], weight[...], (((1,), (1,)), ((), ())), preferred_element_type=jnp.float32
        ).astype(jnp.bfloat16)
        keys_t[i] = key_ref[own, :].astype(jnp.float32).T.astype(jnp.bfloat16)
        start_row, first = start_of(starts, i)
        query_row = lax.broadcasted_iota(jnp.int32, (1, BLOCK), 1) + i * BLOCK
        queries = [query_ref[own, head[h]] for h in range(2)]
        grad = [grad_heads[:, head[h]] for h in range(2)]

        def score(j, sums):
            out = []
            at = pl.ds(pl.multiple_of(j * BLOCK, BLOCK), BLOCK)
            for h in range(2):
                soft, e = scored(key_ref[at, :], queries[h], j * BLOCK, start_row, query_row)
                p = e * inverse_ref[h : h + 1, :]
                dp = lax.dot_general(
                    value_ref[at, :], grad[h], (((1,), (1,)), ((), ())), preferred_element_type=jnp.float32
                )
                dvalue[at, :] += jnp.dot(p.astype(jnp.bfloat16), grad[h], preferred_element_type=jnp.float32)
                out.append(sums[h] + jnp.sum(p * dp, axis=0, keepdims=True))
                slope[h, j] = p * ((1.0 - soft * soft) * query_scale)
                dprob[h, j] = dp
            return tuple(out)

        zero = jnp.zeros((1, BLOCK), jnp.float32)
        sums = lax.fori_loop(first, i + 1, score, (zero, zero))

        def mix(j, accs):
            out = []
            at = pl.ds(pl.multiple_of(j * BLOCK, BLOCK), BLOCK)
            for h in range(2):
                ds = (slope[h, j] * (dprob[h, j] - sums[h])).astype(jnp.bfloat16)
                dkey[at, :] += jnp.dot(ds, queries[h], preferred_element_type=jnp.float32)
                out.append(accs[h] + jnp.dot(keys_t[j], ds, preferred_element_type=jnp.float32))
            return tuple(out)

        zero = jnp.zeros((128, BLOCK), jnp.float32)
        accs = lax.fori_loop(first, i + 1, mix, (zero, zero))
        for h in range(2):
            grad_proj[own, head[h]] = turn(accs[h].T, cosine[own, :], -sine[own, :])

    @pl.when(i == STEPS)
    def _():
        grad_proj[:, 256:384] = turn(dkey[...], cosine[...], -sine[...])
        grad_proj[:, 384:512] = dvalue[...]
        turned[...] = grad_proj[...].T.astype(jnp.bfloat16)
        heads_t[...] = heads[...].T.astype(jnp.bfloat16)
        for n in range(STEPS):
            load(n, 1).wait()

    @pl.when(i >= STEPS)
    def _():
        at = pl.ds(pl.multiple_of((i - STEPS) * CHUNK, CHUNK), CHUNK)
        for j in range(4):
            part = jnp.dot(turned[j * 128 : j * 128 + 128, :], x[:, at], preferred_element_type=jnp.float32)
            mixed[pl.ds(j, CHUNK, stride=4), :] = part.T
        out_out[...] = jnp.dot(heads_t[...], grads[:, at], preferred_element_type=jnp.float32).astype(jnp.bfloat16)
        qkv_out[...] = mixed[...].astype(jnp.bfloat16)
        mean_delta = delta[...].astype(jnp.float32) / 8.0
        moment = 0.9 * momentum[...] + mean_delta
        new_momentum[...] = moment
        new_fragment[...] = fragment[...] - 0.7 * (mean_delta + 0.9 * moment)
        new_output[...] = output[...]


def backward(grads, gathered, weight, heads, query, key, value, inverse, cosine, sine, doc_ids, delta, momentum, fragment, output):
    whole = lambda *shape: pl.BlockSpec(shape, lambda i: (0, 0), pipeline_mode=pl.Buffered(1))
    chunk_of = lambda i: jnp.maximum(i - STEPS, 0)
    columns = lambda n: pl.BlockSpec((n, CHUNK), lambda i: (0, chunk_of(i)))
    hbm = pl.BlockSpec(memory_space=pl.ANY)
    return pl.pallas_call(
        backward_kernel,
        grid=(STEPS + CHUNKS,),
        in_specs=[
            hbm,
            hbm,
            whole(256, WIDTH),
            whole(1024, 256),
            whole(1024, 256),
            whole(1024, 128),
            whole(1024, 128),
            pl.BlockSpec((8, BLOCK), lambda i: (0, jnp.minimum(i, STEPS - 1))),
            whole(1024, 128),
            whole(1024, 128),
            whole(8, 128),
            columns(128),
            columns(128),
            columns(128),
            columns(ROWS),
        ],
        out_specs=[
            pl.BlockSpec((4 * CHUNK, 128), lambda i: (chunk_of(i), 0)),
            columns(256),
            columns(128),
            columns(128),
            columns(ROWS),
        ],
        scratch_shapes=[
            pltpu.VMEM((1024, WIDTH), jnp.bfloat16),
            pltpu.VMEM((1024, WIDTH), jnp.bfloat16),
            pltpu.VMEM((2, STEPS, BLOCK, BLOCK), jnp.float32),
            pltpu.VMEM((2, STEPS, BLOCK, BLOCK), jnp.float32),
            pltpu.VMEM((1024, 128), jnp.float32),
            pltpu.VMEM((1024, 128), jnp.float32),
            pltpu.VMEM((STEPS, 128, BLOCK), jnp.bfloat16),
            pltpu.VMEM((1024, 512), jnp.float32),
            pltpu.VMEM((512, 1024), jnp.bfloat16),
            pltpu.VMEM((256, 1024), jnp.bfloat16),
            pltpu.VMEM((4 * CHUNK, 128), jnp.float32),
            pltpu.VMEM((8, 128), jnp.int32),
            pltpu.SemaphoreType.DMA((2, STEPS)),
        ],
        out_shape=[
            jax.ShapeDtypeStruct((4 * WIDTH, 128), jnp.bfloat16),
            jax.ShapeDtypeStruct((256, WIDTH), jnp.bfloat16),
            jax.ShapeDtypeStruct((128, WIDTH), jnp.float32),
            jax.ShapeDtypeStruct((128, WIDTH), jnp.float32),
            jax.ShapeDtypeStruct((ROWS, WIDTH), jnp.bfloat16),
        ],
        compiler_params=pltpu.CompilerParams(vmem_limit_bytes=60 * 2**20),
        name="backward",
    )(
        grads, gathered, weight, heads, query, key, value, inverse, cosine, sine, doc_ids, delta, momentum, fragment, output
    )


def local(
    tokens,
    pre_gain,
    post_gain,
    qkv_weight,
    out_weight,
    doc_ids,
    cotangent,
    outer_delta,
    momentum,
    fragment,
):
    cosine, sine = tables(16 * ROWS, 128)
    doc_ids = doc_ids.reshape(8, 128)
    out_flat = out_weight.reshape(256, WIDTH)
    output, gathered, grad_rows, delta, query, key, value, inverse, heads = front(
        tokens, pre_gain.reshape(36, 128), post_gain.reshape(36, 128), qkv_weight.reshape(4 * WIDTH, 128), out_flat,
        doc_ids, cotangent, outer_delta[0], cosine, sine,
    )
    gathered, heads = gathered.reshape(16 * ROWS, WIDTH), heads.reshape(16 * ROWS, 256)
    grad_qkv, grad_out, new_momentum, new_fragment, output = backward(
        grad_rows.reshape(16 * ROWS, WIDTH), gathered, out_flat, heads, query, key, value, inverse, cosine, sine,
        doc_ids, delta.reshape(128, WIDTH), momentum, fragment, output,
    )
    return (output, grad_qkv.reshape(qkv_weight.shape), grad_out.reshape(out_weight.shape), new_momentum, new_fragment)


def solution(mesh):
    placed = (
        P("fsdp", None),
        P(),
        P(),
        P(None, "fsdp", None, None),
        P("fsdp", None, None, None),
        P(),
        P("fsdp", None),
        P("group", "fsdp", None),
        P("fsdp", None),
        P("fsdp", None),
    )
    return jax.shard_map(
        local,
        mesh=mesh,
        in_specs=placed,
        out_specs=(
            P("fsdp", None),
            P(None, "fsdp", None, None),
            P("fsdp", None, None, None),
            P("fsdp", None),
            P("fsdp", None),
        ),
        check_vma=False,
    )
```

```python
import functools

import jax
import jax.numpy as jnp
import numpy as np
from jax import lax
from jax.experimental import pallas as pl
from jax.experimental.pallas import tpu as pltpu
from jax.sharding import PartitionSpec as P

softcap = 50.0
query_scale = 1.0 / 12.0
MESH = pl.DeviceIdType.MESH
WIDTH = 4608
HALF = WIDTH // 2
ROWS = 64
N1, N2, NQ = 10 * 128, 10 * 128, 4 * 128
NP = N1 + N2
REGIONS = {"q": (NP, 4 * NQ), "a": (0, N1), "b": (N1, N2)}


def place():
    group, fsdp = lax.axis_index("group"), lax.axis_index("fsdp")
    return group // 2, group % 2, fsdp // 8, (fsdp // 2) % 4, fsdp % 2


def device(x, zh, zl, y, c):
    return (x * 2 + zh, (zl * 4 + y) * 2 + c)


class Sender:
    def __init__(self, sems):
        self.sems, self.copies = sems, []

    def __call__(self, src, dst, recv, to):
        copy = pltpu.make_async_remote_copy(
            src_ref=src,
            dst_ref=dst,
            send_sem=self.sems.at[len(self.copies)],
            recv_sem=recv,
            device_id=to,
            device_id_type=MESH,
        )
        copy.start()
        self.copies.append(copy)

    def arrived(self, ref, recv, to):
        pltpu.make_async_remote_copy(
            src_ref=ref,
            dst_ref=ref,
            send_sem=self.sems.at[0],
            recv_sem=recv,
            device_id=to,
            device_id_type=MESH,
        ).wait_recv()

    def finish(self):
        for copy in self.copies:
            copy.wait_send()


SPREAD_SENDS = 69


def spread(own, full, send, piece_sems, pair_sems, local_sem, work=iter(()), ready=lambda region: None):
    x, zh, zl, y, c = place()
    k, kz = zl * 4 + y, (1 - zl) * 4 + y
    near_k, near_kz = ([b * 4 + (y + s) % 4 for s in (1, 3, 2)] for b in (zl, 1 - zl))
    to_sib = device(x, zh, zl, y, 1 - c)
    to_z = device(x, zh, 1 - zl, y, c)
    to_y = [device(x, zh, zl, (y + s) % 4, c) for s in (1, 3)]
    to_x = [device((x + s) % 4, zh, zl, y, c) for s in (1, 3)]
    quarters = [x, (x + 1) % 4, (x + 3) % 4, (x + 2) % 4]
    starts = {"a": 0, "b": N1} | {w: NP + quarters[w] * NQ for w in range(4)}
    sizes = {"a": N1, "b": N2} | {w: NQ for w in range(4)}
    index = {"a": 0, "b": 1} | {w: 2 + quarters[w] for w in range(4)}

    def cols(t, half):
        lo, size = starts[t], sizes[t]
        if half is not None:
            size = size // 2
            lo = lo + half * size
        if not isinstance(lo, int):
            lo = pl.multiple_of(lo, 128)
        return pl.ds(lo, size)

    def push(kk, t, to, half=None):
        at = cols(t, half)
        src = own.at[:, at] if kk is k else full.at[2 * kk + c, :, at]
        send(src, full.at[2 * kk + c, :, at], piece_sems.at[half or 0, index[t], kk], to)

    def here(kk, t, half=None):
        next(work, None)
        send.arrived(full.at[2 * kk + c, :, cols(t, half)], piece_sems.at[half or 0, index[t], kk], to_sib)

    def pair(kk, lo, size, slot):
        ref = full.at[2 * kk + c, :, pl.ds(lo, size)]
        send(ref, ref, pair_sems.at[kk, slot], to_sib)

    def ring(kk, t, links, side):
        push(kk, t, links[1 - side], side)

    def both(kk, t, links):
        for to in links:
            push(kk, t, to)

    ready("q")
    push(k, 0, to_z)
    both(k, 0, to_y)
    ready("a")
    push(k, "a", to_z)
    ready("b")
    both(k, "b", to_y)
    push(k, "b", to_z)
    both(k, "a", to_y)
    keep = pltpu.make_async_copy(own, full.at[2 * k + c], local_sem)
    keep.start()
    send(own, full.at[2 * k + c], pair_sems.at[k, 0], to_sib)

    here(kz, 0)
    both(kz, 0, to_y)
    both(kz, 0, to_x)
    for side in range(2):
        kk = near_k[side]
        here(kk, 0)
        ring(kk, 0, to_y, side)
        both(kk, 0, to_x)
    here(kz, "a")
    both(kz, "a", to_y)
    for side in range(2):
        kk = near_k[side]
        here(kk, "b")
        push(kk, "b", to_z)
        ring(kk, "b", to_y, side)
    for side in range(2):
        kk = near_kz[side]
        here(kk, 0)
        ring(kk, 0, to_y, side)
        both(kk, 0, to_x)
    here(near_k[2], 0, 0)
    here(near_k[2], 0, 1)
    both(near_k[2], 0, to_x)
    for side in range(2):
        kk = near_k[side]
        here(kk, "a")
        ring(kk, "a", to_y, side)
        pair(kk, 0, NP, 0)
    here(near_k[2], "b", 0)
    here(near_k[2], "b", 1)
    push(near_k[2], "b", to_z)
    here(near_kz[2], 0, 0)
    here(near_kz[2], 0, 1)
    both(near_kz[2], 0, to_x)
    for side in range(2):
        here(near_kz[side], "a")
        ring(near_kz[side], "a", to_y, side)
    others = [kz, near_k[0], near_k[1], near_kz[0], near_kz[1], near_k[2], near_kz[2]]
    for kk in others[:5]:
        for side in range(2):
            here(kk, 1 + side)
            ring(kk, 1 + side, to_x, side)
    here(kz, "b")
    pair(kz, 0, NP, 0)
    for kk in others[5:]:
        for side in range(2):
            here(kk, 1 + side)
            ring(kk, 1 + side, to_x, side)
    here(near_k[2], "a", 0)
    here(near_k[2], "a", 1)
    pair(near_k[2], 0, NP, 0)
    for side in range(2):
        here(near_kz[side], "b")
        pair(near_kz[side], 0, NP, 0)
    for kk in others[:5]:
        here(kk, 3, 0)
        here(kk, 3, 1)
        pair(kk, NP, 4 * NQ, 1)
    here(near_kz[2], "a", 0)
    here(near_kz[2], "a", 1)
    here(near_kz[2], "b")
    pair(near_kz[2], 0, NP, 0)
    for kk in others[5:]:
        here(kk, 3, 0)
        here(kk, 3, 1)
        pair(kk, NP, 4 * NQ, 1)
    for _ in work:
        pass
    send.arrived(full.at[2 * k + 1 - c], pair_sems.at[k, 0], to_sib)
    for kk in others:
        send.arrived(full.at[2 * kk + 1 - c, :, pl.ds(0, NP)], pair_sems.at[kk, 0], to_sib)
        send.arrived(full.at[2 * kk + 1 - c, :, pl.ds(NP, 4 * NQ)], pair_sems.at[kk, 1], to_sib)
    keep.wait()


def greet(devices):
    barrier = pltpu.get_barrier_semaphore()
    for to in devices:
        pl.semaphore_signal(barrier, inc=1, device_id=to, device_id_type=MESH)


def met(devices):
    pl.semaphore_wait(pltpu.get_barrier_semaphore(), len(devices))


def stacked(rows):
    half = rows.shape[1] // 2
    return jnp.concatenate([rows[:, :half], rows[:, half:]], axis=0)


def unstacked(rows):
    return jnp.concatenate([rows[:8], rows[8:]], axis=1)


def tables(length, width):
    half = width // 2
    positions = np.arange(length, dtype=np.float32)[:, None]
    freqs = np.power(np.float32(10000.0), -(np.float32(2.0) * np.arange(half, dtype=np.float32) / np.float32(width)))
    angle = positions * freqs[None, :].astype(np.float32)
    cosine, sine = np.cos(angle), np.sin(angle)
    return (
        jnp.asarray(np.concatenate([cosine, cosine], axis=1)),
        jnp.asarray(np.concatenate([-sine, sine], axis=1)),
    )


BLOCK = 256
STEPS = 4


def turn(values, cosine, sine):
    return values * cosine + pltpu.roll(values, 64, 1) * sine


def document_starts(doc_ids, starts):
    ids = doc_ids[...]
    first = jnp.zeros_like(ids)
    for n in range(3):
        first += jnp.where(ids > n, jnp.sum((ids == n).astype(jnp.int32)), 0)
    starts[...] = first


def start_of(starts, i):
    row = jnp.concatenate([starts[pl.ds(2 * i, 1), :], starts[pl.ds(2 * i + 1, 1), :]], axis=1)
    return row, jnp.min(row) // BLOCK


def scored(keys, queries, first_key, start_row, query_row):
    raw = lax.dot_general(keys, queries, (((1,), (1,)), ((), ())), preferred_element_type=jnp.float32)
    soft = jnp.tanh(raw * (query_scale / softcap))
    row = lax.broadcasted_iota(jnp.int32, raw.shape, 0) + first_key
    allowed = (row >= start_row) & (row <= query_row)
    return soft, jnp.where(allowed, jnp.exp(softcap * soft), 0.0)


def as_row(gain):
    return jnp.concatenate([gain[n : n + 1, :] for n in range(WIDTH // 128)], axis=1)


PARTS = 8
PART = WIDTH // PARTS


def weight_parts(weight, wide, rough, mixed, in_sems):
    def load(n):
        return pltpu.make_async_copy(weight.at[pl.ds(4 * PART * n, 4 * PART), :], rough.at[n % 2], in_sems.at[n])

    load(0).start()
    for n in range(PARTS):
        if n + 1 < PARTS:
            load(n + 1).start()
        yield
        load(n).wait()
        mixed[...] = rough[n % 2].astype(jnp.float32)
        for j in range(4):
            wide[pl.ds(PART * n, PART), j * 128 : j * 128 + 128] = mixed[pl.ds(j, PART, stride=4), :].astype(jnp.bfloat16)


def front_kernel(
    tokens, pre_gain, post_gain, qkv_hbm, weight_hbm, doc_ids, cotangent, delta, cosine, sine,
    output, gathered, full, delta_sum, query_ref, key_ref, value_ref, sums_ref, heads_ref,
    everything, own, own_grad, wide, rough, mixed, own_part, parts_in, summed, other, delta_part, starts, scores, values_t,
    weight, partial, received, mate, total, group_q, group_a, group_b, out_in,
    send_sems, piece_sems, pair_sems, local_sems, in_sems, delta_sems,
    mate_sems, part_sems, group_sems, out_sems, sum_sems,
):
    x, zh, zl, y, c = place()
    k, g = zl * 4 + y, x * 2 + zh
    sib = device(x, zh, zl, y, 1 - c)
    chips = [(a, b) for a in range(2) for b in range(4)][1:]
    fellows = [((zl + a) % 2, (y + b) % 4) for a, b in chips]
    to_fellows = [device(x, zh, a, b, c) for a, b in fellows]
    kin = [((x + b) % 4, (zh + a) % 2) for a, b in chips]
    to_kin = [device(a, b, zl, y, c) for a, b in kin]
    to_x = [device((x + step) % 4, zh, zl, y, c) for step in (1, 2, 3)]
    to_zh = device(x, 1 - zh, zl, y, c)
    group_in = {"q": group_q, "a": group_a, "b": group_b}
    greet([sib] + to_fellows + to_kin)
    send = Sender(send_sems)
    rows_of = lambda n: pl.ds(pl.multiple_of(n % 4 * 32, 32), 32)
    load_part = pltpu.make_async_copy(delta.at[rows_of(x), :], own_part, delta_sems.at[4])
    load_part.start()

    def background():
        for _ in weight_parts(qkv_hbm, wide, rough, mixed, in_sems):
            yield
        load_weight.start()

    load_weight = pltpu.make_async_copy(weight_hbm, weight, local_sems.at[1])
    work = background()
    next(work)
    values = tokens[...].astype(jnp.float32)
    scale = lax.rsqrt(jnp.mean(values * values, axis=-1, keepdims=True) + 1e-06)
    own[...] = (values * scale * as_row(pre_gain)).astype(jnp.bfloat16)
    document_starts(doc_ids, starts)
    met([sib] + to_fellows + to_kin)
    for n, step in enumerate((1, 2, 3)):
        send(delta.at[rows_of(x + step), :], parts_in.at[n], delta_sems.at[n], to_x[n])
    spread(own, everything, send, piece_sems.at[0], pair_sems.at[0], local_sems.at[0], work)
    store = pltpu.make_async_copy(everything, gathered, local_sems.at[3])
    store.start()

    for i in range(STEPS):
        at = pl.ds(i * BLOCK, BLOCK)
        rows = everything[pl.ds(4 * i, 4)].reshape(BLOCK, WIDTH)
        proj = jnp.dot(rows, wide[...], preferred_element_type=jnp.float32)
        queries = [turn(proj[:, h * 128 : h * 128 + 128], cosine[at, :], sine[at, :]).astype(jnp.bfloat16) for h in range(2)]
        query_ref[at, :128] = queries[0]
        query_ref[at, 128:] = queries[1]
        key_ref[at, :] = turn(proj[:, 256:384], cosine[at, :], sine[at, :]).astype(jnp.bfloat16)
        value_ref[at, :] = proj[:, 384:].astype(jnp.bfloat16)
        values_t[i] = proj[:, 384:].T.astype(jnp.bfloat16)
        start_row, _ = start_of(starts, i)
        query_row = lax.broadcasted_iota(jnp.int32, (1, BLOCK), 1) + i * BLOCK
        blocks = range(max(0, i - 2), i + 1)
        for h in range(2):
            sums = jnp.zeros((1, BLOCK), jnp.float32)
            for n, j in enumerate(blocks):
                _, e = scored(key_ref[j * BLOCK : j * BLOCK + BLOCK, :], queries[h], j * BLOCK, start_row, query_row)
                scores[h, n] = e
                sums = sums + jnp.sum(e, axis=0, keepdims=True)
            inverse = 1.0 / sums
            sums_ref[h : h + 1, at] = inverse
            acc = jnp.zeros((128, BLOCK), jnp.float32)
            for n, j in enumerate(blocks):
                p = (scores[h, n] * inverse).astype(jnp.bfloat16)
                acc = acc + jnp.dot(values_t[j], p, preferred_element_type=jnp.float32)
            heads_ref[pl.ds(4 * i, 4), :, h * 128 : h * 128 + 128] = acc.T.reshape(4, ROWS, 128)
        if i == 0:
            load_part.wait()
            delta_total = own_part[...].astype(jnp.float32)
            for n in range(3):
                send.arrived(parts_in.at[n], delta_sems.at[n], sib)
                delta_total = delta_total + parts_in[n].astype(jnp.float32)
            summed[...] = delta_total.astype(jnp.bfloat16)
            send(summed, other, delta_sems.at[3], to_zh)

    share = heads_ref[:, pl.ds(pl.multiple_of(g * 8, 8), 8), :]
    load_weight.wait()
    for core in range(2):
        rows = jnp.concatenate([share[2 * kk + core] for kk in range(8)], axis=0).astype(jnp.bfloat16)
        left = jnp.dot(rows, weight[:, :HALF], preferred_element_type=jnp.float32)
        right = jnp.dot(rows, weight[:, HALF:], preferred_element_type=jnp.float32)
        for kk in range(8):
            both = jnp.concatenate([left[kk * 8 : kk * 8 + 8], right[kk * 8 : kk * 8 + 8]], axis=0)
            partial[core, kk] = both.astype(jnp.bfloat16)
    for n, (a, b) in enumerate(fellows):
        kk = a * 4 + b
        send(partial.at[1 - c, kk], mate.at[kk], mate_sems.at[kk], sib)
    send(partial.at[1 - c, k], mate.at[k], mate_sems.at[k], sib)
    for (a, b), to in zip(fellows, to_fellows):
        kk = a * 4 + b
        send.arrived(mate.at[kk], mate_sems.at[kk], sib)
        total[kk] = (partial[c, kk].astype(jnp.float32) + mate[kk].astype(jnp.float32)).astype(jnp.bfloat16)
        send(total.at[kk], received.at[k], part_sems.at[k], to)
    send.arrived(mate.at[k], mate_sems.at[k], sib)
    both = partial[c, k].astype(jnp.float32) + mate[k].astype(jnp.float32)
    send.arrived(other, delta_sems.at[3], sib)
    delta_part[...] = (summed[...].astype(jnp.float32) + other[...].astype(jnp.float32)).astype(jnp.bfloat16)
    keep = pltpu.make_async_copy(delta_part, delta_sum.at[x], local_sems.at[2])
    keep.start()
    for to in (to_x[0], to_x[2]):
        send(delta_part, delta_sum.at[x], sum_sems.at[0, x], to)
    gain_row = as_row(post_gain)
    pick = lambda rows: jnp.where(g % 2 == 0, rows[:8], rows[8:])
    near_rows = pl.ds(pl.multiple_of(g // 2 * 16, 16), 16)
    own_tokens = pick(tokens[near_rows, :].astype(jnp.float32))
    dnorm = pick(cotangent[near_rows, :].astype(jnp.float32)) * gain_row
    for a, b in fellows:
        kk = a * 4 + b
        send.arrived(received.at[kk], part_sems.at[kk], sib)
        both = both + received[kk].astype(jnp.float32)
    attn = unstacked(both)
    scale = lax.rsqrt(jnp.mean(attn * attn, axis=-1, keepdims=True) + 1e-06)
    normal = attn * scale
    grad = scale * (dnorm - normal * jnp.mean(dnorm * normal, axis=-1, keepdims=True))
    for t, (region, (lo, size)) in enumerate(REGIONS.items()):
        into = group_in[region]
        into[g] = stacked(grad[:, lo : lo + size]).astype(jnp.bfloat16)
        for to in to_kin:
            send(into.at[g], into.at[g], group_sems.at[t, g], to)
    out_in[zh, x] = stacked(own_tokens + normal * gain_row).astype(jnp.bfloat16)
    for side, step in enumerate((1, 3)):
        n = (x + step) % 4
        send.arrived(delta_sum.at[n], sum_sems.at[0, n], sib)
        half = delta_sum.at[n, pl.ds(side * 16, 16), :]
        send(half, half, sum_sems.at[1 + side, n], to_x[2 - 2 * side])

    def ready(region):
        t, (lo, size) = list(REGIONS).index(region), REGIONS[region]
        into = group_in[region]
        for a, b in kin:
            gg = a * 2 + b
            send.arrived(into.at[gg], group_sems.at[t, gg], sib)
        for gg in range(0, 8, 2):
            first = unstacked(into[gg].astype(jnp.float32))
            second = unstacked(into[gg + 1].astype(jnp.float32))
            own_grad[pl.ds(gg * 8, 16), pl.ds(lo, size)] = jnp.concatenate([first, second], axis=0).astype(jnp.bfloat16)

    def returning():
        for _ in range(9):
            yield
        for to in to_x:
            send(out_in.at[zh, x], out_in.at[zh, x], out_sems.at[x], to)
        for _ in range(12):
            yield
        for step in (1, 2, 3):
            there = out_in.at[zh, (x + step) % 4]
            send.arrived(there, out_sems.at[(x + step) % 4], sib)
        send(out_in.at[zh], out_in.at[zh], out_sems.at[4], to_zh)

    spread(own_grad, full, send, piece_sems.at[1], pair_sems.at[1], local_sems.at[0], returning(), ready)
    send.arrived(out_in.at[1 - zh], out_sems.at[4], sib)
    for gg in range(0, 8, 2):
        first = unstacked(out_in[0, gg // 2].astype(jnp.float32))
        second = unstacked(out_in[1, gg // 2].astype(jnp.float32))
        output[pl.ds(gg * 8, 16), :] = jnp.concatenate([first, second], axis=0).astype(jnp.bfloat16)
    n = (x + 2) % 4
    for side in range(2):
        send.arrived(delta_sum.at[n, pl.ds(side * 16, 16), :], sum_sems.at[1 + side, n], sib)
    keep.wait()
    store.wait()
    send.finish()


def front(tokens, pre_gain, post_gain, qkv_weight, weight, doc_ids, cotangent, delta, cosine, sine):
    vmem = pl.BlockSpec(memory_space=pltpu.VMEM)
    hbm = pl.BlockSpec(memory_space=pl.ANY)
    shape = jax.ShapeDtypeStruct
    bf16, f32 = jnp.bfloat16, jnp.float32
    return pl.pallas_call(
        front_kernel,
        out_shape=(
            shape((ROWS, WIDTH), bf16),
            shape((16, ROWS, WIDTH), bf16),
            shape((16, ROWS, WIDTH), bf16),
            shape((4, 32, WIDTH), bf16),
            shape((1024, 256), bf16),
            shape((1024, 128), bf16),
            shape((1024, 128), bf16),
            shape((8, 1024), f32),
            shape((16, ROWS, 256), f32),
        ),
        in_specs=[vmem, vmem, vmem, hbm, hbm, vmem, vmem, hbm, vmem, vmem],
        out_specs=(vmem, hbm, hbm, hbm, vmem, vmem, vmem, vmem, vmem),
        scratch_shapes=[
            pltpu.VMEM((16, ROWS, WIDTH), bf16),
            pltpu.VMEM((ROWS, WIDTH), bf16),
            pltpu.VMEM((ROWS, WIDTH), bf16),
            pltpu.VMEM((WIDTH, 512), bf16),
            pltpu.VMEM((2, 4 * PART, 128), bf16),
            pltpu.VMEM((4 * PART, 128), f32),
            pltpu.VMEM((32, WIDTH), bf16),
            pltpu.VMEM((3, 32, WIDTH), bf16),
            pltpu.VMEM((32, WIDTH), bf16),
            pltpu.VMEM((32, WIDTH), bf16),
            pltpu.VMEM((32, WIDTH), bf16),
            pltpu.VMEM((8, 128), jnp.int32),
            pltpu.VMEM((2, 3, BLOCK, BLOCK), f32),
            pltpu.VMEM((STEPS, 128, BLOCK), bf16),
            pltpu.VMEM((256, WIDTH), bf16),
            pltpu.VMEM((2, 8, 16, HALF), bf16),
            pltpu.VMEM((8, 16, HALF), bf16),
            pltpu.VMEM((8, 16, HALF), bf16),
            pltpu.VMEM((8, 16, HALF), bf16),
            pltpu.VMEM((8, 16, 2 * NQ), bf16),
            pltpu.VMEM((8, 16, N1 // 2), bf16),
            pltpu.VMEM((8, 16, N2 // 2), bf16),
            pltpu.VMEM((2, 4, 16, HALF), bf16),
            pltpu.SemaphoreType.DMA((4 + 8 + 2 + 7 + 21 + 2 + 4 + 2 * SPREAD_SENDS,)),
            pltpu.SemaphoreType.DMA((2, 2, 6, 8)),
            pltpu.SemaphoreType.DMA((2, 8, 2)),
            pltpu.SemaphoreType.DMA((4,)),
            pltpu.SemaphoreType.DMA((PARTS,)),
            pltpu.SemaphoreType.DMA((5,)),
            pltpu.SemaphoreType.DMA((8,)),
            pltpu.SemaphoreType.DMA((8,)),
            pltpu.SemaphoreType.DMA((3, 8)),
            pltpu.SemaphoreType.DMA((5,)),
            pltpu.SemaphoreType.DMA((3, 4)),
        ],
        compiler_params=pltpu.CompilerParams(
            collective_id=0, has_side_effects=True, vmem_limit_bytes=60 * 2**20
        ),
        name="front",
    )(tokens, pre_gain, post_gain, qkv_weight, weight, doc_ids, cotangent, delta, cosine, sine)


CHUNK = 768
CHUNKS = WIDTH // CHUNK


def backward_kernel(
    grads_hbm, x_hbm, weight, heads, query_ref, key_ref, value_ref, inverse_ref, cosine, sine, doc_ids,
    delta, momentum, fragment, output, qkv_out, out_out, new_momentum, new_fragment, new_output, grads, x, slope, dprob, dkey, dvalue, keys_t, grad_proj, turned, heads_t, mixed, starts, sems,
):
    i = pl.program_id(0)

    def load(n, which):
        rows = pl.ds(n * BLOCK, BLOCK)
        src, dst = ((grads_hbm, grads), (x_hbm, x))[which]
        return pltpu.make_async_copy(src.at[rows, :], dst.at[rows, :], sems.at[which, n])

    @pl.when(i == 0)
    def _():
        for which in range(2):
            for n in range(STEPS):
                load(n, which).start()
        document_starts(doc_ids, starts)
        dkey[...] = jnp.zeros_like(dkey)
        dvalue[...] = jnp.zeros_like(dvalue)

    head = [slice(h * 128, h * 128 + 128) for h in range(2)]

    @pl.when(i < STEPS)
    def _():
        load(i, 0).wait()
        own = pl.ds(pl.multiple_of(i * BLOCK, BLOCK), BLOCK)
        grad_heads = lax.dot_general(
            grads[own, :], weight[...], (((1,), (1,)), ((), ())), preferred_element_type=jnp.float32
        ).astype(jnp.bfloat16)
        keys_t[i] = key_ref[own, :].astype(jnp.float32).T.astype(jnp.bfloat16)
        start_row, first = start_of(starts, i)
        query_row = lax.broadcasted_iota(jnp.int32, (1, BLOCK), 1) + i * BLOCK
        queries = [query_ref[own, head[h]] for h in range(2)]
        grad = [grad_heads[:, head[h]] for h in range(2)]

        def score(j, sums):
            out = []
            at = pl.ds(pl.multiple_of(j * BLOCK, BLOCK), BLOCK)
            for h in range(2):
                soft, e = scored(key_ref[at, :], queries[h], j * BLOCK, start_row, query_row)
                p = e * inverse_ref[h : h + 1, :]
                dp = lax.dot_general(
                    value_ref[at, :], grad[h], (((1,), (1,)), ((), ())), preferred_element_type=jnp.float32
                )
                dvalue[at, :] += jnp.dot(p.astype(jnp.bfloat16), grad[h], preferred_element_type=jnp.float32)
                out.append(sums[h] + jnp.sum(p * dp, axis=0, keepdims=True))
                slope[h, j] = p * ((1.0 - soft * soft) * query_scale)
                dprob[h, j] = dp
            return tuple(out)

        zero = jnp.zeros((1, BLOCK), jnp.float32)
        sums = lax.fori_loop(first, i + 1, score, (zero, zero))

        def mix(j, accs):
            out = []
            at = pl.ds(pl.multiple_of(j * BLOCK, BLOCK), BLOCK)
            for h in range(2):
                ds = (slope[h, j] * (dprob[h, j] - sums[h])).astype(jnp.bfloat16)
                dkey[at, :] += jnp.dot(ds, queries[h], preferred_element_type=jnp.float32)
                out.append(accs[h] + jnp.dot(keys_t[j], ds, preferred_element_type=jnp.float32))
            return tuple(out)

        zero = jnp.zeros((128, BLOCK), jnp.float32)
        accs = lax.fori_loop(first, i + 1, mix, (zero, zero))
        for h in range(2):
            grad_proj[own, head[h]] = turn(accs[h].T, cosine[own, :], -sine[own, :])

    @pl.when(i == STEPS)
    def _():
        grad_proj[:, 256:384] = turn(dkey[...], cosine[...], -sine[...])
        grad_proj[:, 384:512] = dvalue[...]
        turned[...] = grad_proj[...].T.astype(jnp.bfloat16)
        heads_t[...] = heads[...].T.astype(jnp.bfloat16)
        for n in range(STEPS):
            load(n, 1).wait()

    @pl.when(i >= STEPS)
    def _():
        at = pl.ds(pl.multiple_of((i - STEPS) * CHUNK, CHUNK), CHUNK)
        for j in range(4):
            part = jnp.dot(turned[j * 128 : j * 128 + 128, :], x[:, at], preferred_element_type=jnp.float32)
            mixed[pl.ds(j, CHUNK, stride=4), :] = part.T
        out_out[...] = jnp.dot(heads_t[...], grads[:, at], preferred_element_type=jnp.float32).astype(jnp.bfloat16)
        qkv_out[...] = mixed[...].astype(jnp.bfloat16)

    @pl.when((i >= 1) & (i <= CHUNKS))
    def _():
        mean_delta = delta[...].astype(jnp.float32) / 8.0
        moment = 0.9 * momentum[...] + mean_delta
        new_momentum[...] = moment
        new_fragment[...] = fragment[...] - 0.7 * (mean_delta + 0.9 * moment)
        new_output[...] = output[...]


def backward(grads, gathered, weight, heads, query, key, value, inverse, cosine, sine, doc_ids, delta, momentum, fragment, output):
    whole = lambda *shape: pl.BlockSpec(shape, lambda i: (0, 0), pipeline_mode=pl.Buffered(1))
    chunk_of = lambda i: jnp.maximum(i - STEPS, 0)
    columns = lambda n: pl.BlockSpec((n, CHUNK), lambda i: (0, chunk_of(i)))
    early = lambda n: pl.BlockSpec((n, CHUNK), lambda i: (0, jnp.clip(i - 1, 0, CHUNKS - 1)))
    hbm = pl.BlockSpec(memory_space=pl.ANY)
    return pl.pallas_call(
        backward_kernel,
        grid=(STEPS + CHUNKS,),
        in_specs=[
            hbm,
            hbm,
            whole(256, WIDTH),
            whole(1024, 256),
            whole(1024, 256),
            whole(1024, 128),
            whole(1024, 128),
            pl.BlockSpec((8, BLOCK), lambda i: (0, jnp.minimum(i, STEPS - 1))),
            whole(1024, 128),
            whole(1024, 128),
            whole(8, 128),
            early(128),
            early(128),
            early(128),
            early(ROWS),
        ],
        out_specs=[
            pl.BlockSpec((4 * CHUNK, 128), lambda i: (chunk_of(i), 0)),
            columns(256),
            early(128),
            early(128),
            early(ROWS),
        ],
        scratch_shapes=[
            pltpu.VMEM((1024, WIDTH), jnp.bfloat16),
            pltpu.VMEM((1024, WIDTH), jnp.bfloat16),
            pltpu.VMEM((2, STEPS, BLOCK, BLOCK), jnp.float32),
            pltpu.VMEM((2, STEPS, BLOCK, BLOCK), jnp.float32),
            pltpu.VMEM((1024, 128), jnp.float32),
            pltpu.VMEM((1024, 128), jnp.float32),
            pltpu.VMEM((STEPS, 128, BLOCK), jnp.bfloat16),
            pltpu.VMEM((1024, 512), jnp.float32),
            pltpu.VMEM((512, 1024), jnp.bfloat16),
            pltpu.VMEM((256, 1024), jnp.bfloat16),
            pltpu.VMEM((4 * CHUNK, 128), jnp.float32),
            pltpu.VMEM((8, 128), jnp.int32),
            pltpu.SemaphoreType.DMA((2, STEPS)),
        ],
        out_shape=[
            jax.ShapeDtypeStruct((4 * WIDTH, 128), jnp.bfloat16),
            jax.ShapeDtypeStruct((256, WIDTH), jnp.bfloat16),
            jax.ShapeDtypeStruct((128, WIDTH), jnp.float32),
            jax.ShapeDtypeStruct((128, WIDTH), jnp.float32),
            jax.ShapeDtypeStruct((ROWS, WIDTH), jnp.bfloat16),
        ],
        compiler_params=pltpu.CompilerParams(vmem_limit_bytes=60 * 2**20),
        name="backward",
    )(
        grads, gathered, weight, heads, query, key, value, inverse, cosine, sine, doc_ids, delta, momentum, fragment, output
    )


def local(
    tokens,
    pre_gain,
    post_gain,
    qkv_weight,
    out_weight,
    doc_ids,
    cotangent,
    outer_delta,
    momentum,
    fragment,
):
    cosine, sine = tables(16 * ROWS, 128)
    doc_ids = doc_ids.reshape(8, 128)
    out_flat = out_weight.reshape(256, WIDTH)
    output, gathered, grad_rows, delta, query, key, value, inverse, heads = front(
        tokens, pre_gain.reshape(36, 128), post_gain.reshape(36, 128), qkv_weight.reshape(4 * WIDTH, 128), out_flat,
        doc_ids, cotangent, outer_delta[0], cosine, sine,
    )
    gathered, heads = gathered.reshape(16 * ROWS, WIDTH), heads.reshape(16 * ROWS, 256)
    grad_qkv, grad_out, new_momentum, new_fragment, output = backward(
        grad_rows.reshape(16 * ROWS, WIDTH), gathered, out_flat, heads, query, key, value, inverse, cosine, sine,
        doc_ids, delta.reshape(128, WIDTH), momentum, fragment, output,
    )
    return (output, grad_qkv.reshape(qkv_weight.shape), grad_out.reshape(out_weight.shape), new_momentum, new_fragment)


def solution(mesh):
    placed = (
        P("fsdp", None),
        P(),
        P(),
        P(None, "fsdp", None, None),
        P("fsdp", None, None, None),
        P(),
        P("fsdp", None),
        P("group", "fsdp", None),
        P("fsdp", None),
        P("fsdp", None),
    )
    return jax.shard_map(
        local,
        mesh=mesh,
        in_specs=placed,
        out_specs=(
            P("fsdp", None),
            P(None, "fsdp", None, None),
            P("fsdp", None, None, None),
            P("fsdp", None),
            P("fsdp", None),
        ),
        check_vma=False,
    )
```

```python
import functools

import jax
import jax.numpy as jnp
import numpy as np
from jax import lax
from jax.experimental import pallas as pl
from jax.experimental.pallas import tpu as pltpu
from jax.sharding import PartitionSpec as P

softcap = 50.0
query_scale = 1.0 / 12.0
MESH = pl.DeviceIdType.MESH
WIDTH = 4608
HALF = WIDTH // 2
ROWS = 64
N1, N2, NQ = 10 * 128, 10 * 128, 4 * 128
NP = N1 + N2
REGIONS = {"q": (NP, 4 * NQ), "a": (0, N1), "b": (N1, N2)}


def place():
    group, fsdp = lax.axis_index("group"), lax.axis_index("fsdp")
    return group // 2, group % 2, fsdp // 8, (fsdp // 2) % 4, fsdp % 2


def device(x, zh, zl, y, c):
    return (x * 2 + zh, (zl * 4 + y) * 2 + c)


class Sender:
    def __init__(self, sems):
        self.sems, self.copies = sems, []

    def __call__(self, src, dst, recv, to):
        copy = pltpu.make_async_remote_copy(
            src_ref=src,
            dst_ref=dst,
            send_sem=self.sems.at[len(self.copies)],
            recv_sem=recv,
            device_id=to,
            device_id_type=MESH,
        )
        copy.start()
        self.copies.append(copy)

    def arrived(self, ref, recv, to):
        pltpu.make_async_remote_copy(
            src_ref=ref,
            dst_ref=ref,
            send_sem=self.sems.at[0],
            recv_sem=recv,
            device_id=to,
            device_id_type=MESH,
        ).wait_recv()

    def finish(self):
        for copy in self.copies:
            copy.wait_send()


SPREAD_SENDS = 69


def spread(own, full, send, piece_sems, pair_sems, local_sem, work=iter(()), ready=lambda region: None):
    x, zh, zl, y, c = place()
    k, kz = zl * 4 + y, (1 - zl) * 4 + y
    near_k, near_kz = ([b * 4 + (y + s) % 4 for s in (1, 3, 2)] for b in (zl, 1 - zl))
    to_sib = device(x, zh, zl, y, 1 - c)
    to_z = device(x, zh, 1 - zl, y, c)
    to_y = [device(x, zh, zl, (y + s) % 4, c) for s in (1, 3)]
    to_x = [device((x + s) % 4, zh, zl, y, c) for s in (1, 3)]
    quarters = [x, (x + 1) % 4, (x + 3) % 4, (x + 2) % 4]
    starts = {"a": 0, "b": N1} | {w: NP + quarters[w] * NQ for w in range(4)}
    sizes = {"a": N1, "b": N2} | {w: NQ for w in range(4)}
    index = {"a": 0, "b": 1} | {w: 2 + quarters[w] for w in range(4)}

    def cols(t, half):
        lo, size = starts[t], sizes[t]
        if half is not None:
            size = size // 2
            lo = lo + half * size
        if not isinstance(lo, int):
            lo = pl.multiple_of(lo, 128)
        return pl.ds(lo, size)

    def push(kk, t, to, half=None):
        at = cols(t, half)
        src = own.at[:, at] if kk is k else full.at[2 * kk + c, :, at]
        send(src, full.at[2 * kk + c, :, at], piece_sems.at[half or 0, index[t], kk], to)

    def here(kk, t, half=None):
        next(work, None)
        send.arrived(full.at[2 * kk + c, :, cols(t, half)], piece_sems.at[half or 0, index[t], kk], to_sib)

    def pair(kk, lo, size, slot):
        ref = full.at[2 * kk + c, :, pl.ds(lo, size)]
        send(ref, ref, pair_sems.at[kk, slot], to_sib)

    def ring(kk, t, links, side):
        push(kk, t, links[1 - side], side)

    def both(kk, t, links):
        for to in links:
            push(kk, t, to)

    ready("q")
    push(k, 0, to_z)
    both(k, 0, to_y)
    ready("a")
    push(k, "a", to_z)
    ready("b")
    both(k, "b", to_y)
    push(k, "b", to_z)
    both(k, "a", to_y)
    keep = pltpu.make_async_copy(own, full.at[2 * k + c], local_sem)
    keep.start()
    send(own, full.at[2 * k + c], pair_sems.at[k, 0], to_sib)

    here(kz, 0)
    both(kz, 0, to_y)
    both(kz, 0, to_x)
    for side in range(2):
        kk = near_k[side]
        here(kk, 0)
        ring(kk, 0, to_y, side)
        both(kk, 0, to_x)
    here(kz, "a")
    both(kz, "a", to_y)
    for side in range(2):
        kk = near_k[side]
        here(kk, "b")
        push(kk, "b", to_z)
        ring(kk, "b", to_y, side)
    for side in range(2):
        kk = near_kz[side]
        here(kk, 0)
        ring(kk, 0, to_y, side)
        both(kk, 0, to_x)
    here(near_k[2], 0, 0)
    here(near_k[2], 0, 1)
    both(near_k[2], 0, to_x)
    for side in range(2):
        kk = near_k[side]
        here(kk, "a")
        ring(kk, "a", to_y, side)
        pair(kk, 0, NP, 0)
    here(near_k[2], "b", 0)
    here(near_k[2], "b", 1)
    push(near_k[2], "b", to_z)
    here(near_kz[2], 0, 0)
    here(near_kz[2], 0, 1)
    both(near_kz[2], 0, to_x)
    for side in range(2):
        here(near_kz[side], "a")
        ring(near_kz[side], "a", to_y, side)
    others = [kz, near_k[0], near_k[1], near_kz[0], near_kz[1], near_k[2], near_kz[2]]
    for kk in others[:5]:
        for side in range(2):
            here(kk, 1 + side)
            ring(kk, 1 + side, to_x, side)
    here(kz, "b")
    pair(kz, 0, NP, 0)
    for kk in others[5:]:
        for side in range(2):
            here(kk, 1 + side)
            ring(kk, 1 + side, to_x, side)
    here(near_k[2], "a", 0)
    here(near_k[2], "a", 1)
    pair(near_k[2], 0, NP, 0)
    for side in range(2):
        here(near_kz[side], "b")
        pair(near_kz[side], 0, NP, 0)
    for kk in others[:5]:
        here(kk, 3, 0)
        here(kk, 3, 1)
        pair(kk, NP, 4 * NQ, 1)
    here(near_kz[2], "a", 0)
    here(near_kz[2], "a", 1)
    here(near_kz[2], "b")
    pair(near_kz[2], 0, NP, 0)
    for kk in others[5:]:
        here(kk, 3, 0)
        here(kk, 3, 1)
        pair(kk, NP, 4 * NQ, 1)
    for _ in work:
        pass
    send.arrived(full.at[2 * k + 1 - c], pair_sems.at[k, 0], to_sib)
    for kk in others:
        send.arrived(full.at[2 * kk + 1 - c, :, pl.ds(0, NP)], pair_sems.at[kk, 0], to_sib)
        send.arrived(full.at[2 * kk + 1 - c, :, pl.ds(NP, 4 * NQ)], pair_sems.at[kk, 1], to_sib)
    keep.wait()


def greet(devices):
    barrier = pltpu.get_barrier_semaphore()
    for to in devices:
        pl.semaphore_signal(barrier, inc=1, device_id=to, device_id_type=MESH)


def met(devices):
    pl.semaphore_wait(pltpu.get_barrier_semaphore(), len(devices))


def stacked(rows):
    half = rows.shape[1] // 2
    return jnp.concatenate([rows[:, :half], rows[:, half:]], axis=0)


def unstacked(rows):
    return jnp.concatenate([rows[:8], rows[8:]], axis=1)


def tables(length, width):
    half = width // 2
    positions = np.arange(length, dtype=np.float32)[:, None]
    freqs = np.power(np.float32(10000.0), -(np.float32(2.0) * np.arange(half, dtype=np.float32) / np.float32(width)))
    angle = positions * freqs[None, :].astype(np.float32)
    cosine, sine = np.cos(angle), np.sin(angle)
    return (
        jnp.asarray(np.concatenate([cosine, cosine], axis=1)),
        jnp.asarray(np.concatenate([-sine, sine], axis=1)),
    )


BLOCK = 256
STEPS = 4


def turn(values, cosine, sine):
    return values * cosine + pltpu.roll(values, 64, 1) * sine


def document_starts(doc_ids, starts):
    ids = doc_ids[...]
    first = jnp.zeros_like(ids)
    for n in range(3):
        first += jnp.where(ids > n, jnp.sum((ids == n).astype(jnp.int32)), 0)
    starts[...] = first


def start_of(starts, i):
    return jnp.concatenate([starts[2 * i : 2 * i + 1, :], starts[2 * i + 1 : 2 * i + 2, :]], axis=1)


def scored(keys, queries, first_key, start_row, query_row):
    raw = lax.dot_general(keys, queries, (((1,), (1,)), ((), ())), preferred_element_type=jnp.float32)
    soft = jnp.tanh(raw * (query_scale / softcap))
    row = lax.broadcasted_iota(jnp.int32, raw.shape, 0) + first_key
    allowed = (row >= start_row) & (row <= query_row)
    return soft, jnp.where(allowed, jnp.exp(softcap * soft), 0.0)


def as_row(gain):
    return jnp.concatenate([gain[n : n + 1, :] for n in range(WIDTH // 128)], axis=1)


PARTS = 8
PART = WIDTH // PARTS


def weight_parts(weight, wide, rough, mixed, in_sems):
    def load(n):
        return pltpu.make_async_copy(weight.at[pl.ds(4 * PART * n, 4 * PART), :], rough.at[n % 2], in_sems.at[n])

    load(0).start()
    for n in range(PARTS):
        if n + 1 < PARTS:
            load(n + 1).start()
        yield
        load(n).wait()
        mixed[...] = rough[n % 2].astype(jnp.float32)
        for j in range(4):
            wide[pl.ds(PART * n, PART), j * 128 : j * 128 + 128] = mixed[pl.ds(j, PART, stride=4), :].astype(jnp.bfloat16)


KEPT = (0, 256, 768, 1536, 2304)


def front_kernel(
    tokens, pre_gain, post_gain, qkv_hbm, weight_hbm, doc_ids, cotangent, delta, cosine, sine,
    output, gathered, delta_sum, grad_proj_t, grad_out,
    query_ref, key_ref, value_ref, heads_ref, full, probs, slopes, keys_t, dkey, dvalue, grad_proj, out_grad, weight_t,
    everything, own, own_grad, wide, rough, mixed, own_part, parts_in, summed, other, delta_part, starts, values_t,
    weight, partial, received, mate, total, group_q, group_a, group_b, out_in,
    send_sems, piece_sems, pair_sems, local_sems, in_sems, delta_sems,
    mate_sems, part_sems, group_sems, out_sems, sum_sems,
):
    x, zh, zl, y, c = place()
    k, g = zl * 4 + y, x * 2 + zh
    sib = device(x, zh, zl, y, 1 - c)
    chips = [(a, b) for a in range(2) for b in range(4)][1:]
    fellows = [((zl + a) % 2, (y + b) % 4) for a, b in chips]
    to_fellows = [device(x, zh, a, b, c) for a, b in fellows]
    kin = [((x + b) % 4, (zh + a) % 2) for a, b in chips]
    to_kin = [device(a, b, zl, y, c) for a, b in kin]
    to_x = [device((x + step) % 4, zh, zl, y, c) for step in (1, 2, 3)]
    to_zh = device(x, 1 - zh, zl, y, c)
    group_in = {"q": group_q, "a": group_a, "b": group_b}
    greet([sib] + to_fellows + to_kin)
    send = Sender(send_sems)
    rows_of = lambda n: pl.ds(pl.multiple_of(n % 4 * 32, 32), 32)
    load_part = pltpu.make_async_copy(delta.at[rows_of(x), :], own_part, delta_sems.at[4])
    load_part.start()

    def background():
        for _ in weight_parts(qkv_hbm, wide, rough, mixed, in_sems):
            yield
        load_weight.start()

    load_weight = pltpu.make_async_copy(weight_hbm, weight, local_sems.at[1])
    work = background()
    next(work)
    values = tokens[...].astype(jnp.float32)
    scale = lax.rsqrt(jnp.mean(values * values, axis=-1, keepdims=True) + 1e-06)
    own[...] = (values * scale * as_row(pre_gain)).astype(jnp.bfloat16)
    document_starts(doc_ids, starts)
    met([sib] + to_fellows + to_kin)
    for n, step in enumerate((1, 2, 3)):
        send(delta.at[rows_of(x + step), :], parts_in.at[n], delta_sems.at[n], to_x[n])
    spread(own, everything, send, piece_sems.at[0], pair_sems.at[0], local_sems.at[0], work)
    store = pltpu.make_async_copy(everything, gathered, local_sems.at[3])
    store.start()

    for i in range(STEPS):
        at = pl.ds(i * BLOCK, BLOCK)
        rows = everything[pl.ds(4 * i, 4)].reshape(BLOCK, WIDTH)
        proj = jnp.dot(rows, wide[...], preferred_element_type=jnp.float32)
        queries = [turn(proj[:, h * 128 : h * 128 + 128], cosine[at, :], sine[at, :]).astype(jnp.bfloat16) for h in range(2)]
        query_ref[i] = jnp.concatenate(queries, axis=0)
        key_ref[at, :] = turn(proj[:, 256:384], cosine[at, :], sine[at, :]).astype(jnp.bfloat16)
        value_ref[at, :] = proj[:, 384:].astype(jnp.bfloat16)
        keys_t[:, at] = key_ref[at, :].astype(jnp.float32).T.astype(jnp.bfloat16)
        values_t[:, at] = proj[:, 384:].T.astype(jnp.bfloat16)
        start_row = jnp.concatenate([start_of(starts, i)] * 2, axis=1)
        query_row = lax.broadcasted_iota(jnp.int32, (1, 2 * BLOCK), 1) % BLOCK + i * BLOCK
        first = max(0, i - 2) * BLOCK
        keys_at = slice(first, i * BLOCK + BLOCK)
        soft, e = scored(key_ref[keys_at, :], query_ref[i], first, start_row, query_row)
        p = e * (1.0 / jnp.sum(e, axis=0, keepdims=True))
        kept = slice(KEPT[i], KEPT[i + 1])
        probs[kept, :] = p
        slopes[kept, :] = p * ((1.0 - soft * soft) * query_scale)
        acc = jnp.dot(values_t[:, keys_at], p.astype(jnp.bfloat16), preferred_element_type=jnp.float32)
        for h in range(2):
            part = acc[:, h * BLOCK : h * BLOCK + BLOCK].T.reshape(4, ROWS, 128)
            heads_ref[pl.ds(4 * i, 4), :, h * 128 : h * 128 + 128] = part
        if i == 0:
            load_part.wait()
            delta_total = own_part[...].astype(jnp.float32)
            for n in range(3):
                send.arrived(parts_in.at[n], delta_sems.at[n], sib)
                delta_total = delta_total + parts_in[n].astype(jnp.float32)
            summed[...] = delta_total.astype(jnp.bfloat16)
            send(summed, other, delta_sems.at[3], to_zh)

    share = heads_ref[:, pl.ds(pl.multiple_of(g * 8, 8), 8), :]
    load_weight.wait()
    for core in range(2):
        rows = jnp.concatenate([share[2 * kk + core] for kk in range(8)], axis=0).astype(jnp.bfloat16)
        left = jnp.dot(rows, weight[:, :HALF], preferred_element_type=jnp.float32)
        right = jnp.dot(rows, weight[:, HALF:], preferred_element_type=jnp.float32)
        for kk in range(8):
            both = jnp.concatenate([left[kk * 8 : kk * 8 + 8], right[kk * 8 : kk * 8 + 8]], axis=0)
            partial[core, kk] = both.astype(jnp.bfloat16)
    for n, (a, b) in enumerate(fellows):
        kk = a * 4 + b
        send(partial.at[1 - c, kk], mate.at[kk], mate_sems.at[kk], sib)
    send(partial.at[1 - c, k], mate.at[k], mate_sems.at[k], sib)
    for (a, b), to in zip(fellows, to_fellows):
        kk = a * 4 + b
        send.arrived(mate.at[kk], mate_sems.at[kk], sib)
        total[kk] = (partial[c, kk].astype(jnp.float32) + mate[kk].astype(jnp.float32)).astype(jnp.bfloat16)
        send(total.at[kk], received.at[k], part_sems.at[k], to)
    send.arrived(mate.at[k], mate_sems.at[k], sib)
    both = partial[c, k].astype(jnp.float32) + mate[k].astype(jnp.float32)
    send.arrived(other, delta_sems.at[3], sib)
    delta_part[...] = (summed[...].astype(jnp.float32) + other[...].astype(jnp.float32)).astype(jnp.bfloat16)
    keep = pltpu.make_async_copy(delta_part, delta_sum.at[x], local_sems.at[2])
    keep.start()
    for to in (to_x[0], to_x[2]):
        send(delta_part, delta_sum.at[x], sum_sems.at[0, x], to)
    gain_row = as_row(post_gain)
    pick = lambda rows: jnp.where(g % 2 == 0, rows[:8], rows[8:])
    near_rows = pl.ds(pl.multiple_of(g // 2 * 16, 16), 16)
    own_tokens = pick(tokens[near_rows, :].astype(jnp.float32))
    dnorm = pick(cotangent[near_rows, :].astype(jnp.float32)) * gain_row
    for a, b in fellows:
        kk = a * 4 + b
        send.arrived(received.at[kk], part_sems.at[kk], sib)
        both = both + received[kk].astype(jnp.float32)
    attn = unstacked(both)
    scale = lax.rsqrt(jnp.mean(attn * attn, axis=-1, keepdims=True) + 1e-06)
    normal = attn * scale
    grad = scale * (dnorm - normal * jnp.mean(dnorm * normal, axis=-1, keepdims=True))
    for t, (region, (lo, size)) in enumerate(REGIONS.items()):
        into = group_in[region]
        into[g] = stacked(grad[:, lo : lo + size]).astype(jnp.bfloat16)
        for to in to_kin:
            send(into.at[g], into.at[g], group_sems.at[t, g], to)
    out_in[zh, x] = stacked(own_tokens + normal * gain_row).astype(jnp.bfloat16)
    for side, step in enumerate((1, 3)):
        n = (x + step) % 4
        send.arrived(delta_sum.at[n], sum_sems.at[0, n], sib)
        half = delta_sum.at[n, pl.ds(side * 16, 16), :]
        send(half, half, sum_sems.at[1 + side, n], to_x[2 - 2 * side])

    def ready(region):
        t, (lo, size) = list(REGIONS).index(region), REGIONS[region]
        into = group_in[region]
        for a, b in kin:
            gg = a * 2 + b
            send.arrived(into.at[gg], group_sems.at[t, gg], sib)
        for gg in range(0, 8, 2):
            first = unstacked(into[gg].astype(jnp.float32))
            second = unstacked(into[gg + 1].astype(jnp.float32))
            own_grad[pl.ds(gg * 8, 16), pl.ds(lo, size)] = jnp.concatenate([first, second], axis=0).astype(jnp.bfloat16)

    def returning():
        for lo in range(0, WIDTH, 768):
            weight_t[lo : lo + 768, :] = weight[:, lo : lo + 768].astype(jnp.float32).T.astype(jnp.bfloat16)
            yield
        for _ in range(3):
            yield
        for to in to_x:
            send(out_in.at[zh, x], out_in.at[zh, x], out_sems.at[x], to)
        for _ in range(12):
            yield
        for step in (1, 2, 3):
            there = out_in.at[zh, (x + step) % 4]
            send.arrived(there, out_sems.at[(x + step) % 4], sib)
        send(out_in.at[zh], out_in.at[zh], out_sems.at[4], to_zh)

    spread(own_grad, full, send, piece_sems.at[1], pair_sems.at[1], local_sems.at[0], returning(), ready)

    heads_t = heads_ref[...].reshape(16 * ROWS, 256).T.astype(jnp.bfloat16)
    for lo in range(0, WIDTH, 768):
        columns = full[:, :, lo : lo + 768].reshape(16 * ROWS, 768)
        out_grad[:, lo : lo + 768] = jnp.dot(heads_t, columns, preferred_element_type=jnp.float32).astype(jnp.bfloat16)
    store_out = pltpu.make_async_copy(out_grad, grad_out, local_sems.at[0])
    store_out.start()
    dkey[...] = jnp.zeros_like(dkey)
    dvalue[...] = jnp.zeros_like(dvalue)
    for i in range(STEPS):
        at = slice(i * BLOCK, i * BLOCK + BLOCK)
        keys_at = slice(max(0, i - 2) * BLOCK, i * BLOCK + BLOCK)
        kept = slice(KEPT[i], KEPT[i + 1])
        rows = full[pl.ds(4 * i, 4)].reshape(BLOCK, WIDTH)
        grad_heads = jnp.dot(rows, weight_t[...], preferred_element_type=jnp.float32).astype(jnp.bfloat16)
        grad = jnp.concatenate([grad_heads[:, :128], grad_heads[:, 128:]], axis=0)
        p = probs[kept, :]
        dp = lax.dot_general(value_ref[keys_at, :], grad, (((1,), (1,)), ((), ())), preferred_element_type=jnp.float32)
        dvalue[keys_at, :] += jnp.dot(p.astype(jnp.bfloat16), grad, preferred_element_type=jnp.float32)
        ds = (slopes[kept, :] * (dp - jnp.sum(p * dp, axis=0, keepdims=True))).astype(jnp.bfloat16)
        dkey[keys_at, :] += jnp.dot(ds, query_ref[i], preferred_element_type=jnp.float32)
        acc = jnp.dot(keys_t[:, keys_at], ds, preferred_element_type=jnp.float32)
        for h in range(2):
            turned_back = turn(acc[:, h * BLOCK : h * BLOCK + BLOCK].T, cosine[at, :], -sine[at, :])
            grad_proj[at, h * 128 : h * 128 + 128] = turned_back
    grad_proj[:, 256:384] = turn(dkey[...], cosine[...], -sine[...])
    grad_proj[:, 384:512] = dvalue[...]
    grad_proj_t[...] = grad_proj[...].T.astype(jnp.bfloat16)

    send.arrived(out_in.at[1 - zh], out_sems.at[4], sib)
    for gg in range(0, 8, 2):
        first = unstacked(out_in[0, gg // 2].astype(jnp.float32))
        second = unstacked(out_in[1, gg // 2].astype(jnp.float32))
        output[pl.ds(gg * 8, 16), :] = jnp.concatenate([first, second], axis=0).astype(jnp.bfloat16)
    n = (x + 2) % 4
    for side in range(2):
        send.arrived(delta_sum.at[n, pl.ds(side * 16, 16), :], sum_sems.at[1 + side, n], sib)
    keep.wait()
    store.wait()
    store_out.wait()
    send.finish()


def front(tokens, pre_gain, post_gain, qkv_weight, weight, doc_ids, cotangent, delta, cosine, sine):
    vmem = pl.BlockSpec(memory_space=pltpu.VMEM)
    hbm = pl.BlockSpec(memory_space=pl.ANY)
    shape = jax.ShapeDtypeStruct
    bf16, f32 = jnp.bfloat16, jnp.float32
    return pl.pallas_call(
        front_kernel,
        out_shape=(
            shape((ROWS, WIDTH), bf16),
            shape((16, ROWS, WIDTH), bf16),
            shape((4, 32, WIDTH), bf16),
            shape((512, 1024), bf16),
            shape((256, WIDTH), bf16),
        ),
        in_specs=[vmem, vmem, vmem, hbm, hbm, vmem, vmem, hbm, vmem, vmem],
        out_specs=(vmem, hbm, hbm, vmem, hbm),
        scratch_shapes=[
            pltpu.VMEM((STEPS, 2 * BLOCK, 128), bf16),
            pltpu.VMEM((1024, 128), bf16),
            pltpu.VMEM((1024, 128), bf16),
            pltpu.VMEM((16, ROWS, 256), f32),
            pltpu.VMEM((16, ROWS, WIDTH), bf16),
            pltpu.VMEM((KEPT[-1], 2 * BLOCK), f32),
            pltpu.VMEM((KEPT[-1], 2 * BLOCK), f32),
            pltpu.VMEM((128, 1024), bf16),
            pltpu.VMEM((1024, 128), f32),
            pltpu.VMEM((1024, 128), f32),
            pltpu.VMEM((1024, 512), f32),
            pltpu.VMEM((256, WIDTH), bf16),
            pltpu.VMEM((WIDTH, 256), bf16),
            pltpu.VMEM((16, ROWS, WIDTH), bf16),
            pltpu.VMEM((ROWS, WIDTH), bf16),
            pltpu.VMEM((ROWS, WIDTH), bf16),
            pltpu.VMEM((WIDTH, 512), bf16),
            pltpu.VMEM((2, 4 * PART, 128), bf16),
            pltpu.VMEM((4 * PART, 128), f32),
            pltpu.VMEM((32, WIDTH), bf16),
            pltpu.VMEM((3, 32, WIDTH), bf16),
            pltpu.VMEM((32, WIDTH), bf16),
            pltpu.VMEM((32, WIDTH), bf16),
            pltpu.VMEM((32, WIDTH), bf16),
            pltpu.VMEM((8, 128), jnp.int32),
            pltpu.VMEM((128, 1024), bf16),
            pltpu.VMEM((256, WIDTH), bf16),
            pltpu.VMEM((2, 8, 16, HALF), bf16),
            pltpu.VMEM((8, 16, HALF), bf16),
            pltpu.VMEM((8, 16, HALF), bf16),
            pltpu.VMEM((8, 16, HALF), bf16),
            pltpu.VMEM((8, 16, 2 * NQ), bf16),
            pltpu.VMEM((8, 16, N1 // 2), bf16),
            pltpu.VMEM((8, 16, N2 // 2), bf16),
            pltpu.VMEM((2, 4, 16, HALF), bf16),
            pltpu.SemaphoreType.DMA((4 + 8 + 2 + 7 + 21 + 2 + 4 + 2 * SPREAD_SENDS,)),
            pltpu.SemaphoreType.DMA((2, 2, 6, 8)),
            pltpu.SemaphoreType.DMA((2, 8, 2)),
            pltpu.SemaphoreType.DMA((4,)),
            pltpu.SemaphoreType.DMA((PARTS,)),
            pltpu.SemaphoreType.DMA((5,)),
            pltpu.SemaphoreType.DMA((8,)),
            pltpu.SemaphoreType.DMA((8,)),
            pltpu.SemaphoreType.DMA((3, 8)),
            pltpu.SemaphoreType.DMA((5,)),
            pltpu.SemaphoreType.DMA((3, 4)),
        ],
        compiler_params=pltpu.CompilerParams(
            collective_id=0, has_side_effects=True, vmem_limit_bytes=60 * 2**20
        ),
        name="front",
    )(tokens, pre_gain, post_gain, qkv_weight, weight, doc_ids, cotangent, delta, cosine, sine)


CHUNK = 768
CHUNKS = WIDTH // CHUNK


def finish_kernel(
    x_hbm, turned, delta, momentum, fragment, output, grad_out, qkv_out, new_momentum, new_fragment, new_output, out_out,
    x, mixed, sems,
):
    i = pl.program_id(0)

    def load(n):
        rows = pl.ds(n * BLOCK, BLOCK)
        return pltpu.make_async_copy(x_hbm.at[rows, :], x.at[rows, :], sems.at[n])

    @pl.when(i == 0)
    def _():
        for n in range(STEPS):
            load(n).start()

    mean_delta = delta[...].astype(jnp.float32) / 8.0
    moment = 0.9 * momentum[...] + mean_delta
    new_momentum[...] = moment
    new_fragment[...] = fragment[...] - 0.7 * (mean_delta + 0.9 * moment)
    new_output[...] = output[...]
    out_out[...] = grad_out[...]

    @pl.when(i == 0)
    def _():
        for n in range(STEPS):
            load(n).wait()

    at = pl.ds(pl.multiple_of(i * CHUNK, CHUNK), CHUNK)
    part = jnp.dot(turned[...], x[:, at], preferred_element_type=jnp.float32)
    for j in range(4):
        mixed[pl.ds(j, CHUNK, stride=4), :] = part[j * 128 : j * 128 + 128].T
    qkv_out[...] = mixed[...].astype(jnp.bfloat16)


def finish(gathered, turned, delta, momentum, fragment, output, grad_out):
    columns = lambda n: pl.BlockSpec((n, CHUNK), lambda i: (0, i))
    return pl.pallas_call(
        finish_kernel,
        grid=(CHUNKS,),
        in_specs=[
            pl.BlockSpec(memory_space=pl.ANY),
            pl.BlockSpec((512, 1024), lambda i: (0, 0)),
            columns(128),
            columns(128),
            columns(128),
            columns(ROWS),
            columns(256),
        ],
        out_specs=[
            pl.BlockSpec((4 * CHUNK, 128), lambda i: (i, 0)),
            columns(128),
            columns(128),
            columns(ROWS),
            columns(256),
        ],
        scratch_shapes=[
            pltpu.VMEM((1024, WIDTH), jnp.bfloat16),
            pltpu.VMEM((4 * CHUNK, 128), jnp.float32),
            pltpu.SemaphoreType.DMA((STEPS,)),
        ],
        out_shape=[
            jax.ShapeDtypeStruct((4 * WIDTH, 128), jnp.bfloat16),
            jax.ShapeDtypeStruct((128, WIDTH), jnp.float32),
            jax.ShapeDtypeStruct((128, WIDTH), jnp.float32),
            jax.ShapeDtypeStruct((ROWS, WIDTH), jnp.bfloat16),
            jax.ShapeDtypeStruct((256, WIDTH), jnp.bfloat16),
        ],
        compiler_params=pltpu.CompilerParams(vmem_limit_bytes=60 * 2**20),
        name="finish",
    )(gathered, turned, delta, momentum, fragment, output, grad_out)


def local(
    tokens,
    pre_gain,
    post_gain,
    qkv_weight,
    out_weight,
    doc_ids,
    cotangent,
    outer_delta,
    momentum,
    fragment,
):
    cosine, sine = tables(16 * ROWS, 128)
    doc_ids = doc_ids.reshape(8, 128)
    out_flat = out_weight.reshape(256, WIDTH)
    output, gathered, delta, turned, grad_out = front(
        tokens, pre_gain.reshape(36, 128), post_gain.reshape(36, 128), qkv_weight.reshape(4 * WIDTH, 128), out_flat,
        doc_ids, cotangent, outer_delta[0], cosine, sine,
    )
    grad_qkv, new_momentum, new_fragment, output, grad_out = finish(
        gathered.reshape(16 * ROWS, WIDTH), turned, delta.reshape(128, WIDTH), momentum, fragment, output, grad_out
    )
    return (output, grad_qkv.reshape(qkv_weight.shape), grad_out.reshape(out_weight.shape), new_momentum, new_fragment)


def solution(mesh):
    placed = (
        P("fsdp", None),
        P(),
        P(),
        P(None, "fsdp", None, None),
        P("fsdp", None, None, None),
        P(),
        P("fsdp", None),
        P("group", "fsdp", None),
        P("fsdp", None),
        P("fsdp", None),
    )
    return jax.shard_map(
        local,
        mesh=mesh,
        in_specs=placed,
        out_specs=(
            P("fsdp", None),
            P(None, "fsdp", None, None),
            P("fsdp", None, None, None),
            P("fsdp", None),
            P("fsdp", None),
        ),
        check_vma=False,
    )
```

```python
import functools

import jax
import jax.numpy as jnp
import numpy as np
from jax import lax
from jax.experimental import pallas as pl
from jax.experimental.pallas import tpu as pltpu
from jax.sharding import PartitionSpec as P

softcap = 50.0
query_scale = 1.0 / 12.0
MESH = pl.DeviceIdType.MESH
WIDTH = 4608
HALF = WIDTH // 2
ROWS = 64
N1, N2, NQ = 10 * 128, 10 * 128, 4 * 128
NP = N1 + N2
REGIONS = {"q": (NP, 4 * NQ), "a": (0, N1), "b": (N1, N2)}


def place():
    group, fsdp = lax.axis_index("group"), lax.axis_index("fsdp")
    return group // 2, group % 2, fsdp // 8, (fsdp // 2) % 4, fsdp % 2


def device(x, zh, zl, y, c):
    return (x * 2 + zh, (zl * 4 + y) * 2 + c)


class Sender:
    def __init__(self, sems):
        self.sems, self.copies = sems, []

    def __call__(self, src, dst, recv, to):
        copy = pltpu.make_async_remote_copy(
            src_ref=src,
            dst_ref=dst,
            send_sem=self.sems.at[len(self.copies)],
            recv_sem=recv,
            device_id=to,
            device_id_type=MESH,
        )
        copy.start()
        self.copies.append(copy)

    def arrived(self, ref, recv, to):
        pltpu.make_async_remote_copy(
            src_ref=ref,
            dst_ref=ref,
            send_sem=self.sems.at[0],
            recv_sem=recv,
            device_id=to,
            device_id_type=MESH,
        ).wait_recv()

    def finish(self):
        for copy in self.copies:
            copy.wait_send()


SPREAD_SENDS = 69


def spread(own, full, send, piece_sems, pair_sems, local_sem, work=iter(()), ready=lambda region: None):
    x, zh, zl, y, c = place()
    k, kz = zl * 4 + y, (1 - zl) * 4 + y
    near_k, near_kz = ([b * 4 + (y + s) % 4 for s in (1, 3, 2)] for b in (zl, 1 - zl))
    to_sib = device(x, zh, zl, y, 1 - c)
    to_z = device(x, zh, 1 - zl, y, c)
    to_y = [device(x, zh, zl, (y + s) % 4, c) for s in (1, 3)]
    to_x = [device((x + s) % 4, zh, zl, y, c) for s in (1, 3)]
    quarters = [x, (x + 1) % 4, (x + 3) % 4, (x + 2) % 4]
    starts = {"a": 0, "b": N1} | {w: NP + quarters[w] * NQ for w in range(4)}
    sizes = {"a": N1, "b": N2} | {w: NQ for w in range(4)}
    index = {"a": 0, "b": 1} | {w: 2 + quarters[w] for w in range(4)}

    def cols(t, half):
        lo, size = starts[t], sizes[t]
        if half is not None:
            size = size // 2
            lo = lo + half * size
        if not isinstance(lo, int):
            lo = pl.multiple_of(lo, 128)
        return pl.ds(lo, size)

    def push(kk, t, to, half=None):
        at = cols(t, half)
        src = own.at[:, at] if kk is k else full.at[2 * kk + c, :, at]
        send(src, full.at[2 * kk + c, :, at], piece_sems.at[half or 0, index[t], kk], to)

    def here(kk, t, half=None):
        next(work, None)
        send.arrived(full.at[2 * kk + c, :, cols(t, half)], piece_sems.at[half or 0, index[t], kk], to_sib)

    def pair(kk, lo, size, slot):
        ref = full.at[2 * kk + c, :, pl.ds(lo, size)]
        send(ref, ref, pair_sems.at[kk, slot], to_sib)

    def ring(kk, t, links, side):
        push(kk, t, links[1 - side], side)

    def both(kk, t, links):
        for to in links:
            push(kk, t, to)

    ready("q")
    push(k, 0, to_z)
    both(k, 0, to_y)
    ready("a")
    push(k, "a", to_z)
    ready("b")
    both(k, "b", to_y)
    push(k, "b", to_z)
    both(k, "a", to_y)
    keep = pltpu.make_async_copy(own, full.at[2 * k + c], local_sem)
    keep.start()
    send(own, full.at[2 * k + c], pair_sems.at[k, 0], to_sib)

    here(kz, 0)
    both(kz, 0, to_y)
    both(kz, 0, to_x)
    for side in range(2):
        kk = near_k[side]
        here(kk, 0)
        ring(kk, 0, to_y, side)
        both(kk, 0, to_x)
    here(kz, "a")
    both(kz, "a", to_y)
    for side in range(2):
        kk = near_k[side]
        here(kk, "b")
        push(kk, "b", to_z)
        ring(kk, "b", to_y, side)
    for side in range(2):
        kk = near_kz[side]
        here(kk, 0)
        ring(kk, 0, to_y, side)
        both(kk, 0, to_x)
    here(near_k[2], 0, 0)
    here(near_k[2], 0, 1)
    both(near_k[2], 0, to_x)
    for side in range(2):
        kk = near_k[side]
        here(kk, "a")
        ring(kk, "a", to_y, side)
        pair(kk, 0, NP, 0)
    here(near_k[2], "b", 0)
    here(near_k[2], "b", 1)
    push(near_k[2], "b", to_z)
    here(near_kz[2], 0, 0)
    here(near_kz[2], 0, 1)
    both(near_kz[2], 0, to_x)
    for side in range(2):
        here(near_kz[side], "a")
        ring(near_kz[side], "a", to_y, side)
    others = [kz, near_k[0], near_k[1], near_kz[0], near_kz[1], near_k[2], near_kz[2]]
    for kk in others[:5]:
        for side in range(2):
            here(kk, 1 + side)
            ring(kk, 1 + side, to_x, side)
    here(kz, "b")
    pair(kz, 0, NP, 0)
    for kk in others[5:]:
        for side in range(2):
            here(kk, 1 + side)
            ring(kk, 1 + side, to_x, side)
    here(near_k[2], "a", 0)
    here(near_k[2], "a", 1)
    pair(near_k[2], 0, NP, 0)
    for side in range(2):
        here(near_kz[side], "b")
        pair(near_kz[side], 0, NP, 0)
    for kk in others[:5]:
        here(kk, 3, 0)
        here(kk, 3, 1)
        pair(kk, NP, 4 * NQ, 1)
    here(near_kz[2], "a", 0)
    here(near_kz[2], "a", 1)
    here(near_kz[2], "b")
    pair(near_kz[2], 0, NP, 0)
    for kk in others[5:]:
        here(kk, 3, 0)
        here(kk, 3, 1)
        pair(kk, NP, 4 * NQ, 1)
    for _ in work:
        pass
    send.arrived(full.at[2 * k + 1 - c], pair_sems.at[k, 0], to_sib)
    for kk in others:
        send.arrived(full.at[2 * kk + 1 - c, :, pl.ds(0, NP)], pair_sems.at[kk, 0], to_sib)
        send.arrived(full.at[2 * kk + 1 - c, :, pl.ds(NP, 4 * NQ)], pair_sems.at[kk, 1], to_sib)
    keep.wait()


def greet(devices):
    barrier = pltpu.get_barrier_semaphore()
    for to in devices:
        pl.semaphore_signal(barrier, inc=1, device_id=to, device_id_type=MESH)


def met(devices):
    pl.semaphore_wait(pltpu.get_barrier_semaphore(), len(devices))


def stacked(rows):
    half = rows.shape[1] // 2
    return jnp.concatenate([rows[:, :half], rows[:, half:]], axis=0)


def unstacked(rows):
    return jnp.concatenate([rows[:8], rows[8:]], axis=1)


def tables(length, width):
    half = width // 2
    positions = np.arange(length, dtype=np.float32)[:, None]
    freqs = np.power(np.float32(10000.0), -(np.float32(2.0) * np.arange(half, dtype=np.float32) / np.float32(width)))
    angle = positions * freqs[None, :].astype(np.float32)
    cosine, sine = np.cos(angle), np.sin(angle)
    return (
        jnp.asarray(np.concatenate([cosine, cosine], axis=1)),
        jnp.asarray(np.concatenate([-sine, sine], axis=1)),
    )


BLOCK = 256
STEPS = 4


def turn(values, cosine, sine):
    return values * cosine + pltpu.roll(values, 64, 1) * sine


def document_starts(doc_ids, starts):
    ids = doc_ids[...]
    first = jnp.zeros_like(ids)
    for n in range(3):
        first += jnp.where(ids > n, jnp.sum((ids == n).astype(jnp.int32)), 0)
    starts[...] = first


def start_of(starts, i):
    return jnp.concatenate([starts[2 * i : 2 * i + 1, :], starts[2 * i + 1 : 2 * i + 2, :]], axis=1)


def scored(keys, queries, first_key, start_row, query_row):
    raw = lax.dot_general(keys, queries, (((1,), (1,)), ((), ())), preferred_element_type=jnp.float32)
    soft = jnp.tanh(raw * (query_scale / softcap))
    row = lax.broadcasted_iota(jnp.int32, raw.shape, 0) + first_key
    allowed = (row >= start_row) & (row <= query_row)
    return soft, jnp.where(allowed, jnp.exp(softcap * soft), 0.0)


def as_row(gain):
    return jnp.concatenate([gain[n : n + 1, :] for n in range(WIDTH // 128)], axis=1)


PARTS = 8
PART = WIDTH // PARTS


def weight_parts(weight, wide, rough, mixed, in_sems):
    def load(n):
        return pltpu.make_async_copy(weight.at[pl.ds(4 * PART * n, 4 * PART), :], rough.at[n % 2], in_sems.at[n])

    load(0).start()
    for n in range(PARTS):
        if n + 1 < PARTS:
            load(n + 1).start()
        yield
        load(n).wait()
        mixed[...] = rough[n % 2].astype(jnp.float32)
        for j in range(4):
            wide[pl.ds(PART * n, PART), j * 128 : j * 128 + 128] = mixed[pl.ds(j, PART, stride=4), :].astype(jnp.bfloat16)


KEPT = (0, 256, 768, 1536, 2304)


def front_kernel(
    tokens, pre_gain, post_gain, qkv_hbm, weight_hbm, doc_ids, cotangent, delta, cosine, sine,
    output, gathered, delta_sum, grad_proj_t, grad_out,
    query_ref, key_ref, value_ref, heads_ref, full, probs, slopes, keys_t, dkey, dvalue, grad_proj, out_grad, weight_t,
    everything, own, own_grad, wide, rough, mixed, own_part, parts_in, summed, other, delta_part, starts, values_t,
    weight, partial, received, mate, total, group_q, group_a, group_b, out_in,
    send_sems, piece_sems, pair_sems, local_sems, in_sems, delta_sems,
    mate_sems, part_sems, group_sems, out_sems, sum_sems,
):
    x, zh, zl, y, c = place()
    k, g = zl * 4 + y, x * 2 + zh
    sib = device(x, zh, zl, y, 1 - c)
    chips = [(a, b) for a in range(2) for b in range(4)][1:]
    fellows = [((zl + a) % 2, (y + b) % 4) for a, b in chips]
    to_fellows = [device(x, zh, a, b, c) for a, b in fellows]
    kin = [((x + b) % 4, (zh + a) % 2) for a, b in chips]
    to_kin = [device(a, b, zl, y, c) for a, b in kin]
    to_x = [device((x + step) % 4, zh, zl, y, c) for step in (1, 2, 3)]
    to_zh = device(x, 1 - zh, zl, y, c)
    group_in = {"q": group_q, "a": group_a, "b": group_b}
    greet([sib] + to_fellows + to_kin)
    send = Sender(send_sems)
    rows_of = lambda n: pl.ds(pl.multiple_of(n % 4 * 32, 32), 32)
    load_part = pltpu.make_async_copy(delta.at[rows_of(x), :], own_part, delta_sems.at[4])
    load_part.start()

    def background():
        for _ in weight_parts(qkv_hbm, wide, rough, mixed, in_sems):
            yield
        load_weight.start()

    load_weight = pltpu.make_async_copy(weight_hbm, weight, local_sems.at[1])
    work = background()
    next(work)
    values = tokens[...].astype(jnp.float32)
    scale = lax.rsqrt(jnp.mean(values * values, axis=-1, keepdims=True) + 1e-06)
    own[...] = (values * scale * as_row(pre_gain)).astype(jnp.bfloat16)
    document_starts(doc_ids, starts)
    met([sib] + to_fellows + to_kin)
    for n, step in enumerate((1, 2, 3)):
        send(delta.at[rows_of(x + step), :], parts_in.at[n], delta_sems.at[n], to_x[n])
    spread(own, everything, send, piece_sems.at[0], pair_sems.at[0], local_sems.at[0], work)
    store = pltpu.make_async_copy(everything, gathered, local_sems.at[3])
    store.start()

    for i in range(STEPS):
        at = pl.ds(i * BLOCK, BLOCK)
        rows = everything[pl.ds(4 * i, 4)].reshape(BLOCK, WIDTH)
        proj = jnp.dot(rows, wide[...], preferred_element_type=jnp.float32)
        queries = [turn(proj[:, h * 128 : h * 128 + 128], cosine[at, :], sine[at, :]).astype(jnp.bfloat16) for h in range(2)]
        query_ref[i] = jnp.concatenate(queries, axis=0)
        key_ref[at, :] = turn(proj[:, 256:384], cosine[at, :], sine[at, :]).astype(jnp.bfloat16)
        value_ref[at, :] = proj[:, 384:].astype(jnp.bfloat16)
        keys_t[:, at] = key_ref[at, :].astype(jnp.float32).T.astype(jnp.bfloat16)
        values_t[:, at] = proj[:, 384:].T.astype(jnp.bfloat16)
        start_row = jnp.concatenate([start_of(starts, i)] * 2, axis=1)
        query_row = lax.broadcasted_iota(jnp.int32, (1, 2 * BLOCK), 1) % BLOCK + i * BLOCK
        first = max(0, i - 2) * BLOCK
        keys_at = slice(first, i * BLOCK + BLOCK)
        soft, e = scored(key_ref[keys_at, :], query_ref[i], first, start_row, query_row)
        p = e * (1.0 / jnp.sum(e, axis=0, keepdims=True))
        kept = slice(KEPT[i], KEPT[i + 1])
        probs[kept, :] = p
        slopes[kept, :] = p * ((1.0 - soft * soft) * query_scale)
        acc = jnp.dot(values_t[:, keys_at], p.astype(jnp.bfloat16), preferred_element_type=jnp.float32)
        for h in range(2):
            part = acc[:, h * BLOCK : h * BLOCK + BLOCK].T.reshape(4, ROWS, 128)
            heads_ref[pl.ds(4 * i, 4), :, h * 128 : h * 128 + 128] = part
        if i == 0:
            load_part.wait()
            delta_total = own_part[...].astype(jnp.float32)
            for n in range(3):
                send.arrived(parts_in.at[n], delta_sems.at[n], sib)
                delta_total = delta_total + parts_in[n].astype(jnp.float32)
            summed[...] = delta_total.astype(jnp.bfloat16)
            send(summed, other, delta_sems.at[3], to_zh)

    share = heads_ref[:, pl.ds(pl.multiple_of(g * 8, 8), 8), :]
    load_weight.wait()
    for core in range(2):
        rows = jnp.concatenate([share[2 * kk + core] for kk in range(8)], axis=0).astype(jnp.bfloat16)
        left = jnp.dot(rows, weight[:, :HALF], preferred_element_type=jnp.float32)
        right = jnp.dot(rows, weight[:, HALF:], preferred_element_type=jnp.float32)
        for kk in range(8):
            both = jnp.concatenate([left[kk * 8 : kk * 8 + 8], right[kk * 8 : kk * 8 + 8]], axis=0)
            partial[core, kk] = both.astype(jnp.bfloat16)
    for n, (a, b) in enumerate(fellows):
        kk = a * 4 + b
        send(partial.at[1 - c, kk], mate.at[kk], mate_sems.at[kk], sib)
    send(partial.at[1 - c, k], mate.at[k], mate_sems.at[k], sib)
    for (a, b), to in zip(fellows, to_fellows):
        kk = a * 4 + b
        send.arrived(mate.at[kk], mate_sems.at[kk], sib)
        total[kk] = (partial[c, kk].astype(jnp.float32) + mate[kk].astype(jnp.float32)).astype(jnp.bfloat16)
        send(total.at[kk], received.at[k], part_sems.at[k], to)
    send.arrived(mate.at[k], mate_sems.at[k], sib)
    both = partial[c, k].astype(jnp.float32) + mate[k].astype(jnp.float32)
    send.arrived(other, delta_sems.at[3], sib)
    delta_part[...] = (summed[...].astype(jnp.float32) + other[...].astype(jnp.float32)).astype(jnp.bfloat16)
    keep = pltpu.make_async_copy(delta_part, delta_sum.at[x], local_sems.at[2])
    keep.start()
    for to in (to_x[0], to_x[2]):
        send(delta_part, delta_sum.at[x], sum_sems.at[0, x], to)
    gain_row = as_row(post_gain)
    pick = lambda rows: jnp.where(g % 2 == 0, rows[:8], rows[8:])
    near_rows = pl.ds(pl.multiple_of(g // 2 * 16, 16), 16)
    own_tokens = pick(tokens[near_rows, :].astype(jnp.float32))
    dnorm = pick(cotangent[near_rows, :].astype(jnp.float32)) * gain_row
    for a, b in fellows:
        kk = a * 4 + b
        send.arrived(received.at[kk], part_sems.at[kk], sib)
        both = both + received[kk].astype(jnp.float32)
    attn = unstacked(both)
    scale = lax.rsqrt(jnp.mean(attn * attn, axis=-1, keepdims=True) + 1e-06)
    normal = attn * scale
    grad = scale * (dnorm - normal * jnp.mean(dnorm * normal, axis=-1, keepdims=True))
    for t, (region, (lo, size)) in enumerate(REGIONS.items()):
        into = group_in[region]
        into[g] = stacked(grad[:, lo : lo + size]).astype(jnp.bfloat16)
        for to in to_kin:
            send(into.at[g], into.at[g], group_sems.at[t, g], to)
    out_in[zh, x] = stacked(own_tokens + normal * gain_row).astype(jnp.bfloat16)
    for side, step in enumerate((1, 3)):
        n = (x + step) % 4
        send.arrived(delta_sum.at[n], sum_sems.at[0, n], sib)
        half = delta_sum.at[n, pl.ds(side * 16, 16), :]
        send(half, half, sum_sems.at[1 + side, n], to_x[2 - 2 * side])

    def ready(region):
        t, (lo, size) = list(REGIONS).index(region), REGIONS[region]
        into = group_in[region]
        for a, b in kin:
            gg = a * 2 + b
            send.arrived(into.at[gg], group_sems.at[t, gg], sib)
        for gg in range(0, 8, 2):
            first = unstacked(into[gg].astype(jnp.float32))
            second = unstacked(into[gg + 1].astype(jnp.float32))
            own_grad[pl.ds(gg * 8, 16), pl.ds(lo, size)] = jnp.concatenate([first, second], axis=0).astype(jnp.bfloat16)

    def returning():
        for lo in range(0, WIDTH, 768):
            weight_t[lo : lo + 768, :] = weight[:, lo : lo + 768].astype(jnp.float32).T.astype(jnp.bfloat16)
            yield
        for _ in range(3):
            yield
        for to in to_x:
            send(out_in.at[zh, x], out_in.at[zh, x], out_sems.at[x], to)
        for _ in range(12):
            yield
        for step in (1, 2, 3):
            there = out_in.at[zh, (x + step) % 4]
            send.arrived(there, out_sems.at[(x + step) % 4], sib)
        send(out_in.at[zh], out_in.at[zh], out_sems.at[4], to_zh)

    spread(own_grad, full, send, piece_sems.at[1], pair_sems.at[1], local_sems.at[0], returning(), ready)

    heads_t = heads_ref[...].reshape(16 * ROWS, 256).T.astype(jnp.bfloat16)
    for lo in range(0, WIDTH, 768):
        columns = full[:, :, lo : lo + 768].reshape(16 * ROWS, 768)
        out_grad[:, lo : lo + 768] = jnp.dot(heads_t, columns, preferred_element_type=jnp.float32).astype(jnp.bfloat16)
    store_out = pltpu.make_async_copy(out_grad, grad_out, local_sems.at[0])
    store_out.start()
    dkey[...] = jnp.zeros_like(dkey)
    dvalue[...] = jnp.zeros_like(dvalue)
    for i in range(STEPS):
        at = slice(i * BLOCK, i * BLOCK + BLOCK)
        keys_at = slice(max(0, i - 2) * BLOCK, i * BLOCK + BLOCK)
        kept = slice(KEPT[i], KEPT[i + 1])
        rows = full[pl.ds(4 * i, 4)].reshape(BLOCK, WIDTH)
        grad_heads = jnp.dot(rows, weight_t[...], preferred_element_type=jnp.float32).astype(jnp.bfloat16)
        grad = jnp.concatenate([grad_heads[:, :128], grad_heads[:, 128:]], axis=0)
        p = probs[kept, :]
        dp = lax.dot_general(value_ref[keys_at, :], grad, (((1,), (1,)), ((), ())), preferred_element_type=jnp.float32)
        dvalue[keys_at, :] += jnp.dot(p.astype(jnp.bfloat16), grad, preferred_element_type=jnp.float32)
        ds = (slopes[kept, :] * (dp - jnp.sum(p * dp, axis=0, keepdims=True))).astype(jnp.bfloat16)
        dkey[keys_at, :] += jnp.dot(ds, query_ref[i], preferred_element_type=jnp.float32)
        acc = jnp.dot(keys_t[:, keys_at], ds, preferred_element_type=jnp.float32)
        for h in range(2):
            turned_back = turn(acc[:, h * BLOCK : h * BLOCK + BLOCK].T, cosine[at, :], -sine[at, :])
            grad_proj[at, h * 128 : h * 128 + 128] = turned_back
    grad_proj[:, 256:384] = turn(dkey[...], cosine[...], -sine[...])
    grad_proj[:, 384:512] = dvalue[...]
    grad_proj_t[...] = grad_proj[...].T.astype(jnp.bfloat16)

    send.arrived(out_in.at[1 - zh], out_sems.at[4], sib)
    for gg in range(0, 8, 2):
        first = unstacked(out_in[0, gg // 2].astype(jnp.float32))
        second = unstacked(out_in[1, gg // 2].astype(jnp.float32))
        output[pl.ds(gg * 8, 16), :] = jnp.concatenate([first, second], axis=0).astype(jnp.bfloat16)
    n = (x + 2) % 4
    for side in range(2):
        send.arrived(delta_sum.at[n, pl.ds(side * 16, 16), :], sum_sems.at[1 + side, n], sib)
    keep.wait()
    store.wait()
    store_out.wait()
    send.finish()


def front(tokens, pre_gain, post_gain, qkv_weight, weight, doc_ids, cotangent, delta, cosine, sine):
    vmem = pl.BlockSpec(memory_space=pltpu.VMEM)
    hbm = pl.BlockSpec(memory_space=pl.ANY)
    shape = jax.ShapeDtypeStruct
    bf16, f32 = jnp.bfloat16, jnp.float32
    return pl.pallas_call(
        front_kernel,
        out_shape=(
            shape((ROWS, WIDTH), bf16),
            shape((16, ROWS, WIDTH), bf16),
            shape((4, 32, WIDTH), bf16),
            shape((512, 1024), bf16),
            shape((256, WIDTH), bf16),
        ),
        in_specs=[vmem, vmem, vmem, hbm, hbm, vmem, vmem, hbm, vmem, vmem],
        out_specs=(vmem, hbm, hbm, vmem, hbm),
        scratch_shapes=[
            pltpu.VMEM((STEPS, 2 * BLOCK, 128), bf16),
            pltpu.VMEM((1024, 128), bf16),
            pltpu.VMEM((1024, 128), bf16),
            pltpu.VMEM((16, ROWS, 256), f32),
            pltpu.VMEM((16, ROWS, WIDTH), bf16),
            pltpu.VMEM((KEPT[-1], 2 * BLOCK), f32),
            pltpu.VMEM((KEPT[-1], 2 * BLOCK), f32),
            pltpu.VMEM((128, 1024), bf16),
            pltpu.VMEM((1024, 128), f32),
            pltpu.VMEM((1024, 128), f32),
            pltpu.VMEM((1024, 512), f32),
            pltpu.VMEM((256, WIDTH), bf16),
            pltpu.VMEM((WIDTH, 256), bf16),
            pltpu.VMEM((16, ROWS, WIDTH), bf16),
            pltpu.VMEM((ROWS, WIDTH), bf16),
            pltpu.VMEM((ROWS, WIDTH), bf16),
            pltpu.VMEM((WIDTH, 512), bf16),
            pltpu.VMEM((2, 4 * PART, 128), bf16),
            pltpu.VMEM((4 * PART, 128), f32),
            pltpu.VMEM((32, WIDTH), bf16),
            pltpu.VMEM((3, 32, WIDTH), bf16),
            pltpu.VMEM((32, WIDTH), bf16),
            pltpu.VMEM((32, WIDTH), bf16),
            pltpu.VMEM((32, WIDTH), bf16),
            pltpu.VMEM((8, 128), jnp.int32),
            pltpu.VMEM((128, 1024), bf16),
            pltpu.VMEM((256, WIDTH), bf16),
            pltpu.VMEM((2, 8, 16, HALF), bf16),
            pltpu.VMEM((8, 16, HALF), bf16),
            pltpu.VMEM((8, 16, HALF), bf16),
            pltpu.VMEM((8, 16, HALF), bf16),
            pltpu.VMEM((8, 16, 2 * NQ), bf16),
            pltpu.VMEM((8, 16, N1 // 2), bf16),
            pltpu.VMEM((8, 16, N2 // 2), bf16),
            pltpu.VMEM((2, 4, 16, HALF), bf16),
            pltpu.SemaphoreType.DMA((4 + 8 + 2 + 7 + 21 + 2 + 4 + 2 * SPREAD_SENDS,)),
            pltpu.SemaphoreType.DMA((2, 2, 6, 8)),
            pltpu.SemaphoreType.DMA((2, 8, 2)),
            pltpu.SemaphoreType.DMA((4,)),
            pltpu.SemaphoreType.DMA((PARTS,)),
            pltpu.SemaphoreType.DMA((5,)),
            pltpu.SemaphoreType.DMA((8,)),
            pltpu.SemaphoreType.DMA((8,)),
            pltpu.SemaphoreType.DMA((3, 8)),
            pltpu.SemaphoreType.DMA((5,)),
            pltpu.SemaphoreType.DMA((3, 4)),
        ],
        compiler_params=pltpu.CompilerParams(
            collective_id=0, has_side_effects=True, vmem_limit_bytes=60 * 2**20
        ),
        name="front",
    )(tokens, pre_gain, post_gain, qkv_weight, weight, doc_ids, cotangent, delta, cosine, sine)


CHUNK = 1152
CHUNKS = WIDTH // CHUNK


def finish_kernel(
    x, turned, delta, momentum, fragment, output, grad_out, qkv_out, new_momentum, new_fragment, new_output, out_out,
    mixed,
):
    i = pl.program_id(0)

    mean_delta = delta[...].astype(jnp.float32) / 8.0
    moment = 0.9 * momentum[...] + mean_delta
    new_momentum[...] = moment
    new_fragment[...] = fragment[...] - 0.7 * (mean_delta + 0.9 * moment)
    new_output[...] = output[...]
    out_out[...] = grad_out[...]

    at = pl.ds(pl.multiple_of(i * CHUNK, CHUNK), CHUNK)
    part = jnp.dot(turned[...], x[...], preferred_element_type=jnp.float32)
    for j in range(4):
        mixed[pl.ds(j, CHUNK, stride=4), :] = part[j * 128 : j * 128 + 128].T
    qkv_out[...] = mixed[...].astype(jnp.bfloat16)


def finish(gathered, turned, delta, momentum, fragment, output, grad_out):
    columns = lambda n: pl.BlockSpec((n, CHUNK), lambda i: (0, i))
    return pl.pallas_call(
        finish_kernel,
        grid=(CHUNKS,),
        in_specs=[
            columns(1024),
            pl.BlockSpec((512, 1024), lambda i: (0, 0)),
            columns(128),
            columns(128),
            columns(128),
            columns(ROWS),
            columns(256),
        ],
        out_specs=[
            pl.BlockSpec((4 * CHUNK, 128), lambda i: (i, 0)),
            columns(128),
            columns(128),
            columns(ROWS),
            columns(256),
        ],
        scratch_shapes=[
            pltpu.VMEM((4 * CHUNK, 128), jnp.float32),
        ],
        out_shape=[
            jax.ShapeDtypeStruct((4 * WIDTH, 128), jnp.bfloat16),
            jax.ShapeDtypeStruct((128, WIDTH), jnp.float32),
            jax.ShapeDtypeStruct((128, WIDTH), jnp.float32),
            jax.ShapeDtypeStruct((ROWS, WIDTH), jnp.bfloat16),
            jax.ShapeDtypeStruct((256, WIDTH), jnp.bfloat16),
        ],
        compiler_params=pltpu.CompilerParams(vmem_limit_bytes=60 * 2**20),
        name="finish",
    )(gathered, turned, delta, momentum, fragment, output, grad_out)


def local(
    tokens,
    pre_gain,
    post_gain,
    qkv_weight,
    out_weight,
    doc_ids,
    cotangent,
    outer_delta,
    momentum,
    fragment,
):
    cosine, sine = tables(16 * ROWS, 128)
    doc_ids = doc_ids.reshape(8, 128)
    out_flat = out_weight.reshape(256, WIDTH)
    output, gathered, delta, turned, grad_out = front(
        tokens, pre_gain.reshape(36, 128), post_gain.reshape(36, 128), qkv_weight.reshape(4 * WIDTH, 128), out_flat,
        doc_ids, cotangent, outer_delta[0], cosine, sine,
    )
    grad_qkv, new_momentum, new_fragment, output, grad_out = finish(
        gathered.reshape(16 * ROWS, WIDTH), turned, delta.reshape(128, WIDTH), momentum, fragment, output, grad_out
    )
    return (output, grad_qkv.reshape(qkv_weight.shape), grad_out.reshape(out_weight.shape), new_momentum, new_fragment)


def solution(mesh):
    placed = (
        P("fsdp", None),
        P(),
        P(),
        P(None, "fsdp", None, None),
        P("fsdp", None, None, None),
        P(),
        P("fsdp", None),
        P("group", "fsdp", None),
        P("fsdp", None),
        P("fsdp", None),
    )
    return jax.shard_map(
        local,
        mesh=mesh,
        in_specs=placed,
        out_specs=(
            P("fsdp", None),
            P(None, "fsdp", None, None),
            P("fsdp", None, None, None),
            P("fsdp", None),
            P("fsdp", None),
        ),
        check_vma=False,
    )
```
